32 devices in a mesh: groups: 2 (over x), row: 16 (over z, y, core).
Axes of the slice: x: 2, y: 2, z: 4, core: 2. Of those that a mesh axis runs over, the one named last changes fastest.
Arguments:
- pair_rep: bfloat16 [64, 32, 128], P(('groups', 'row')), parts along dimension 0, may hold values from -6 to 6
- pair_mask: int32 [64, 32], P(('groups', 'row')), parts along dimension 0, may hold values from 0 to 1, as said below
- gain_in: float32 [2, 128], replicated, may hold values from 0.25 to 1.75
- shift_in: float32 [2, 128], replicated, may hold values from -3 to 3
- proj_weight: bfloat16 [2, 128, 512], replicated, may hold values from -0.5 to 0.5
- gate_weight: bfloat16 [2, 128, 128], replicated, may hold values from -0.5 to 0.5
- gain_out: float32 [2, 128], replicated, may hold values from 0.25 to 1.75
- shift_out: float32 [2, 128], replicated, may hold values from -3 to 3
- out_weight: bfloat16 [2, 128, 128], replicated, may hold values from -0.5 to 0.5
Outputs:
- pair_out: bfloat16 [64, 32, 128], P(('groups', 'row')), parts along dimension 0
The draws below stay inside these ranges and needn't reach their ends.
There are 2 independent parts, one for each index of `groups`. The reference program is written for one: setup_inputs(seed, part) draws one part's arguments, and reference() takes and returns one part's arrays. A program takes and returns all parts, laid end to end along the dimension named above; an argument that names none is the same for every part. Nothing has to cross between parts.
Inputs may be any that keep to these rules, and one draw needn't show every extreme that they name: Each token is real or padding on its own, padding with probability one in four; pair_mask[i, j] = 1 exactly when tokens i and j are both real.
All inputs are finite; a program needn't handle non-finite values.
Results may differ from the reference program's by a relative error of at most 0.0095.
Values may be sent and summed in bfloat16 or wider, within the bound.
No kernel may reach another device: no remote copies, remote signals or barrier semaphores. Data moves between devices by JAX's collectives and lax.ppermute only.
A program may use at most 64 MiB of HBM per device.

```python
import jax
import jax.numpy as jnp
from jax import lax

C = 128
H = 128
NTOK = 32
N_ROW = 16


def draw_pair_mask(key, part):
    key = jax.random.fold_in(key, 4099)
    levels = jax.random.randint(key, (NTOK,), 0, 4)
    valid = (levels > 0).astype(jnp.int32)
    return valid[:, None] * valid[None, :]


def block_scale(own_key, extent, shards, low, top_value):
    factor_of = 1.0
    for dim, shards_of in shards:
        steps = jax.random.uniform(jax.random.fold_in(jax.random.fold_in(own_key, 6), dim), (shards_of,), jnp.float32, low / len(shards), top_value / len(shards))
        factor_of = factor_of * jnp.repeat(jnp.exp(steps), extent[dim] // shards_of).reshape((-1,) + (1,) * (len(extent) - 1 - dim))
    return factor_of


def normal_values(stream_key, shape, deviation, most, shards=(), held_as=jnp.bfloat16):
    entries = deviation * jax.random.normal(stream_key, shape, jnp.float32)
    if shards:
        entries = entries * block_scale(stream_key, shape, shards, -0.22, 0.18)
    return jnp.clip(entries, -most, most).astype(held_as)


def setup_inputs(seed: int = 0, part: int = 0) -> dict:
    key_of = jax.random.split(jax.random.key(seed), 10)
    part_keys = jax.random.split(jax.random.fold_in(key_of[9], part), 10)
    pair_rep = normal_values(part_keys[0], (NTOK, NTOK, C), 1.0, 6.0, ((0, 16),))
    pair_mask = draw_pair_mask(jax.random.fold_in(jax.random.fold_in(key_of[9], part), 71), part)
    gain_in = jnp.clip(1.0 + 0.15 * jax.random.normal(key_of[2], (2, C), jnp.float32), 0.25, 1.75)
    shift_in = normal_values(key_of[3], (2, C), 0.5, 3.0, (), jnp.float32)
    proj_weight = normal_values(key_of[4], (2, C, 4 * H), C ** -0.5, 0.5)
    gate_weight = normal_values(key_of[5], (2, C, C), C ** -0.5, 0.5)
    gain_out = jnp.clip(1.0 + 0.15 * jax.random.normal(key_of[6], (2, H), jnp.float32), 0.25, 1.75)
    shift_out = normal_values(key_of[7], (2, H), 0.5, 3.0, (), jnp.float32)
    out_weight = normal_values(key_of[8], (2, H, C), H ** -0.5, 0.5)
    return {"pair_rep": pair_rep, "pair_mask": pair_mask, "gain_in": gain_in, "shift_in": shift_in, "proj_weight": proj_weight, "gate_weight": gate_weight, "gain_out": gain_out, "shift_out": shift_out, "out_weight": out_weight}


def layer_norm(values, gain, offset, axis):
    mean = lax.optimization_barrier(jnp.mean(values, axis=axis, keepdims=True))
    centered = values - mean
    variance = lax.optimization_barrier(jnp.mean(centered * centered, axis=axis, keepdims=True))
    return centered * lax.rsqrt(variance + 1e-05) * gain + offset

def project_rows(block, mask_block, gain, offset, weight, gate_w):
    normed = layer_norm(block.astype(jnp.float32), gain, offset, -1).astype(jnp.bfloat16)
    flat = normed.reshape(-1, C)
    packed = jnp.dot(flat, weight, preferred_element_type=jnp.float32).reshape(block.shape[0], NTOK, 4 * H)
    masked = mask_block.astype(jnp.float32)[:, :, None]
    left = (masked * jax.nn.sigmoid(packed[:, :, 0:H]) * packed[:, :, H:2 * H]).astype(jnp.bfloat16)
    right = (masked * jax.nn.sigmoid(packed[:, :, 2 * H:3 * H]) * packed[:, :, 3 * H:]).astype(jnp.bfloat16)
    gating = jax.nn.sigmoid(jnp.dot(flat, gate_w, preferred_element_type=jnp.float32)).reshape(block.shape[0], NTOK, C)
    return (left, right, gating)

def one_update(pair_now, pair_mask, layer_index, gain_in, shift_in, proj_weight, gate_weight, gain_out, shift_out, out_weight):
    blocks = NTOK // N_ROW
    pair_blocks = pair_now.reshape(blocks, N_ROW, NTOK, C)
    mask_blocks = pair_mask.reshape(blocks, N_ROW, NTOK)

    def per_block(items):
        return project_rows(items[0], items[1], gain_in[layer_index], shift_in[layer_index], proj_weight[layer_index], gate_weight[layer_index])
    left, right, gating = lax.map(per_block, (pair_blocks, mask_blocks))
    left = jnp.transpose(left.reshape(NTOK, NTOK, H), (2, 0, 1))
    right = jnp.transpose(right.reshape(NTOK, NTOK, H), (2, 0, 1))

    def per_channel(items):
        if layer_index == 0:
            return jnp.dot(items[0], items[1].T, preferred_element_type=jnp.float32).astype(jnp.bfloat16)
        return jnp.dot(items[0].T, items[1], preferred_element_type=jnp.float32).astype(jnp.bfloat16)
    product = lax.map(per_channel, (left, right))
    product_blocks = jnp.transpose(product.reshape(H, blocks, N_ROW, NTOK), (1, 0, 2, 3))

    def finish_block(items):
        normed = layer_norm(items[0].astype(jnp.float32), gain_out[layer_index][:, None, None], shift_out[layer_index][:, None, None], 0).astype(jnp.bfloat16)
        update = jnp.einsum('hrn,hc->rnc', normed.astype(jnp.float32), out_weight[layer_index].astype(jnp.float32))
        return (items[1].astype(jnp.float32) + items[2] * update).astype(jnp.bfloat16)
    result = lax.map(finish_block, (product_blocks, pair_blocks, gating))
    return result.reshape(NTOK, NTOK, C)

def reference(pair_rep, pair_mask, gain_in, shift_in, proj_weight, gate_weight, gain_out, shift_out, out_weight):
    middle = one_update(pair_rep, pair_mask, 0, gain_in, shift_in, proj_weight, gate_weight, gain_out, shift_out, out_weight)
    return one_update(middle, pair_mask, 1, gain_in, shift_in, proj_weight, gate_weight, gain_out, shift_out, out_weight)
```

```python
import functools

import jax
import jax.numpy as jnp
from jax import lax
from jax.experimental import pallas as pl
from jax.experimental.pallas import tpu as pltpu
from jax.sharding import PartitionSpec as P

EPS = 1e-05
MARK_ROWS = 16
GATHER_LIMIT = 4 << 20


def sigmoid(values):
    return 0.5 * jnp.tanh(0.5 * values) + 0.5


def norm_rows(values, gain, offset):
    mean = jnp.mean(values, axis=-1, keepdims=True)
    centered = values - mean
    variance = jnp.mean(centered * centered, axis=-1, keepdims=True)
    return (centered * lax.rsqrt(variance + EPS) * gain + offset).astype(jnp.bfloat16)


def matmul(left, right):
    return jnp.dot(left, right, preferred_element_type=jnp.float32)


def gated(mask, packed, width):
    value = mask * sigmoid(packed[:, :width]) * packed[:, width:]
    return value.astype(jnp.bfloat16).astype(jnp.float32)


def updates_kernel(
    n_row,
    order,
    me_ref,
    own_ref,
    other_ref,
    gain_in,
    shift_in,
    proj_weight,
    gate_weight,
    gain_out,
    shift_out,
    out_weight,
    out_ref,
    pair,
    valid,
    left0,
    right0,
    gate0,
    middle,
    right1,
):
    me = me_ref[0]
    half, block_rows, width = own_ref.shape
    tokens = valid.shape[0]
    per = tokens // n_row
    rows = per * tokens

    for half_index, ref in enumerate((own_ref, other_ref)):
        for slot, step in enumerate(order):
            at = me ^ (step ^ half_index)
            pair[pl.ds(pl.multiple_of(at * rows, rows), rows), :] = ref[slot, 0:rows, :]
            marks = ref[slot, rows:block_rows, :].astype(jnp.float32)
            valid[pl.ds(at * per, per), :] = marks[0:per]

    step_i = 8
    chunk = step_i * tokens

    def project(i, _):
        at = pl.ds(pl.multiple_of(i * chunk, chunk), chunk)
        normed = norm_rows(pair[at, :].astype(jnp.float32), gain_in[0:1, :], shift_in[0:1, :])
        rowmask = valid[pl.ds(i * step_i, step_i), :]
        mask = (rowmask[:, None, :] * valid[...][None, :, :]).reshape(chunk, width)
        packed = matmul(normed, proj_weight[0])
        left0[at, :] = gated(mask, packed[:, 0 : 2 * width], width)
        right0[at, :] = gated(mask, packed[:, 2 * width :], width)
        gate0[at, :] = sigmoid(matmul(normed, gate_weight[0]))
        return 0

    lax.fori_loop(0, tokens // step_i, project, 0)

    for k in range(tokens):
        right1[k * tokens : (k + 1) * tokens, :] = right0[pl.ds(k, tokens, stride=tokens), :]

    def update(i, _):
        base = pl.multiple_of(i * chunk, chunk)
        at = pl.ds(base, chunk)
        totals = [jnp.zeros((tokens, width), jnp.float32)] * step_i
        for k in range(tokens):
            row = right1[k * tokens : (k + 1) * tokens, :]
            for r in range(step_i):
                totals[r] = totals[r] + left0[pl.ds(base + (r * tokens + k), 1), :] * row
        product = jnp.concatenate(totals, axis=0).astype(jnp.bfloat16).astype(jnp.float32)
        scaled = norm_rows(product, gain_out[0:1, :], shift_out[0:1, :])
        moved = pair[at, :].astype(jnp.float32) + gate0[at, :] * matmul(scaled, out_weight[0])
        middle[at, :] = moved.astype(jnp.bfloat16).astype(jnp.float32)
        return 0

    lax.fori_loop(0, tokens // step_i, update, 0)

    def project_last(i, _):
        at = pl.ds(pl.multiple_of(i * chunk, chunk), chunk)
        normed = norm_rows(middle[at, :], gain_in[1:2, :], shift_in[1:2, :])
        rowmask = valid[pl.ds(i * step_i, step_i), :]
        mask = (rowmask[:, None, :] * valid[...][None, :, :]).reshape(chunk, width)
        right0[at, :] = gated(mask, matmul(normed, proj_weight[1, :, 2 * width :]), width)
        return 0

    lax.fori_loop(0, tokens // step_i, project_last, 0)

    first = me * per
    columns = jnp.concatenate([middle[pl.ds(first + r, tokens, stride=tokens), :] for r in range(per)], axis=0)
    normed = norm_rows(columns, gain_in[1:2, :], shift_in[1:2, :])
    mask = jnp.concatenate([valid[...] * valid[pl.ds(first + r, 1), :] for r in range(per)], axis=0)
    left0[0:rows, :] = gated(mask, matmul(normed, proj_weight[1, :, 0 : 2 * width]), width)
    totals = [jnp.zeros((tokens, width), jnp.float32)] * per
    for k in range(tokens):
        row = right0[k * tokens : (k + 1) * tokens, :]
        for r in range(per):
            totals[r] = totals[r] + left0[r * tokens + k : r * tokens + k + 1, :] * row
    product = jnp.concatenate(totals, axis=0).astype(jnp.bfloat16).astype(jnp.float32)
    scaled = norm_rows(product, gain_out[1:2, :], shift_out[1:2, :])
    held = middle[pl.ds(pl.multiple_of(first * tokens, rows), rows), :]
    gate = sigmoid(matmul(norm_rows(held, gain_in[1:2, :], shift_in[1:2, :]), gate_weight[1]))
    out_ref[...] = (held + gate * matmul(scaled, out_weight[1])).astype(jnp.bfloat16)


def updates(n_row, order, tokens, me, own, other, params):
    width = own.shape[-1]
    rows = tokens * tokens // n_row
    pairs = tokens * tokens
    vmem = pl.BlockSpec(memory_space=pltpu.VMEM)
    return pl.pallas_call(
        functools.partial(updates_kernel, n_row, order),
        out_shape=jax.ShapeDtypeStruct((rows, width), jnp.bfloat16),
        in_specs=[pl.BlockSpec(memory_space=pltpu.SMEM)] + [vmem] * 9,
        out_specs=vmem,
        scratch_shapes=[
            pltpu.VMEM((pairs, width), jnp.bfloat16),
            pltpu.VMEM((tokens, width), jnp.float32),
        ]
        + [pltpu.VMEM((pairs, width), jnp.float32)] * 5,
        compiler_params=pltpu.CompilerParams(vmem_limit_bytes=24 << 20),
    )(me, own, other, *params)


def swap(values, step, n_row):
    return lax.ppermute(values, "row", [(i, i ^ step) for i in range(n_row)])


def gathered(n_row, pair_rep, pair_mask, *params):
    per, tokens, width = pair_rep.shape
    rows = per * tokens
    me = lax.axis_index("row")
    first = me * per
    diagonal = [lax.dynamic_slice(pair_mask, (r, first + r), (1, 1)) for r in range(per)]
    marks = jnp.concatenate(diagonal, axis=0).astype(jnp.bfloat16)
    marks = jnp.pad(jnp.broadcast_to(marks, (per, width)), ((0, MARK_ROWS - per), (0, 0)))
    held = jnp.concatenate([pair_rep.reshape(rows, width), marks], axis=0)[None]
    order = [0]
    step = n_row // 2
    while step > 1:
        held = jnp.concatenate([held, swap(held, step, n_row)], axis=0)
        order = order + [s ^ step for s in order]
        step //= 2
    other = swap(held, 1, n_row)
    out = updates(n_row, tuple(order), tokens, me.astype(jnp.int32).reshape(1), held, other, params)
    return out.reshape(per, tokens, width)


H = 128


def layer_norm(values, gain, offset, axis):
    mean = jnp.mean(values, axis=axis, keepdims=True)
    centered = values - mean
    variance = jnp.mean(centered * centered, axis=axis, keepdims=True)
    return centered * lax.rsqrt(variance + 1e-05) * gain + offset


def triangle(
    pair_now,
    pair_mask,
    layer_index,
    gain_in,
    shift_in,
    proj_weight,
    gate_weight,
    gain_out,
    shift_out,
    out_weight,
):
    normed = layer_norm(
        pair_now.astype(jnp.float32), gain_in[layer_index], shift_in[layer_index], -1
    ).astype(jnp.bfloat16)
    packed = jnp.einsum(
        "rnc,ch->hrn", normed, proj_weight[layer_index], preferred_element_type=jnp.float32
    )
    masked = pair_mask.astype(jnp.float32)[None, :, :]
    left = (masked * jax.nn.sigmoid(packed[0:H]) * packed[H : 2 * H]).astype(jnp.bfloat16)
    right = (masked * jax.nn.sigmoid(packed[2 * H : 3 * H]) * packed[3 * H :]).astype(jnp.bfloat16)
    gating = jax.nn.sigmoid(
        jnp.einsum(
            "rnc,cd->rnd", normed, gate_weight[layer_index], preferred_element_type=jnp.float32
        )
    )
    lifted_left, lifted_right = (
        lax.all_to_all(left, "row", split_axis=0, concat_axis=1, tiled=True),
        lax.all_to_all(right, "row", split_axis=0, concat_axis=1, tiled=True),
    )
    if layer_index == 0:
        product = jnp.einsum(
            "hik,hjk->hij", lifted_left, lifted_right, preferred_element_type=jnp.float32
        )
    else:
        product = jnp.einsum(
            "hki,hkj->hij", lifted_left, lifted_right, preferred_element_type=jnp.float32
        )
    product = product.astype(jnp.bfloat16)
    out_gain = gain_out[layer_index][:, None, None]
    out_shift = shift_out[layer_index][:, None, None]
    out_proj = out_weight[layer_index]
    returned = lax.all_to_all(product, "row", split_axis=1, concat_axis=0, tiled=True)
    scaled = layer_norm(returned.astype(jnp.float32), out_gain, out_shift, 0).astype(jnp.bfloat16)
    update = jnp.einsum("hrn,hc->rnc", scaled, out_proj, preferred_element_type=jnp.float32)
    return (pair_now.astype(jnp.float32) + gating * update).astype(jnp.bfloat16)


def exchanged(
    pair_rep,
    pair_mask,
    gain_in,
    shift_in,
    proj_weight,
    gate_weight,
    gain_out,
    shift_out,
    out_weight,
):
    current = pair_rep
    for layer_index in range(2):
        current = triangle(
            current,
            pair_mask,
            layer_index,
            gain_in,
            shift_in,
            proj_weight,
            gate_weight,
            gain_out,
            shift_out,
            out_weight,
        )
    return current


def solution(mesh):
    n_row = mesh.shape["row"]

    def shards(pair_rep, *rest):
        per, tokens, _ = pair_rep.shape
        small = pair_rep.size * n_row * 2 <= GATHER_LIMIT
        fits = n_row & (n_row - 1) == 0 and n_row > 1 and tokens % 8 == 0 and per <= MARK_ROWS
        if small and fits:
            return gathered(n_row, pair_rep, *rest)
        return exchanged(pair_rep, *rest)

    in_specs = (
        P(("groups", "row"), None, None),
        P(("groups", "row"), None),
        P(),
        P(),
        P(),
        P(),
        P(),
        P(),
        P(),
    )
    out_specs = P(("groups", "row"), None, None)
    return jax.shard_map(shards, mesh=mesh, in_specs=in_specs, out_specs=out_specs, check_vma=False)
```

```python
import functools

import jax
import jax.numpy as jnp
from jax import lax
from jax.experimental import pallas as pl
from jax.experimental.pallas import tpu as pltpu
from jax.sharding import PartitionSpec as P

EPS = 1e-05
MARK_ROWS = 16
GATHER_LIMIT = 4 << 20


def sigmoid(values):
    return 0.5 * jnp.tanh(0.5 * values) + 0.5


def norm_rows(values, gain, offset):
    mean = jnp.mean(values, axis=-1, keepdims=True)
    centered = values - mean
    variance = jnp.mean(centered * centered, axis=-1, keepdims=True)
    return (centered * lax.rsqrt(variance + EPS) * gain + offset).astype(jnp.bfloat16)


def matmul(left, right):
    return jnp.dot(left, right, preferred_element_type=jnp.float32)


def gated(mask, packed, width):
    value = mask * sigmoid(packed[:, :width]) * packed[:, width:]
    return value.astype(jnp.bfloat16).astype(jnp.float32)


def updates_kernel(
    n_row,
    order,
    me_ref,
    own_ref,
    other_ref,
    gain_in,
    shift_in,
    proj_weight,
    gate_weight,
    gain_out,
    shift_out,
    out_weight,
    out_ref,
    pair,
    valid,
    left0,
    right0,
    gate0,
    middle,
    right1,
):
    me = me_ref[0]
    half, block_rows, width = own_ref.shape
    tokens = valid.shape[0]
    per = tokens // n_row
    rows = per * tokens

    for half_index, ref in enumerate((own_ref, other_ref)):
        for slot, step in enumerate(order):
            at = me ^ (step ^ half_index)
            pair[pl.ds(pl.multiple_of(at * rows, rows), rows), :] = ref[slot, 0:rows, :]
            marks = ref[slot, rows:block_rows, :].astype(jnp.float32)
            valid[pl.ds(at * per, per), :] = marks[0:per]

    step_i = 8
    pitch = tokens + 8
    chunk = step_i * tokens

    def project(i, _):
        at = pl.ds(pl.multiple_of(i * chunk, chunk), chunk)
        normed = norm_rows(pair[at, :].astype(jnp.float32), gain_in[0:1, :], shift_in[0:1, :])
        rowmask = valid[pl.ds(i * step_i, step_i), :]
        mask = (rowmask[:, None, :] * valid[...][None, :, :]).reshape(chunk, width)
        packed = matmul(normed, proj_weight[0])
        left0[at, :] = gated(mask, packed[:, 0 : 2 * width], width)
        right = gated(mask, packed[:, 2 * width :], width)
        for r in range(step_i):
            right0[pl.ds((i * step_i + r) * pitch, tokens), :] = right[r * tokens : (r + 1) * tokens, :]
        gate0[at, :] = sigmoid(matmul(normed, gate_weight[0]))
        return 0

    lax.fori_loop(0, tokens // step_i, project, 0, unroll=True)

    for k in range(tokens):
        right1[k * tokens : (k + 1) * tokens, :] = right0[pl.ds(k, tokens, stride=pitch), :]

    def update(i, _):
        base = pl.multiple_of(i * chunk, chunk)
        at = pl.ds(base, chunk)
        totals = [jnp.zeros((tokens, width), jnp.float32)] * step_i
        for k in range(tokens):
            row = right1[k * tokens : (k + 1) * tokens, :]
            for r in range(step_i):
                totals[r] = totals[r] + left0[pl.ds(base + (r * tokens + k), 1), :] * row
        product = jnp.concatenate(totals, axis=0).astype(jnp.bfloat16).astype(jnp.float32)
        scaled = norm_rows(product, gain_out[0:1, :], shift_out[0:1, :])
        moved = pair[at, :].astype(jnp.float32) + gate0[at, :] * matmul(scaled, out_weight[0])
        middle[at, :] = moved.astype(jnp.bfloat16).astype(jnp.float32)
        return 0

    lax.fori_loop(0, tokens // step_i, update, 0, unroll=True)

    def project_last(i, _):
        at = pl.ds(pl.multiple_of(i * chunk, chunk), chunk)
        normed = norm_rows(middle[at, :], gain_in[1:2, :], shift_in[1:2, :])
        rowmask = valid[pl.ds(i * step_i, step_i), :]
        mask = (rowmask[:, None, :] * valid[...][None, :, :]).reshape(chunk, width)
        right0[at, :] = gated(mask, matmul(normed, proj_weight[1, :, 2 * width :]), width)
        return 0

    lax.fori_loop(0, tokens // step_i, project_last, 0, unroll=True)

    first = me * per
    columns = jnp.concatenate([middle[pl.ds(first + r, tokens, stride=tokens), :] for r in range(per)], axis=0)
    normed = norm_rows(columns, gain_in[1:2, :], shift_in[1:2, :])
    mask = jnp.concatenate([valid[...] * valid[pl.ds(first + r, 1), :] for r in range(per)], axis=0)
    left0[0:rows, :] = gated(mask, matmul(normed, proj_weight[1, :, 0 : 2 * width]), width)
    totals = [jnp.zeros((tokens, width), jnp.float32)] * per
    for k in range(tokens):
        row = right0[k * tokens : (k + 1) * tokens, :]
        for r in range(per):
            totals[r] = totals[r] + left0[r * tokens + k : r * tokens + k + 1, :] * row
    product = jnp.concatenate(totals, axis=0).astype(jnp.bfloat16).astype(jnp.float32)
    scaled = norm_rows(product, gain_out[1:2, :], shift_out[1:2, :])
    held = middle[pl.ds(pl.multiple_of(first * tokens, rows), rows), :]
    gate = sigmoid(matmul(norm_rows(held, gain_in[1:2, :], shift_in[1:2, :]), gate_weight[1]))
    out_ref[...] = (held + gate * matmul(scaled, out_weight[1])).astype(jnp.bfloat16)


def updates(n_row, order, tokens, me, own, other, params):
    width = own.shape[-1]
    rows = tokens * tokens // n_row
    pairs = tokens * tokens
    vmem = pl.BlockSpec(memory_space=pltpu.VMEM)
    return pl.pallas_call(
        functools.partial(updates_kernel, n_row, order),
        out_shape=jax.ShapeDtypeStruct((rows, width), jnp.bfloat16),
        in_specs=[pl.BlockSpec(memory_space=pltpu.SMEM)] + [vmem] * 9,
        out_specs=vmem,
        scratch_shapes=[
            pltpu.VMEM((pairs, width), jnp.bfloat16),
            pltpu.VMEM((tokens, width), jnp.float32),
        ]
        + [pltpu.VMEM((pairs + 8 * tokens, width), jnp.float32)] * 5,
        compiler_params=pltpu.CompilerParams(vmem_limit_bytes=24 << 20),
    )(me, own, other, *params)


def swap(values, step, n_row):
    return lax.ppermute(values, "row", [(i, i ^ step) for i in range(n_row)])


def gathered(n_row, pair_rep, pair_mask, *params):
    per, tokens, width = pair_rep.shape
    rows = per * tokens
    me = lax.axis_index("row")
    first = me * per
    diagonal = [lax.dynamic_slice(pair_mask, (r, first + r), (1, 1)) for r in range(per)]
    marks = jnp.concatenate(diagonal, axis=0).astype(jnp.bfloat16)
    marks = jnp.pad(jnp.broadcast_to(marks, (per, width)), ((0, MARK_ROWS - per), (0, 0)))
    held = jnp.concatenate([pair_rep.reshape(rows, width), marks], axis=0)[None]
    order = [0]
    step = n_row // 2
    while step > 1:
        held = jnp.concatenate([held, swap(held, step, n_row)], axis=0)
        order = order + [s ^ step for s in order]
        step //= 2
    other = swap(held, 1, n_row)
    out = updates(n_row, tuple(order), tokens, me.astype(jnp.int32).reshape(1), held, other, params)
    return out.reshape(per, tokens, width)


H = 128


def layer_norm(values, gain, offset, axis):
    mean = jnp.mean(values, axis=axis, keepdims=True)
    centered = values - mean
    variance = jnp.mean(centered * centered, axis=axis, keepdims=True)
    return centered * lax.rsqrt(variance + 1e-05) * gain + offset


def triangle(
    pair_now,
    pair_mask,
    layer_index,
    gain_in,
    shift_in,
    proj_weight,
    gate_weight,
    gain_out,
    shift_out,
    out_weight,
):
    normed = layer_norm(
        pair_now.astype(jnp.float32), gain_in[layer_index], shift_in[layer_index], -1
    ).astype(jnp.bfloat16)
    packed = jnp.einsum(
        "rnc,ch->hrn", normed, proj_weight[layer_index], preferred_element_type=jnp.float32
    )
    masked = pair_mask.astype(jnp.float32)[None, :, :]
    left = (masked * jax.nn.sigmoid(packed[0:H]) * packed[H : 2 * H]).astype(jnp.bfloat16)
    right = (masked * jax.nn.sigmoid(packed[2 * H : 3 * H]) * packed[3 * H :]).astype(jnp.bfloat16)
    gating = jax.nn.sigmoid(
        jnp.einsum(
            "rnc,cd->rnd", normed, gate_weight[layer_index], preferred_element_type=jnp.float32
        )
    )
    lifted_left, lifted_right = (
        lax.all_to_all(left, "row", split_axis=0, concat_axis=1, tiled=True),
        lax.all_to_all(right, "row", split_axis=0, concat_axis=1, tiled=True),
    )
    if layer_index == 0:
        product = jnp.einsum(
            "hik,hjk->hij", lifted_left, lifted_right, preferred_element_type=jnp.float32
        )
    else:
        product = jnp.einsum(
            "hki,hkj->hij", lifted_left, lifted_right, preferred_element_type=jnp.float32
        )
    product = product.astype(jnp.bfloat16)
    out_gain = gain_out[layer_index][:, None, None]
    out_shift = shift_out[layer_index][:, None, None]
    out_proj = out_weight[layer_index]
    returned = lax.all_to_all(product, "row", split_axis=1, concat_axis=0, tiled=True)
    scaled = layer_norm(returned.astype(jnp.float32), out_gain, out_shift, 0).astype(jnp.bfloat16)
    update = jnp.einsum("hrn,hc->rnc", scaled, out_proj, preferred_element_type=jnp.float32)
    return (pair_now.astype(jnp.float32) + gating * update).astype(jnp.bfloat16)


def exchanged(
    pair_rep,
    pair_mask,
    gain_in,
    shift_in,
    proj_weight,
    gate_weight,
    gain_out,
    shift_out,
    out_weight,
):
    current = pair_rep
    for layer_index in range(2):
        current = triangle(
            current,
            pair_mask,
            layer_index,
            gain_in,
            shift_in,
            proj_weight,
            gate_weight,
            gain_out,
            shift_out,
            out_weight,
        )
    return current


def solution(mesh):
    n_row = mesh.shape["row"]

    def shards(pair_rep, *rest):
        per, tokens, _ = pair_rep.shape
        small = pair_rep.size * n_row * 2 <= GATHER_LIMIT
        fits = n_row & (n_row - 1) == 0 and n_row > 1 and tokens % 8 == 0 and per <= MARK_ROWS
        if small and fits:
            return gathered(n_row, pair_rep, *rest)
        return exchanged(pair_rep, *rest)

    in_specs = (
        P(("groups", "row"), None, None),
        P(("groups", "row"), None),
        P(),
        P(),
        P(),
        P(),
        P(),
        P(),
        P(),
    )
    out_specs = P(("groups", "row"), None, None)
    return jax.shard_map(shards, mesh=mesh, in_specs=in_specs, out_specs=out_specs, check_vma=False)
```

```python
import functools

import jax
import jax.numpy as jnp
from jax import lax
from jax.experimental import pallas as pl
from jax.experimental.pallas import tpu as pltpu
from jax.sharding import PartitionSpec as P

EPS = 1e-05
MARK_ROWS = 16
GATHER_LIMIT = 4 << 20


def sigmoid(values):
    return 0.5 * jnp.tanh(0.5 * values) + 0.5


def norm_rows(values, gain, offset):
    mean = jnp.mean(values, axis=-1, keepdims=True)
    centered = values - mean
    variance = jnp.mean(centered * centered, axis=-1, keepdims=True)
    return (centered * lax.rsqrt(variance + EPS) * gain + offset).astype(jnp.bfloat16)


def matmul(left, right):
    return jnp.dot(left, right, preferred_element_type=jnp.float32)


def gated(mask, packed, width):
    value = mask * sigmoid(packed[:, :width]) * packed[:, width:]
    return value.astype(jnp.bfloat16).astype(jnp.float32)


def seat(device, n_row):
    place = device % 2
    step, weight = n_row // 2, 2
    while step > 4:
        place = place + weight * (device // step % 2)
        step, weight = step // 2, 2 * weight
    return place


def seats(n_row):
    return max(2, n_row // 4)


def pack_kernel(n_row, pair_ref, mask_ref, out_ref, mask, at, sems):
    rows = pair_ref.shape[0]
    per = mask_ref.shape[0]
    whole = pltpu.make_async_copy(pair_ref, out_ref.at[0:rows], sems.at[0])
    part = pltpu.make_async_copy(mask_ref, mask, sems.at[1])
    whole.start()
    part.start()
    first = seat(lax.axis_index("row"), n_row) * per
    at[...] = jnp.zeros_like(at)
    part.wait()
    real = jnp.max(mask[...], axis=1, keepdims=True).astype(jnp.float32)
    at[pl.ds(first, per), :] = jnp.broadcast_to(real, (per, at.shape[1]))
    out_ref[rows:, :] = at[...].astype(jnp.bfloat16)
    whole.wait()


def hold(values):
    return pltpu.with_memory_space_constraint(values, pltpu.HBM)


def pack(n_row, pair_rep, pair_mask):
    per, tokens, width = pair_rep.shape
    rows = per * tokens
    extra = -(-seats(n_row) * per // MARK_ROWS) * MARK_ROWS
    hbm = pl.BlockSpec(memory_space=pltpu.HBM)
    return pl.pallas_call(
        functools.partial(pack_kernel, n_row),
        out_shape=jax.ShapeDtypeStruct((rows + extra, width), jnp.bfloat16),
        in_specs=[hbm, hbm],
        out_specs=pl.BlockSpec(memory_space=pltpu.VMEM),
        scratch_shapes=[
            pltpu.VMEM((per, tokens), jnp.int32),
            pltpu.VMEM((extra, width), jnp.float32),
            pltpu.SemaphoreType.DMA((2,)),
        ],
        compiler_params=pltpu.CompilerParams(vmem_limit_bytes=1 << 20),
    )(hold(pair_rep.reshape(rows, width)), hold(pair_mask))


def updates_kernel(
    n_row,
    order,
    steps,
    me_ref,
    *refs,
):
    blocks = refs[: len(steps)]
    gain_in, shift_in, proj_weight, gate_weight, gain_out, shift_out, out_weight = refs[len(steps) : len(steps) + 7]
    out_even, out_odd, pair, valid, left0, right0, gate0, middle, right1, marks = refs[len(steps) + 7 :]
    me = me_ref[0]
    width = out_even.shape[-1]
    tokens = valid.shape[0]
    per = tokens // n_row
    rows = per * tokens
    step_i = 8
    chunk = step_i * tokens
    pitch = tokens + 8

    def run():
        for step, ref in zip(steps, blocks, strict=True):
            marks[...] = ref[len(order) * rows :, :].astype(jnp.float32)
            for slot, place in enumerate(order):
                at = me ^ (step ^ place)
                pair[pl.ds(pl.multiple_of(at * rows, rows), rows), :] = ref[slot * rows : (slot + 1) * rows, :]
                valid[pl.ds(at * per, per), :] = marks[pl.ds(seat(at, n_row) * per, per), :]

        def mask_of(i):
            rowmask = valid[i * step_i : (i + 1) * step_i, :]
            return (rowmask[:, None, :] * valid[...][None, :, :]).reshape(chunk, width)

        for i in range(tokens // step_i):
            at = pl.ds(i * chunk, chunk)
            normed = norm_rows(pair[at, :].astype(jnp.float32), gain_in[0:1, :], shift_in[0:1, :])
            mask = mask_of(i)
            packed = matmul(normed, proj_weight[0])
            left0[at, :] = gated(mask, packed[:, 0 : 2 * width], width)
            right = gated(mask, packed[:, 2 * width :], width)
            for r in range(step_i):
                right0[pl.ds((i * step_i + r) * pitch, tokens), :] = right[r * tokens : (r + 1) * tokens, :]
            gate0[at, :] = sigmoid(matmul(normed, gate_weight[0]))

        for k in range(tokens):
            right1[k * tokens : (k + 1) * tokens, :] = right0[pl.ds(k, tokens, stride=pitch), :]

        for i in range(tokens // step_i):
            at = pl.ds(i * chunk, chunk)
            totals = [jnp.zeros((tokens, width), jnp.float32)] * step_i
            for k in range(tokens):
                row = right1[k * tokens : (k + 1) * tokens, :]
                for r in range(step_i):
                    totals[r] = totals[r] + left0[pl.ds(i * chunk + r * tokens + k, 1), :] * row
            product = jnp.concatenate(totals, axis=0).astype(jnp.bfloat16).astype(jnp.float32)
            scaled = norm_rows(product, gain_out[0:1, :], shift_out[0:1, :])
            moved = pair[at, :].astype(jnp.float32) + gate0[at, :] * matmul(scaled, out_weight[0])
            middle[at, :] = moved.astype(jnp.bfloat16).astype(jnp.float32)

        for i in range(tokens // step_i):
            at = pl.ds(i * chunk, chunk)
            normed = norm_rows(middle[at, :], gain_in[1:2, :], shift_in[1:2, :])
            right0[at, :] = gated(mask_of(i), matmul(normed, proj_weight[1, :, 2 * width :]), width)

        ours = 2 * per
        first = (me - 1) * per
        columns = jnp.concatenate([middle[pl.ds(first + r, tokens, stride=tokens), :] for r in range(ours)], axis=0)
        normed = norm_rows(columns, gain_in[1:2, :], shift_in[1:2, :])
        mask = jnp.concatenate([valid[...] * valid[pl.ds(first + r, 1), :] for r in range(ours)], axis=0)
        left0[0 : 2 * rows, :] = gated(mask, matmul(normed, proj_weight[1, :, 0 : 2 * width]), width)
        totals = [jnp.zeros((tokens, width), jnp.float32)] * ours
        for k in range(tokens):
            row = right0[k * tokens : (k + 1) * tokens, :]
            for r in range(ours):
                totals[r] = totals[r] + left0[r * tokens + k : r * tokens + k + 1, :] * row
        product = jnp.concatenate(totals, axis=0).astype(jnp.bfloat16).astype(jnp.float32)
        scaled = norm_rows(product, gain_out[1:2, :], shift_out[1:2, :])
        held = middle[pl.ds(pl.multiple_of(first * tokens, 2 * rows), 2 * rows), :]
        gate = sigmoid(matmul(norm_rows(held, gain_in[1:2, :], shift_in[1:2, :]), gate_weight[1]))
        result = (held + gate * matmul(scaled, out_weight[1])).astype(jnp.bfloat16)
        out_even[...] = result[0:rows]
        out_odd[...] = result[rows:]

    pl.when(me % 2 == 1)(run)


def updates(n_row, order, steps, tokens, me, blocks, params):
    width = blocks[0].shape[-1]
    rows = tokens * tokens // n_row
    pairs = tokens * tokens
    vmem = pl.BlockSpec(memory_space=pltpu.VMEM)
    return pl.pallas_call(
        functools.partial(updates_kernel, n_row, order, steps),
        out_shape=[jax.ShapeDtypeStruct((rows, width), jnp.bfloat16)] * 2,
        in_specs=[pl.BlockSpec(memory_space=pltpu.SMEM)] + [vmem] * (len(blocks) + 7),
        out_specs=[vmem] * 2,
        scratch_shapes=[
            pltpu.VMEM((pairs, width), jnp.bfloat16),
            pltpu.VMEM((tokens, width), jnp.float32),
        ]
        + [pltpu.VMEM((pairs + 8 * tokens, width), jnp.float32)] * 5
        + [pltpu.VMEM((blocks[0].shape[0] - len(order) * rows, width), jnp.float32)],
        compiler_params=pltpu.CompilerParams(vmem_limit_bytes=8 << 20),
    )(me, *blocks, *params)


def swap(values, step, n_row):
    return lax.ppermute(values, "row", [(i, i ^ step) for i in range(n_row)])


def odd_swap(values, step, n_group, n_row):
    if n_group % 2:
        return swap(values, step, n_row)
    target = [(g, i ^ step) if i % 2 else (g ^ 1, i) for g in range(n_group) for i in range(n_row)]
    pairs = [(source, g * n_row + i) for source, (g, i) in enumerate(target)]
    return lax.ppermute(values, ("groups", "row"), pairs)


def merge(first, second, rows):
    return jnp.concatenate([first[:rows], second[:rows], first[rows:] + second[rows:]], axis=0)


def gathered(n_group, n_row, pair_rep, pair_mask, *params):
    per, tokens, width = pair_rep.shape
    rows = per * tokens
    me = lax.axis_index("row")
    held = pack(n_row, pair_rep, pair_mask)
    held = merge(held, swap(held, 1, n_row), rows)
    order = [0, 1]
    step = n_row // 2
    while step > 4:
        count = len(order)
        held = merge(held, odd_swap(held, step, n_group, n_row), count * rows)
        order = order + [place ^ step for place in order]
        step //= 2
    steps = [0] + list(range(2, 2 * step, 2))
    blocks = [held] + [odd_swap(held, place, n_group, n_row) for place in steps[1:]]
    even, odd = updates(n_row, tuple(order), tuple(steps), tokens, me.astype(jnp.int32).reshape(1), blocks, params)
    out = jnp.where(me % 2 == 1, odd, swap(even, 1, n_row))
    return out.reshape(per, tokens, width)


H = 128


def layer_norm(values, gain, offset, axis):
    mean = jnp.mean(values, axis=axis, keepdims=True)
    centered = values - mean
    variance = jnp.mean(centered * centered, axis=axis, keepdims=True)
    return centered * lax.rsqrt(variance + 1e-05) * gain + offset


def triangle(
    pair_now,
    pair_mask,
    layer_index,
    gain_in,
    shift_in,
    proj_weight,
    gate_weight,
    gain_out,
    shift_out,
    out_weight,
):
    normed = layer_norm(
        pair_now.astype(jnp.float32), gain_in[layer_index], shift_in[layer_index], -1
    ).astype(jnp.bfloat16)
    packed = jnp.einsum(
        "rnc,ch->hrn", normed, proj_weight[layer_index], preferred_element_type=jnp.float32
    )
    masked = pair_mask.astype(jnp.float32)[None, :, :]
    left = (masked * jax.nn.sigmoid(packed[0:H]) * packed[H : 2 * H]).astype(jnp.bfloat16)
    right = (masked * jax.nn.sigmoid(packed[2 * H : 3 * H]) * packed[3 * H :]).astype(jnp.bfloat16)
    gating = jax.nn.sigmoid(
        jnp.einsum(
            "rnc,cd->rnd", normed, gate_weight[layer_index], preferred_element_type=jnp.float32
        )
    )
    lifted_left, lifted_right = (
        lax.all_to_all(left, "row", split_axis=0, concat_axis=1, tiled=True),
        lax.all_to_all(right, "row", split_axis=0, concat_axis=1, tiled=True),
    )
    if layer_index == 0:
        product = jnp.einsum(
            "hik,hjk->hij", lifted_left, lifted_right, preferred_element_type=jnp.float32
        )
    else:
        product = jnp.einsum(
            "hki,hkj->hij", lifted_left, lifted_right, preferred_element_type=jnp.float32
        )
    product = product.astype(jnp.bfloat16)
    out_gain = gain_out[layer_index][:, None, None]
    out_shift = shift_out[layer_index][:, None, None]
    out_proj = out_weight[layer_index]
    returned = lax.all_to_all(product, "row", split_axis=1, concat_axis=0, tiled=True)
    scaled = layer_norm(returned.astype(jnp.float32), out_gain, out_shift, 0).astype(jnp.bfloat16)
    update = jnp.einsum("hrn,hc->rnc", scaled, out_proj, preferred_element_type=jnp.float32)
    return (pair_now.astype(jnp.float32) + gating * update).astype(jnp.bfloat16)


def exchanged(
    pair_rep,
    pair_mask,
    gain_in,
    shift_in,
    proj_weight,
    gate_weight,
    gain_out,
    shift_out,
    out_weight,
):
    current = pair_rep
    for layer_index in range(2):
        current = triangle(
            current,
            pair_mask,
            layer_index,
            gain_in,
            shift_in,
            proj_weight,
            gate_weight,
            gain_out,
            shift_out,
            out_weight,
        )
    return current


def solution(mesh):
    n_group, n_row = mesh.shape["groups"], mesh.shape["row"]

    def shards(pair_rep, *rest):
        per, tokens, _ = pair_rep.shape
        small = pair_rep.size * n_row * 2 <= GATHER_LIMIT
        fits = n_row & (n_row - 1) == 0 and n_row > 3 and tokens % MARK_ROWS == 0
        if small and fits:
            return gathered(n_group, n_row, pair_rep, *rest)
        return exchanged(pair_rep, *rest)

    in_specs = (
        P(("groups", "row"), None, None),
        P(("groups", "row"), None),
        P(),
        P(),
        P(),
        P(),
        P(),
        P(),
        P(),
    )
    out_specs = P(("groups", "row"), None, None)
    return jax.shard_map(shards, mesh=mesh, in_specs=in_specs, out_specs=out_specs, check_vma=False)
```

```python
import functools

import jax
import jax.numpy as jnp
from jax import lax
from jax.experimental import pallas as pl
from jax.experimental.pallas import tpu as pltpu
from jax.sharding import PartitionSpec as P

EPS = 1e-05
MARK_ROWS = 16
GATHER_LIMIT = 4 << 20


def norm_rows(values, gain, offset):
    mean = jnp.mean(values, axis=-1, keepdims=True)
    centered = values - mean
    variance = jnp.mean(centered * centered, axis=-1, keepdims=True)
    return (centered * lax.rsqrt(variance + EPS) * gain + offset).astype(jnp.bfloat16)


def matmul(left, right):
    return jnp.dot(left, right, preferred_element_type=jnp.float32)


def gated(packed, width):
    return (jnp.tanh(packed[:, :width]) + 1.0) * packed[:, width:]


def seat(device, n_row):
    place = device % 2
    step, weight = n_row // 2, 2
    while step > 4:
        place = place + weight * (device // step % 2)
        step, weight = step // 2, 2 * weight
    return place


def seats(n_row):
    return max(2, n_row // 4)


def pack_kernel(n_row, pair_ref, mask_ref, out_ref, mask, at, sems):
    rows = pair_ref.shape[0]
    per = mask_ref.shape[0]
    whole = pltpu.make_async_copy(pair_ref, out_ref.at[0:rows], sems.at[0])
    part = pltpu.make_async_copy(mask_ref, mask, sems.at[1])
    whole.start()
    part.start()
    first = seat(lax.axis_index("row"), n_row) * per
    at[...] = jnp.zeros_like(at)
    part.wait()
    real = jnp.max(mask[...], axis=1, keepdims=True).astype(jnp.float32)
    at[pl.ds(first, per), :] = jnp.broadcast_to(real, (per, at.shape[1]))
    out_ref[rows:, :] = at[...].astype(jnp.bfloat16)
    whole.wait()


def hold(values):
    return pltpu.with_memory_space_constraint(values, pltpu.HBM)


def pack(n_row, pair_rep, pair_mask):
    per, tokens, width = pair_rep.shape
    rows = per * tokens
    extra = -(-seats(n_row) * per // MARK_ROWS) * MARK_ROWS
    hbm = pl.BlockSpec(memory_space=pltpu.HBM)
    return pl.pallas_call(
        functools.partial(pack_kernel, n_row),
        out_shape=jax.ShapeDtypeStruct((rows + extra, width), jnp.bfloat16),
        in_specs=[hbm, hbm],
        out_specs=pl.BlockSpec(memory_space=pltpu.VMEM),
        scratch_shapes=[
            pltpu.VMEM((per, tokens), jnp.int32),
            pltpu.VMEM((extra, width), jnp.float32),
            pltpu.SemaphoreType.DMA((2,)),
        ],
        compiler_params=pltpu.CompilerParams(vmem_limit_bytes=1 << 20),
    )(hold(pair_rep.reshape(rows, width)), hold(pair_mask))


def load_kernel(count, *refs):
    sources, targets, sems = refs[:count], refs[count : 2 * count], refs[2 * count]
    copies = [pltpu.make_async_copy(s, t, sems.at[n]) for n, (s, t) in enumerate(zip(sources, targets, strict=True))]
    for copy in copies:
        copy.start()
    for copy in copies:
        copy.wait()


def load(*arrays):
    count = len(arrays)
    return pl.pallas_call(
        functools.partial(load_kernel, count),
        out_shape=[jax.ShapeDtypeStruct(a.shape, a.dtype) for a in arrays],
        in_specs=[pl.BlockSpec(memory_space=pltpu.HBM)] * count,
        out_specs=[pl.BlockSpec(memory_space=pltpu.VMEM)] * count,
        scratch_shapes=[pltpu.SemaphoreType.DMA((count,))],
        compiler_params=pltpu.CompilerParams(vmem_limit_bytes=4 << 20),
    )(*[hold(a) for a in arrays])


def project(values, gain_in, shift_in, proj_weight, gate_weight):
    half = jnp.array(0.5, jnp.bfloat16)
    width = values.shape[-1]
    normed = norm_rows(values.astype(jnp.float32), gain_in[0:1, :], shift_in[0:1, :])
    packed = matmul(normed, proj_weight[0] * half)
    left, right = gated(packed[:, 0 : 2 * width], width), gated(packed[:, 2 * width :], width)
    return left, right, jnp.tanh(matmul(normed, gate_weight[0] * half)) + 1.0


def project_kernel(block, gain_in, shift_in, proj_weight, gate_weight, left, right, gate):
    values = block[0 : left.shape[0], :]
    left[...], right[...], gate[...] = project(values, gain_in, shift_in, proj_weight, gate_weight)


def project_block(block, pairs, gain_in, shift_in, proj_weight, gate_weight):
    width = block.shape[-1]
    vmem = pl.BlockSpec(memory_space=pltpu.VMEM)
    return pl.pallas_call(
        project_kernel,
        out_shape=[jax.ShapeDtypeStruct((pairs, width), jnp.float32)] * 3,
        in_specs=[vmem] * 5,
        out_specs=[vmem] * 3,
        cost_estimate=pl.CostEstimate(
            flops=10 * pairs * width * width, bytes_accessed=20 * pairs * width, transcendentals=3 * pairs * width
        ),
        compiler_params=pltpu.CompilerParams(vmem_limit_bytes=4 << 20),
    )(block, gain_in, shift_in, proj_weight, gate_weight)


def updates_kernel(n_row, order, steps, me_ref, *refs):
    count = len(steps)
    blocks, refs = refs[:count], refs[count:]
    done, refs = refs[: 3 * (count - 1)], refs[3 * (count - 1) :]
    gain_in, shift_in, proj_weight, gate_weight, gain_out, shift_out, out_weight = refs[:7]
    out_even, out_odd, valid, near, marks, last_left, last_gate, right0, right1, middle, left1 = refs[7:]
    me = me_ref[0]
    width = out_even.shape[-1]
    tokens = valid.shape[0]
    per = tokens // n_row
    rows = per * tokens
    held_tokens = len(order) * per
    chunk = held_tokens * tokens
    pitch = tokens + 8
    lefts = list(done[0::3]) + [last_left]
    gates = list(done[2::3]) + [last_gate]

    def run():
        for n, (step, ref) in enumerate(zip(steps, blocks, strict=True)):
            marks[...] = ref[chunk:, :].astype(jnp.float32)
            for slot, place in enumerate(order):
                at = me ^ (step ^ place)
                real = marks[pl.ds(seat(at, n_row) * per, per), :]
                valid[pl.ds(at * per, per), :] = real
                near[n * held_tokens + slot * per : n * held_tokens + (slot + 1) * per, :] = real

        def place_right(n, values):
            for slot, place in enumerate(order):
                at = me ^ (steps[n] ^ place)
                for t in range(per):
                    row = pl.multiple_of((at * per + t) * pitch, 8)
                    start = (slot * per + t) * tokens
                    right0[pl.ds(row, tokens), :] = values[start : start + tokens, :]

        left, right, gate = project(blocks[-1][0:chunk, :], gain_in, shift_in, proj_weight, gate_weight)
        last_left[...] = left
        last_gate[...] = gate
        place_right(count - 1, right)
        for n in range(count - 1):
            place_right(n, done[3 * n + 1])

        half = jnp.array(0.5, jnp.bfloat16)
        real = valid[...]
        gate_out = out_weight[0] * half
        for k in range(tokens):
            right1[k * tokens : (k + 1) * tokens, :] = right0[pl.ds(k, tokens, stride=pitch), :] * valid[k : k + 1, :]

        for n in range(count):
            totals = [jnp.zeros((tokens, width), jnp.float32)] * held_tokens
            for k in range(tokens):
                row = right1[k * tokens : (k + 1) * tokens, :]
                for r in range(held_tokens):
                    totals[r] = totals[r] + lefts[n][r * tokens + k : r * tokens + k + 1, :] * row
            first = n * held_tokens
            product = jnp.concatenate(
                [t * (real * near[first + r : first + r + 1, :]) for r, t in enumerate(totals)], axis=0
            )
            scaled = norm_rows(product, gain_out[0:1, :], shift_out[0:1, :])
            moved = blocks[n][0:chunk, :].astype(jnp.float32) + gates[n][...] * matmul(scaled, gate_out)
            middle[n * chunk : (n + 1) * chunk, :] = moved

        proj, gate_in, gate_out = proj_weight[1] * half, gate_weight[1] * half, out_weight[1] * half
        for n in range(count):
            at = pl.ds(n * chunk, chunk)
            normed = norm_rows(middle[at, :], gain_in[1:2, :], shift_in[1:2, :])
            right0[at, :] = gated(matmul(normed, proj[:, 2 * width :]), width)

        ours = 2 * per
        first = (me - 1) * per
        columns = jnp.concatenate([middle[pl.ds(first + r, tokens, stride=tokens), :] for r in range(ours)], axis=0)
        normed = norm_rows(columns, gain_in[1:2, :], shift_in[1:2, :])
        left1[...] = gated(matmul(normed, proj[:, 0 : 2 * width]), width) * jnp.concatenate([near[...]] * ours, axis=0)
        totals = [jnp.zeros((tokens, width), jnp.float32)] * ours
        for k in range(tokens):
            row = right0[k * tokens : (k + 1) * tokens, :]
            for r in range(ours):
                totals[r] = totals[r] + left1[r * tokens + k : r * tokens + k + 1, :] * row
        product = jnp.concatenate([t * (real * valid[pl.ds(first + r, 1), :]) for r, t in enumerate(totals)], axis=0)
        scaled = norm_rows(product, gain_out[1:2, :], shift_out[1:2, :])
        held = jnp.concatenate([middle[rows : 2 * rows, :], middle[0:rows, :]], axis=0)
        gate = jnp.tanh(matmul(norm_rows(held, gain_in[1:2, :], shift_in[1:2, :]), gate_in)) + 1.0
        result = (held + gate * matmul(scaled, gate_out)).astype(jnp.bfloat16)
        out_even[...] = result[0:rows]
        out_odd[...] = result[rows:]

    pl.when(me % 2 == 1)(run)


def updates(n_row, order, steps, tokens, me, blocks, params):
    width = blocks[0].shape[-1]
    rows = tokens * tokens // n_row
    pairs = tokens * tokens
    chunk = len(order) * rows
    gain_in, shift_in, proj_weight, gate_weight = params[:4]
    done = [project_block(block, chunk, gain_in, shift_in, proj_weight, gate_weight) for block in blocks[:-1]]
    done = [array for arrays in done for array in arrays]
    vmem = pl.BlockSpec(memory_space=pltpu.VMEM)
    shapes = [(tokens, width)] * 2 + [(blocks[0].shape[0] - chunk, width)]
    shapes += [(chunk, width)] * 2 + [(pairs + 8 * tokens, width)] + [(pairs, width)] * 2 + [(2 * rows, width)]
    return pl.pallas_call(
        functools.partial(updates_kernel, n_row, order, steps),
        out_shape=[jax.ShapeDtypeStruct((rows, width), jnp.bfloat16)] * 2,
        in_specs=[pl.BlockSpec(memory_space=pltpu.SMEM)] + [vmem] * (len(blocks) + len(done) + 7),
        out_specs=[vmem] * 2,
        scratch_shapes=[pltpu.VMEM(shape, jnp.float32) for shape in shapes],
        compiler_params=pltpu.CompilerParams(vmem_limit_bytes=8 << 20),
    )(me, *blocks, *done, *params)


def swap(values, step, n_row):
    return lax.ppermute(values, "row", [(i, i ^ step) for i in range(n_row)])


def odd_swap(values, step, n_group, n_row):
    if n_group % 2:
        return swap(values, step, n_row)
    target = [(g, i ^ step) if i % 2 else (g ^ 1, i) for g in range(n_group) for i in range(n_row)]
    pairs = [(source, g * n_row + i) for source, (g, i) in enumerate(target)]
    return lax.ppermute(values, ("groups", "row"), pairs)


def merge(first, second, rows):
    return jnp.concatenate([first[:rows], second[:rows], first[rows:] + second[rows:]], axis=0)


def gathered(n_group, n_row, pair_rep, pair_mask, *params):
    per, tokens, width = pair_rep.shape
    rows = per * tokens
    me = lax.axis_index("row")
    held = pack(n_row, pair_rep, pair_mask)
    held = merge(held, swap(held, 1, n_row), rows)
    order = [0, 1]
    step = n_row // 2
    while step > 4:
        count = len(order)
        held = merge(held, odd_swap(held, step, n_group, n_row), count * rows)
        order = order + [place ^ step for place in order]
        step //= 2
    held, *params = lax.optimization_barrier((held, *load(*params)))
    steps = [0] + list(range(2, 2 * step, 2))
    blocks = [held] + [odd_swap(held, place, n_group, n_row) for place in steps[1:]]
    even, odd = updates(n_row, tuple(order), tuple(steps), tokens, me.astype(jnp.int32).reshape(1), blocks, params)
    out = jnp.where(me % 2 == 1, odd, swap(even, 1, n_row))
    return out.reshape(per, tokens, width)


H = 128


def layer_norm(values, gain, offset, axis):
    mean = jnp.mean(values, axis=axis, keepdims=True)
    centered = values - mean
    variance = jnp.mean(centered * centered, axis=axis, keepdims=True)
    return centered * lax.rsqrt(variance + 1e-05) * gain + offset


def triangle(
    pair_now,
    pair_mask,
    layer_index,
    gain_in,
    shift_in,
    proj_weight,
    gate_weight,
    gain_out,
    shift_out,
    out_weight,
):
    normed = layer_norm(
        pair_now.astype(jnp.float32), gain_in[layer_index], shift_in[layer_index], -1
    ).astype(jnp.bfloat16)
    packed = jnp.einsum(
        "rnc,ch->hrn", normed, proj_weight[layer_index], preferred_element_type=jnp.float32
    )
    masked = pair_mask.astype(jnp.float32)[None, :, :]
    left = (masked * jax.nn.sigmoid(packed[0:H]) * packed[H : 2 * H]).astype(jnp.bfloat16)
    right = (masked * jax.nn.sigmoid(packed[2 * H : 3 * H]) * packed[3 * H :]).astype(jnp.bfloat16)
    gating = jax.nn.sigmoid(
        jnp.einsum(
            "rnc,cd->rnd", normed, gate_weight[layer_index], preferred_element_type=jnp.float32
        )
    )
    lifted_left, lifted_right = (
        lax.all_to_all(left, "row", split_axis=0, concat_axis=1, tiled=True),
        lax.all_to_all(right, "row", split_axis=0, concat_axis=1, tiled=True),
    )
    if layer_index == 0:
        product = jnp.einsum(
            "hik,hjk->hij", lifted_left, lifted_right, preferred_element_type=jnp.float32
        )
    else:
        product = jnp.einsum(
            "hki,hkj->hij", lifted_left, lifted_right, preferred_element_type=jnp.float32
        )
    product = product.astype(jnp.bfloat16)
    out_gain = gain_out[layer_index][:, None, None]
    out_shift = shift_out[layer_index][:, None, None]
    out_proj = out_weight[layer_index]
    returned = lax.all_to_all(product, "row", split_axis=1, concat_axis=0, tiled=True)
    scaled = layer_norm(returned.astype(jnp.float32), out_gain, out_shift, 0).astype(jnp.bfloat16)
    update = jnp.einsum("hrn,hc->rnc", scaled, out_proj, preferred_element_type=jnp.float32)
    return (pair_now.astype(jnp.float32) + gating * update).astype(jnp.bfloat16)


def exchanged(
    pair_rep,
    pair_mask,
    gain_in,
    shift_in,
    proj_weight,
    gate_weight,
    gain_out,
    shift_out,
    out_weight,
):
    current = pair_rep
    for layer_index in range(2):
        current = triangle(
            current,
            pair_mask,
            layer_index,
            gain_in,
            shift_in,
            proj_weight,
            gate_weight,
            gain_out,
            shift_out,
            out_weight,
        )
    return current


def solution(mesh):
    n_group, n_row = mesh.shape["groups"], mesh.shape["row"]

    def shards(pair_rep, *rest):
        per, tokens, _ = pair_rep.shape
        small = pair_rep.size * n_row * 2 <= GATHER_LIMIT
        fits = n_row & (n_row - 1) == 0 and n_row > 3 and tokens % MARK_ROWS == 0
        if small and fits:
            return gathered(n_group, n_row, pair_rep, *rest)
        return exchanged(pair_rep, *rest)

    in_specs = (
        P(("groups", "row"), None, None),
        P(("groups", "row"), None),
        P(),
        P(),
        P(),
        P(),
        P(),
        P(),
        P(),
    )
    out_specs = P(("groups", "row"), None, None)
    return jax.shard_map(shards, mesh=mesh, in_specs=in_specs, out_specs=out_specs, check_vma=False)
```

```python
import functools

import jax
import jax.numpy as jnp
from jax import lax
from jax.experimental import pallas as pl
from jax.experimental.pallas import tpu as pltpu
from jax.sharding import PartitionSpec as P

EPS = 1e-05
MARK_ROWS = 16
GATHER_LIMIT = 4 << 20


def norm_rows(values, gain, offset):
    mean = jnp.mean(values, axis=-1, keepdims=True)
    centered = values - mean
    variance = jnp.mean(centered * centered, axis=-1, keepdims=True)
    return (centered * lax.rsqrt(variance + EPS) * gain + offset).astype(jnp.bfloat16)


def matmul(left, right):
    return jnp.dot(left, right, preferred_element_type=jnp.float32)


def gated(packed, width):
    return (jnp.tanh(packed[:, :width]) + 1.0) * packed[:, width:]


def seat(device, n_row):
    place = device % 2
    step, weight = n_row // 2, 2
    while step > 4:
        place = place + weight * (device // step % 2)
        step, weight = step // 2, 2 * weight
    return place


def seats(n_row):
    return max(2, n_row // 4)


def pack_kernel(n_row, pair_ref, mask_ref, out_ref, mask, marks, sems):
    rows = pair_ref.shape[0]
    per, tokens = mask_ref.shape
    width = out_ref.shape[1]
    whole = pltpu.make_async_copy(pair_ref, out_ref.at[0:rows], sems.at[0])
    part = pltpu.make_async_copy(mask_ref, mask, sems.at[1])
    part.start()
    whole.start()
    first = seat(lax.axis_index("row"), n_row) * per
    marks[...] = jnp.zeros_like(marks)
    diagonal = lax.broadcasted_iota(jnp.int32, (tokens, tokens), 0)
    diagonal = diagonal == lax.broadcasted_iota(jnp.int32, (tokens, tokens), 1)
    part.wait()
    mine = mask[...].astype(jnp.float32)
    marks[pl.ds(first, per), :] = jnp.broadcast_to(jnp.max(mine, axis=1, keepdims=True), (per, width))
    seen = jnp.where(diagonal, jnp.max(mine, axis=0, keepdims=True), 0.0)
    seen = jnp.broadcast_to(jnp.sum(seen, axis=1, keepdims=True), (tokens, width))
    out_ref[rows:, :] = jnp.concatenate([marks[...], seen], axis=0).astype(jnp.bfloat16)
    whole.wait()


def hold(values):
    return pltpu.with_memory_space_constraint(values, pltpu.HBM)


def mark_rows(n_row, per):
    return -(-seats(n_row) * per // MARK_ROWS) * MARK_ROWS


def pack(n_row, pair_rep, pair_mask):
    per, tokens, width = pair_rep.shape
    rows = per * tokens
    extra = mark_rows(n_row, per)
    hbm = pl.BlockSpec(memory_space=pltpu.HBM)
    return pl.pallas_call(
        functools.partial(pack_kernel, n_row),
        out_shape=jax.ShapeDtypeStruct((rows + extra + tokens, width), jnp.bfloat16),
        in_specs=[hbm, hbm],
        out_specs=pl.BlockSpec(memory_space=pltpu.VMEM),
        scratch_shapes=[
            pltpu.VMEM((per, tokens), jnp.int32),
            pltpu.VMEM((extra, width), jnp.float32),
            pltpu.SemaphoreType.DMA((2,)),
        ],
        compiler_params=pltpu.CompilerParams(vmem_limit_bytes=1 << 20),
    )(hold(pair_rep.reshape(rows, width)), hold(pair_mask))


def load_kernel(count, *refs):
    sources, targets, sems = refs[:count], refs[count : 2 * count], refs[2 * count]
    copies = [pltpu.make_async_copy(s, t, sems.at[n]) for n, (s, t) in enumerate(zip(sources, targets, strict=True))]
    for copy in copies:
        copy.start()
    for copy in copies:
        copy.wait()


def load(*arrays):
    count = len(arrays)
    return pl.pallas_call(
        functools.partial(load_kernel, count),
        out_shape=[jax.ShapeDtypeStruct(a.shape, a.dtype) for a in arrays],
        in_specs=[pl.BlockSpec(memory_space=pltpu.HBM)] * count,
        out_specs=[pl.BlockSpec(memory_space=pltpu.VMEM)] * count,
        scratch_shapes=[pltpu.SemaphoreType.DMA((count,))],
        compiler_params=pltpu.CompilerParams(vmem_limit_bytes=4 << 20),
    )(*[hold(a) for a in arrays])


class Layout:
    def __init__(self, n_row, order, steps, tokens):
        self.n_row, self.order, self.steps, self.tokens = n_row, order, steps, tokens
        self.per = tokens // n_row
        self.group = len(order) * self.per
        self.chunk = self.group * tokens
        self.pitch = tokens + 8
        self.marks = mark_rows(n_row, self.per)

    def places(self):
        me = lax.axis_index("row")
        for n, step in enumerate(self.steps):
            for slot, place in enumerate(self.order):
                yield n * self.group + slot * self.per, me ^ (step ^ place)

    def pairs(self, n):
        return [(n, q) for q in range(n + 1)] + [(p, n) for p in range(n)]


def prepare(lay, n, block, gain_in, shift_in, proj_weight, gate_weight, outs, scratch):
    z, left, right, gate, near = outs
    marks, rough, seen = scratch
    tokens, group, per, chunk, pitch = lay.tokens, lay.group, lay.per, lay.chunk, lay.pitch
    width = z.shape[-1]
    half = jnp.array(0.5, jnp.bfloat16)
    places = list(lay.places())
    marks[...] = block[chunk:, :].astype(jnp.float32)
    for first, at in places:
        seen[first : first + per, :] = jnp.minimum(marks[pl.ds(lay.marks + at * per, per), :], 1.0)
    for first, at in places[n * len(lay.order) : (n + 1) * len(lay.order)]:
        near[first - n * group : first - n * group + per, :] = marks[pl.ds(seat(at, lay.n_row) * per, per), :]
    for t in range(group):
        rough[t * pitch : t * pitch + tokens, :] = block[t * tokens : (t + 1) * tokens, :].astype(jnp.float32)
    for first, at in places:
        for t in range(per):
            z[pl.ds(first + t, group, stride=pitch), :] = rough[pl.ds(at * per + t, group, stride=pitch), :]
    values = jnp.concatenate([z[t * pitch : t * pitch + tokens, :] for t in range(group)], axis=0)
    normed = norm_rows(values, gain_in[0:1, :], shift_in[0:1, :])
    packed = matmul(normed, proj_weight[0] * half)
    rights = gated(packed[:, 2 * width :], width)
    for t in range(group):
        rough[t * pitch : t * pitch + tokens, :] = rights[t * tokens : (t + 1) * tokens, :]
    left[...] = gated(packed[:, 0 : 2 * width], width)
    for k in range(tokens):
        right[k * group : (k + 1) * group, :] = rough[pl.ds(k, group, stride=pitch), :] * seen[k : k + 1, :]
    gate[...] = jnp.tanh(matmul(normed, gate_weight[0] * half)) + 1.0


def block_sums(lay, left, rights):
    tokens, group = lay.tokens, lay.group
    width = left.shape[-1]
    totals = [[jnp.zeros((group, width), jnp.float32)] * group for _ in rights]
    for k in range(tokens):
        rows = [right[k * group : (k + 1) * group, :] for right in rights]
        for i in range(group):
            value = left[i * tokens + k : i * tokens + k + 1, :]
            for q, row in enumerate(rows):
                totals[q][i] = totals[q][i] + value * row
    return totals


def complete(lay, n, lefts, rights, sums):
    size = lay.group * lay.group
    totals = block_sums(lay, lefts[n], rights)
    for p in range(n):
        totals += block_sums(lay, lefts[p], rights[n : n + 1])
    for place, total in enumerate(totals):
        sums[place * size : (place + 1) * size, :] = jnp.concatenate(total, axis=0)


def group_kernel(lay, n, block, *refs):
    lefts, rights, refs = refs[:n], refs[n : 2 * n], refs[2 * n :]
    params, outs, sums, scratch = refs[:4], refs[4:9], refs[9], refs[10:]
    prepare(lay, n, block, *params, outs, scratch)
    complete(lay, n, [*lefts, outs[1]], [*rights, outs[2]], sums)


def group_shapes(lay, n, width):
    count = len(lay.pairs(n)) * lay.group * lay.group
    rows = [lay.group * lay.pitch, lay.chunk, lay.chunk, lay.chunk, lay.group, count]
    return [(r, width) for r in rows]


def scratch_shapes(lay, width):
    rows = [lay.marks + lay.tokens, lay.group * lay.pitch, lay.tokens]
    return [pltpu.VMEM((r, width), jnp.float32) for r in rows]


def complete_group(lay, n, block, lefts, rights, params):
    width = block.shape[-1]
    vmem = pl.BlockSpec(memory_space=pltpu.VMEM)
    shapes = group_shapes(lay, n, width)
    sums = shapes[-1][0] * lay.tokens * width
    return pl.pallas_call(
        functools.partial(group_kernel, lay, n),
        out_shape=[jax.ShapeDtypeStruct(shape, jnp.float32) for shape in shapes],
        in_specs=[vmem] * (5 + 2 * n),
        out_specs=[vmem] * len(shapes),
        scratch_shapes=scratch_shapes(lay, width),
        cost_estimate=pl.CostEstimate(
            flops=10 * lay.chunk * width * width + 2 * sums,
            bytes_accessed=20 * lay.chunk * width,
            transcendentals=3 * lay.chunk * width,
        ),
        compiler_params=pltpu.CompilerParams(vmem_limit_bytes=4 << 20),
    )(block, *lefts, *rights, *params)


def updates_kernel(lay, block, *refs):
    last = len(lay.steps) - 1
    done = [refs[6 * n : 6 * n + 6] for n in range(last)]
    refs = refs[6 * last :]
    gain_in, shift_in, proj_weight, gate_weight, gain_out, shift_out, out_weight = refs[:7]
    out_even, out_odd = refs[7:9]
    own, scratch = refs[9:15], refs[15:18]
    right1, middle, left1, result1 = refs[18:]
    tokens, per, group, chunk, pitch = lay.tokens, lay.per, lay.group, lay.chunk, lay.pitch
    width = out_even.shape[-1]
    rows = per * tokens
    done = done + [own]

    def run():
        prepare(lay, last, block, gain_in, shift_in, proj_weight, gate_weight, own[:5], scratch)
        complete(lay, last, [arrays[1] for arrays in done], [arrays[2] for arrays in done], own[5])

        half = jnp.array(0.5, jnp.bfloat16)
        real = jnp.concatenate([arrays[4][...] for arrays in done], axis=0)
        gate_out = out_weight[0] * half
        for p in range(last + 1):
            z, _, _, gate, near, _ = done[p]
            products = []
            for i in range(group):
                parts = []
                for q in range(last + 1):
                    n = max(p, q)
                    start = (lay.pairs(n).index((p, q)) * group + i) * group
                    parts.append(done[n][5][start : start + group, :])
                products.append(jnp.concatenate(parts, axis=0) * (real * near[i : i + 1, :]))
            scaled = norm_rows(jnp.concatenate(products, axis=0), gain_out[0:1, :], shift_out[0:1, :])
            held = jnp.concatenate([z[t * pitch : t * pitch + tokens, :] for t in range(group)], axis=0)
            middle[p * chunk : (p + 1) * chunk, :] = held + gate[...] * matmul(scaled, gate_out)

        proj, gate_in, gate_out = proj_weight[1] * half, gate_weight[1] * half, out_weight[1] * half
        for p in range(last + 1):
            at = slice(p * chunk, (p + 1) * chunk)
            normed = norm_rows(middle[at, :], gain_in[1:2, :], shift_in[1:2, :])
            right1[at, :] = gated(matmul(normed, proj[:, 2 * width :]), width)

        ours = [*range(per, 2 * per), *range(per)]
        columns = jnp.concatenate([middle[pl.ds(r, tokens, stride=tokens), :] for r in ours], axis=0)
        normed = norm_rows(columns, gain_in[1:2, :], shift_in[1:2, :])
        left1[...] = gated(matmul(normed, proj[:, 0 : 2 * width]), width) * jnp.concatenate([real] * len(ours), axis=0)
        totals = [jnp.zeros((tokens, width), jnp.float32)] * len(ours)
        for k in range(tokens):
            row = right1[k * tokens : (k + 1) * tokens, :]
            for r in range(len(ours)):
                totals[r] = totals[r] + left1[r * tokens + k : r * tokens + k + 1, :] * row
        near = done[0][4]
        product = jnp.concatenate([t * (real * near[r : r + 1, :]) for r, t in zip(ours, totals, strict=True)], axis=0)
        scaled = norm_rows(product, gain_out[1:2, :], shift_out[1:2, :])
        held = jnp.concatenate([middle[rows : 2 * rows, :], middle[0:rows, :]], axis=0)
        gate = jnp.tanh(matmul(norm_rows(held, gain_in[1:2, :], shift_in[1:2, :]), gate_in)) + 1.0
        result = held + gate * matmul(scaled, gate_out)
        rough = scratch[1]
        for r in range(len(ours)):
            rough[r * pitch : r * pitch + tokens, :] = result[r * tokens : (r + 1) * tokens, :]
        for first, at in lay.places():
            for t in range(per):
                row = rough[pl.ds(first + t, len(ours), stride=pitch), :]
                result1[pl.ds(at * per + t, len(ours), stride=pitch), :] = row
        halves = [result1[r * pitch : r * pitch + tokens, :] for r in range(len(ours))]
        out_even[...] = jnp.concatenate(halves[:per], axis=0).astype(jnp.bfloat16)
        out_odd[...] = jnp.concatenate(halves[per:], axis=0).astype(jnp.bfloat16)

    pl.when(lax.axis_index("row") % 2 == 1)(run)


def updates(lay, blocks, params):
    width = blocks[0].shape[-1]
    rows = lay.per * lay.tokens
    pairs = lay.tokens * lay.tokens
    done = []
    for n, block in enumerate(blocks[:-1]):
        lefts, rights = [arrays[1] for arrays in done], [arrays[2] for arrays in done]
        done.append(complete_group(lay, n, block, lefts, rights, params[:4]))
    arrays = [array for arrays in done for array in arrays]
    vmem = pl.BlockSpec(memory_space=pltpu.VMEM)
    shapes = group_shapes(lay, len(blocks) - 1, width)
    tail = [(pairs, width), (pairs, width), (2 * rows, width), (2 * lay.per * lay.pitch, width)]
    return pl.pallas_call(
        functools.partial(updates_kernel, lay),
        out_shape=[jax.ShapeDtypeStruct((rows, width), jnp.bfloat16)] * 2,
        in_specs=[vmem] * (1 + len(arrays) + 7),
        out_specs=[vmem] * 2,
        scratch_shapes=[pltpu.VMEM(shape, jnp.float32) for shape in shapes]
        + scratch_shapes(lay, width)
        + [pltpu.VMEM(shape, jnp.float32) for shape in tail],
        compiler_params=pltpu.CompilerParams(vmem_limit_bytes=8 << 20),
    )(blocks[-1], *arrays, *params)


def swap(values, step, n_row):
    return lax.ppermute(values, "row", [(i, i ^ step) for i in range(n_row)])


def odd_swap(values, step, n_group, n_row):
    if n_group % 2:
        return swap(values, step, n_row)
    target = [(g, i ^ step) if i % 2 else (g ^ 1, i) for g in range(n_group) for i in range(n_row)]
    pairs = [(source, g * n_row + i) for source, (g, i) in enumerate(target)]
    return lax.ppermute(values, ("groups", "row"), pairs)


def merge(first, second, rows):
    return jnp.concatenate([first[:rows], second[:rows], first[rows:] + second[rows:]], axis=0)


def gathered(n_group, n_row, pair_rep, pair_mask, *params):
    per, tokens, width = pair_rep.shape
    rows = per * tokens
    me = lax.axis_index("row")
    held = pack(n_row, pair_rep, pair_mask)
    held = merge(held, swap(held, 1, n_row), rows)
    order = [0, 1]
    step = n_row // 2
    while step > 4:
        count = len(order)
        held = merge(held, odd_swap(held, step, n_group, n_row), count * rows)
        order = order + [place ^ step for place in order]
        step //= 2
    held, *params = lax.optimization_barrier((held, *load(*params)))
    steps = [0] + list(range(2, 2 * step, 2))
    blocks = [held] + [odd_swap(held, place, n_group, n_row) for place in steps[1:]]
    even, odd = updates(Layout(n_row, order, steps, tokens), blocks, params)
    out = jnp.where(me % 2 == 1, odd, swap(even, 1, n_row))
    return out.reshape(per, tokens, width)


H = 128


def layer_norm(values, gain, offset, axis):
    mean = jnp.mean(values, axis=axis, keepdims=True)
    centered = values - mean
    variance = jnp.mean(centered * centered, axis=axis, keepdims=True)
    return centered * lax.rsqrt(variance + 1e-05) * gain + offset


def triangle(
    pair_now,
    pair_mask,
    layer_index,
    gain_in,
    shift_in,
    proj_weight,
    gate_weight,
    gain_out,
    shift_out,
    out_weight,
):
    normed = layer_norm(
        pair_now.astype(jnp.float32), gain_in[layer_index], shift_in[layer_index], -1
    ).astype(jnp.bfloat16)
    packed = jnp.einsum(
        "rnc,ch->hrn", normed, proj_weight[layer_index], preferred_element_type=jnp.float32
    )
    masked = pair_mask.astype(jnp.float32)[None, :, :]
    left = (masked * jax.nn.sigmoid(packed[0:H]) * packed[H : 2 * H]).astype(jnp.bfloat16)
    right = (masked * jax.nn.sigmoid(packed[2 * H : 3 * H]) * packed[3 * H :]).astype(jnp.bfloat16)
    gating = jax.nn.sigmoid(
        jnp.einsum(
            "rnc,cd->rnd", normed, gate_weight[layer_index], preferred_element_type=jnp.float32
        )
    )
    lifted_left, lifted_right = (
        lax.all_to_all(left, "row", split_axis=0, concat_axis=1, tiled=True),
        lax.all_to_all(right, "row", split_axis=0, concat_axis=1, tiled=True),
    )
    if layer_index == 0:
        product = jnp.einsum(
            "hik,hjk->hij", lifted_left, lifted_right, preferred_element_type=jnp.float32
        )
    else:
        product = jnp.einsum(
            "hki,hkj->hij", lifted_left, lifted_right, preferred_element_type=jnp.float32
        )
    product = product.astype(jnp.bfloat16)
    out_gain = gain_out[layer_index][:, None, None]
    out_shift = shift_out[layer_index][:, None, None]
    out_proj = out_weight[layer_index]
    returned = lax.all_to_all(product, "row", split_axis=1, concat_axis=0, tiled=True)
    scaled = layer_norm(returned.astype(jnp.float32), out_gain, out_shift, 0).astype(jnp.bfloat16)
    update = jnp.einsum("hrn,hc->rnc", scaled, out_proj, preferred_element_type=jnp.float32)
    return (pair_now.astype(jnp.float32) + gating * update).astype(jnp.bfloat16)


def exchanged(
    pair_rep,
    pair_mask,
    gain_in,
    shift_in,
    proj_weight,
    gate_weight,
    gain_out,
    shift_out,
    out_weight,
):
    current = pair_rep
    for layer_index in range(2):
        current = triangle(
            current,
            pair_mask,
            layer_index,
            gain_in,
            shift_in,
            proj_weight,
            gate_weight,
            gain_out,
            shift_out,
            out_weight,
        )
    return current


def solution(mesh):
    n_group, n_row = mesh.shape["groups"], mesh.shape["row"]

    def shards(pair_rep, *rest):
        per, tokens, _ = pair_rep.shape
        small = pair_rep.size * n_row * 2 <= GATHER_LIMIT
        fits = n_row & (n_row - 1) == 0 and n_row > 3 and tokens % 32 == 0
        if small and fits:
            return gathered(n_group, n_row, pair_rep, *rest)
        return exchanged(pair_rep, *rest)

    in_specs = (
        P(("groups", "row"), None, None),
        P(("groups", "row"), None),
        P(),
        P(),
        P(),
        P(),
        P(),
        P(),
        P(),
    )
    out_specs = P(("groups", "row"), None, None)
    return jax.shard_map(shards, mesh=mesh, in_specs=in_specs, out_specs=out_specs, check_vma=False)
```

```python
import functools

import jax
import jax.numpy as jnp
from jax import lax
from jax.experimental import pallas as pl
from jax.experimental.pallas import tpu as pltpu
from jax.sharding import PartitionSpec as P

EPS = 1e-05
MARK_ROWS = 16
GATHER_LIMIT = 4 << 20


def matmul(left, right):
    return jnp.dot(left, right, preferred_element_type=jnp.float32)


def normed_matmul(values, gain, weights, biases):
    centered = values - jnp.mean(values, axis=-1, keepdims=True)
    scale = lax.rsqrt(jnp.mean(centered * centered, axis=-1, keepdims=True) + EPS)
    factor = (centered * gain).astype(jnp.bfloat16)
    return [matmul(factor, weight) * scale + bias for weight, bias in zip(weights, biases, strict=True)]


def gated(packed, width):
    return (jnp.tanh(packed[:, :width]) + 1.0) * packed[:, width:]


def seat(device, n_row):
    place = device % 2
    step, weight = n_row // 2, 2
    while step > 4:
        place = place + weight * (device // step % 2)
        step, weight = step // 2, 2 * weight
    return place


def seats(n_row):
    return max(2, n_row // 4)


def pack_kernel(n_row, pair_ref, mask_ref, out_ref, mask, marks, sems):
    rows = pair_ref.shape[0]
    per, tokens = mask_ref.shape
    width = out_ref.shape[1]
    whole = pltpu.make_async_copy(pair_ref, out_ref.at[0:rows], sems.at[0])
    part = pltpu.make_async_copy(mask_ref, mask, sems.at[1])
    part.start()
    whole.start()
    first = seat(lax.axis_index("row"), n_row) * per
    last = seats(n_row) * per
    marks[...] = jnp.zeros_like(marks)
    part.wait()
    mine = mask[...].astype(jnp.float32)
    marks[pl.ds(first, per), :] = jnp.broadcast_to(jnp.max(mine, axis=1, keepdims=True), (per, width))
    marks[last : last + 1, 0:tokens] = jnp.max(mine, axis=0, keepdims=True)
    out_ref[rows:, :] = marks[...].astype(jnp.bfloat16)
    whole.wait()


def hold(values):
    return pltpu.with_memory_space_constraint(values, pltpu.HBM)


def mark_rows(n_row, per):
    return -(-(seats(n_row) * per + 1) // MARK_ROWS) * MARK_ROWS


def pack(n_row, pair_rep, pair_mask):
    per, tokens, width = pair_rep.shape
    rows = per * tokens
    extra = mark_rows(n_row, per)
    hbm = pl.BlockSpec(memory_space=pltpu.HBM)
    return pl.pallas_call(
        functools.partial(pack_kernel, n_row),
        out_shape=jax.ShapeDtypeStruct((rows + extra, width), jnp.bfloat16),
        in_specs=[hbm, hbm],
        out_specs=pl.BlockSpec(memory_space=pltpu.VMEM),
        scratch_shapes=[
            pltpu.VMEM((per, tokens), jnp.int32),
            pltpu.VMEM((extra, width), jnp.float32),
            pltpu.SemaphoreType.DMA((2,)),
        ],
        compiler_params=pltpu.CompilerParams(vmem_limit_bytes=1 << 20),
    )(hold(pair_rep.reshape(rows, width)), hold(pair_mask))


def load_kernel(sources, targets):
    (gain_in, shift_in, proj, gate, gain_out, shift_out, out), sems = sources[:7], sources[-1]
    held = sources[7:-1]
    copies = [
        pltpu.make_async_copy(source, target, sems.at[n])
        for n, (source, target) in enumerate(
            zip((proj, gate, out, shift_in, shift_out, gain_in, gain_out), (*held, targets[0], targets[1]), strict=True)
        )
    ]
    for copy in copies:
        copy.start()
    for copy in copies:
        copy.wait()
    proj, gate, out, shift_in, shift_out = held
    _, _, proj_half, gate_half, out_half, proj_bias, gate_bias, out_bias = targets
    half = jnp.array(0.5, jnp.bfloat16)
    for weight, halved, bias, shift in (
        (proj, proj_half, proj_bias, shift_in),
        (gate, gate_half, gate_bias, shift_in),
        (out, out_half, out_bias, shift_out),
    ):
        halved[...] = weight[...] * half
        exact = shift[...]
        high = exact.astype(jnp.bfloat16)
        low = (exact - high.astype(jnp.float32)).astype(jnp.bfloat16)
        rows = jnp.concatenate([high, low] + [jnp.zeros_like(high)] * 6, axis=0)
        for u in range(2):
            both = matmul(rows, weight[u])
            bias[u : u + 1, :] = 0.5 * (both[u : u + 1, :] + both[u + 2 : u + 3, :])


def load(gain_in, shift_in, proj, gate, gain_out, shift_out, out):
    arrays = (gain_in, shift_in, proj, gate, gain_out, shift_out, out)
    weights = (proj, gate, out)
    shapes = [(a.shape, a.dtype) for a in (gain_in, gain_out, *weights)]
    shapes += [((a.shape[0], a.shape[2]), jnp.float32) for a in weights]
    vmem = pl.BlockSpec(memory_space=pltpu.VMEM)

    def kernel(*refs):
        load_kernel((*refs[:7], *refs[7 + len(shapes) :]), refs[7 : 7 + len(shapes)])

    return pl.pallas_call(
        kernel,
        out_shape=[jax.ShapeDtypeStruct(*shape) for shape in shapes],
        in_specs=[pl.BlockSpec(memory_space=pltpu.HBM)] * len(arrays),
        out_specs=[vmem] * len(shapes),
        scratch_shapes=[pltpu.VMEM(a.shape, a.dtype) for a in (*weights, shift_in, shift_out)]
        + [pltpu.SemaphoreType.DMA((len(arrays),))],
        compiler_params=pltpu.CompilerParams(vmem_limit_bytes=4 << 20),
    )(*[hold(a) for a in arrays])


class Layout:
    def __init__(self, n_row, order, steps, tokens):
        self.n_row, self.order, self.steps, self.tokens = n_row, order, steps, tokens
        self.per = tokens // n_row
        self.group = len(order) * self.per
        self.chunk = self.group * tokens
        self.pitch = tokens + 8
        self.marks = mark_rows(n_row, self.per)
        self.column_marks = seats(n_row) * self.per

    def places(self):
        me = lax.axis_index("row")
        for n, step in enumerate(self.steps):
            for slot, place in enumerate(self.order):
                yield n * self.group + slot * self.per, me ^ (step ^ place)

    def pairs(self, n):
        return [(n, q) for q in range(n + 1)] + [(p, n) for p in range(n)]


def prepare(lay, n, block, gain, proj, gate_weight, proj_bias, gate_bias, outs, scratch):
    z, left, right_t, gate, near = outs
    marks, rough, right, columns, seen = scratch
    tokens, group, per, chunk, pitch = lay.tokens, lay.group, lay.per, lay.chunk, lay.pitch
    width = z.shape[-1]
    places = list(lay.places())
    marks[...] = block[chunk:, :].astype(jnp.float32)
    diagonal = lax.broadcasted_iota(jnp.int32, (tokens, tokens), 0)
    diagonal = diagonal == lax.broadcasted_iota(jnp.int32, (tokens, tokens), 1)
    row = jnp.minimum(marks[lay.column_marks : lay.column_marks + 1, 0:tokens], 1.0)
    column = jnp.sum(jnp.where(diagonal, row, 0.0), axis=1, keepdims=True)
    columns[...] = jnp.broadcast_to(column, (tokens, width))
    for first, at in places:
        seen[first : first + per, :] = columns[pl.ds(at * per, per), :]
    for first, at in places[n * len(lay.order) : (n + 1) * len(lay.order)]:
        near[first - n * group : first - n * group + per, :] = marks[pl.ds(seat(at, lay.n_row) * per, per), :]
    for t in range(group):
        rough[t * pitch : t * pitch + tokens, :] = block[t * tokens : (t + 1) * tokens, :].astype(jnp.float32)
    for first, at in places:
        for t in range(per):
            z[pl.ds(first + t, group, stride=pitch), :] = rough[pl.ds(at * per + t, group, stride=pitch), :]
    values = jnp.concatenate([z[t * pitch : t * pitch + tokens, :] for t in range(group)], axis=0)
    packed, gates = normed_matmul(
        values, gain[0:1, :], (proj[0], gate_weight[0]), (proj_bias[0:1, :], gate_bias[0:1, :])
    )
    left[...] = gated(packed[:, 0 : 2 * width], width)
    value = gated(packed[:, 2 * width :], width)
    for t in range(group):
        right[t * pitch : t * pitch + tokens, :] = value[t * tokens : (t + 1) * tokens, :]
    for k in range(tokens):
        right_t[k * group : (k + 1) * group, :] = right[pl.ds(k, group, stride=pitch), :] * seen[k : k + 1, :]
    gate[...] = jnp.tanh(gates) + 1.0


def block_sums(lay, left, rights):
    tokens, group = lay.tokens, lay.group
    width = left.shape[-1]
    totals = [[jnp.zeros((group, width), jnp.float32)] * group for _ in rights]
    for k in range(tokens):
        rows = [right[k * group : (k + 1) * group, :] for right in rights]
        for i in range(group):
            value = left[i * tokens + k : i * tokens + k + 1, :]
            for q, row in enumerate(rows):
                totals[q][i] = totals[q][i] + value * row
    return totals


def complete(lay, n, lefts, rights, sums):
    size = lay.group * lay.group
    totals = block_sums(lay, lefts[n], rights)
    for p in range(n):
        totals += block_sums(lay, lefts[p], rights[n : n + 1])
    for place, total in enumerate(totals):
        sums[place * size : (place + 1) * size, :] = jnp.concatenate(total, axis=0)


def group_kernel(lay, n, block, *refs):
    lefts, rights, refs = refs[:n], refs[n : 2 * n], refs[2 * n :]
    params, outs, sums, scratch = refs[:5], refs[5:10], refs[10], refs[11:]
    prepare(lay, n, block, *params, outs, scratch)
    complete(lay, n, [*lefts, outs[1]], [*rights, outs[2]], sums)


def group_shapes(lay, n, width):
    count = len(lay.pairs(n)) * lay.group * lay.group
    rows = [lay.group * lay.pitch, lay.chunk, lay.chunk, lay.chunk, lay.group, count]
    return [(r, width) for r in rows]


def scratch_shapes(lay, width):
    rows = [lay.marks] + [lay.group * lay.pitch] * 2 + [lay.tokens] * 2
    return [pltpu.VMEM((r, width), jnp.float32) for r in rows]


def complete_group(lay, n, block, lefts, rights, params):
    width = block.shape[-1]
    vmem = pl.BlockSpec(memory_space=pltpu.VMEM)
    shapes = group_shapes(lay, n, width)
    sums = shapes[-1][0] * lay.tokens * width
    return pl.pallas_call(
        functools.partial(group_kernel, lay, n),
        out_shape=[jax.ShapeDtypeStruct(shape, jnp.float32) for shape in shapes],
        in_specs=[vmem] * (1 + 2 * n + len(params)),
        out_specs=[vmem] * len(shapes),
        scratch_shapes=scratch_shapes(lay, width),
        cost_estimate=pl.CostEstimate(
            flops=10 * lay.chunk * width * width + 2 * sums,
            bytes_accessed=20 * lay.chunk * width,
            transcendentals=3 * lay.chunk * width,
        ),
        compiler_params=pltpu.CompilerParams(vmem_limit_bytes=4 << 20),
    )(block, *lefts, *rights, *params)


def updates_kernel(lay, block, *refs):
    last = len(lay.steps) - 1
    done = [refs[6 * n : 6 * n + 6] for n in range(last)]
    refs = refs[6 * last :]
    gain_in, gain_out, proj, gate_weight, out_weight, proj_bias, gate_bias, out_bias = refs[:8]
    out_even, out_odd = refs[8:10]
    own, scratch = refs[10:16], refs[16:21]
    right1, middle, left1, result1 = refs[21:]
    tokens, per, group, chunk, pitch = lay.tokens, lay.per, lay.group, lay.chunk, lay.pitch
    width = out_even.shape[-1]
    rows = per * tokens
    done = done + [own]

    def run():
        prepare(lay, last, block, gain_in, proj, gate_weight, proj_bias, gate_bias, own[:5], scratch)
        complete(lay, last, [arrays[1] for arrays in done], [arrays[2] for arrays in done], own[5])

        real = jnp.concatenate([arrays[4][...] for arrays in done], axis=0)
        for p in range(last + 1):
            z, _, _, gate, near, _ = done[p]
            products = []
            for i in range(group):
                parts = []
                for q in range(last + 1):
                    n = max(p, q)
                    start = (lay.pairs(n).index((p, q)) * group + i) * group
                    parts.append(done[n][5][start : start + group, :])
                products.append(jnp.concatenate(parts, axis=0) * (real * near[i : i + 1, :]))
            products = jnp.concatenate(products, axis=0)
            (change,) = normed_matmul(products, gain_out[0:1, :], (out_weight[0],), (out_bias[0:1, :],))
            held = jnp.concatenate([z[t * pitch : t * pitch + tokens, :] for t in range(group)], axis=0)
            middle[p * chunk : (p + 1) * chunk, :] = held + gate[...] * change

        for p in range(last + 1):
            at = slice(p * chunk, (p + 1) * chunk)
            (packed,) = normed_matmul(
                middle[at, :], gain_in[1:2, :], (proj[1, :, 2 * width :],), (proj_bias[1:2, 2 * width :],)
            )
            right1[at, :] = gated(packed, width)

        ours = [*range(per, 2 * per), *range(per)]
        columns = jnp.concatenate([middle[pl.ds(r, tokens, stride=tokens), :] for r in ours], axis=0)
        (packed,) = normed_matmul(
            columns, gain_in[1:2, :], (proj[1, :, 0 : 2 * width],), (proj_bias[1:2, 0 : 2 * width],)
        )
        left1[...] = gated(packed, width) * jnp.concatenate([real] * len(ours), axis=0)
        totals = [jnp.zeros((tokens, width), jnp.float32)] * len(ours)
        for k in range(tokens):
            row = right1[k * tokens : (k + 1) * tokens, :]
            for r in range(len(ours)):
                totals[r] = totals[r] + left1[r * tokens + k : r * tokens + k + 1, :] * row
        near = done[0][4]
        product = jnp.concatenate([t * (real * near[r : r + 1, :]) for r, t in zip(ours, totals, strict=True)], axis=0)
        (change,) = normed_matmul(product, gain_out[1:2, :], (out_weight[1],), (out_bias[1:2, :],))
        held = jnp.concatenate([middle[rows : 2 * rows, :], middle[0:rows, :]], axis=0)
        (gates,) = normed_matmul(held, gain_in[1:2, :], (gate_weight[1],), (gate_bias[1:2, :],))
        result = held + (jnp.tanh(gates) + 1.0) * change
        rough = scratch[1]
        for r in range(len(ours)):
            rough[r * pitch : r * pitch + tokens, :] = result[r * tokens : (r + 1) * tokens, :]
        for first, at in lay.places():
            for t in range(per):
                row = rough[pl.ds(first + t, len(ours), stride=pitch), :]
                result1[pl.ds(at * per + t, len(ours), stride=pitch), :] = row
        halves = [result1[r * pitch : r * pitch + tokens, :] for r in range(len(ours))]
        out_even[...] = jnp.concatenate(halves[:per], axis=0).astype(jnp.bfloat16)
        out_odd[...] = jnp.concatenate(halves[per:], axis=0).astype(jnp.bfloat16)

    pl.when(lax.axis_index("row") % 2 == 1)(run)


def updates(lay, blocks, params):
    width = blocks[0].shape[-1]
    rows = lay.per * lay.tokens
    pairs = lay.tokens * lay.tokens
    gain_in, _, proj, gate_weight, _, proj_bias, gate_bias, _ = params
    group_params = (gain_in, proj, gate_weight, proj_bias, gate_bias)
    done = []
    for n, block in enumerate(blocks[:-1]):
        lefts, rights = [arrays[1] for arrays in done], [arrays[2] for arrays in done]
        done.append(complete_group(lay, n, block, lefts, rights, group_params))
    arrays = [array for arrays in done for array in arrays]
    vmem = pl.BlockSpec(memory_space=pltpu.VMEM)
    shapes = group_shapes(lay, len(blocks) - 1, width)
    tail = [(pairs, width), (pairs, width), (2 * rows, width), (2 * lay.per * lay.pitch, width)]
    return pl.pallas_call(
        functools.partial(updates_kernel, lay),
        out_shape=[jax.ShapeDtypeStruct((rows, width), jnp.bfloat16)] * 2,
        in_specs=[vmem] * (1 + len(arrays) + len(params)),
        out_specs=[vmem] * 2,
        scratch_shapes=[pltpu.VMEM(shape, jnp.float32) for shape in shapes]
        + scratch_shapes(lay, width)
        + [pltpu.VMEM(shape, jnp.float32) for shape in tail],
        compiler_params=pltpu.CompilerParams(vmem_limit_bytes=8 << 20),
    )(blocks[-1], *arrays, *params)


def swap(values, step, n_row):
    return lax.ppermute(values, "row", [(i, i ^ step) for i in range(n_row)])


def odd_swap(values, step, n_group, n_row):
    if n_group % 2:
        return swap(values, step, n_row)
    target = [(g, i ^ step) if i % 2 else (g ^ 1, i) for g in range(n_group) for i in range(n_row)]
    pairs = [(source, g * n_row + i) for source, (g, i) in enumerate(target)]
    return lax.ppermute(values, ("groups", "row"), pairs)


def merge(first, second, rows):
    return jnp.concatenate([first[:rows], second[:rows], first[rows:] + second[rows:]], axis=0)


def gathered(n_group, n_row, pair_rep, pair_mask, *params):
    per, tokens, width = pair_rep.shape
    rows = per * tokens
    me = lax.axis_index("row")
    held = pack(n_row, pair_rep, pair_mask)
    held = merge(held, swap(held, 1, n_row), rows)
    order = [0, 1]
    step = n_row // 2
    while step > 4:
        count = len(order)
        held = merge(held, odd_swap(held, step, n_group, n_row), count * rows)
        order = order + [place ^ step for place in order]
        step //= 2
    held, *params = lax.optimization_barrier((held, *load(*params)))
    steps = [0] + list(range(2, 2 * step, 2))
    steps[2:] = reversed(steps[2:])
    blocks = [held] + [odd_swap(held, place, n_group, n_row) for place in steps[1:]]
    even, odd = updates(Layout(n_row, order, steps, tokens), blocks, params)
    out = jnp.where(me % 2 == 1, odd, swap(even, 1, n_row))
    return out.reshape(per, tokens, width)


H = 128


def layer_norm(values, gain, offset, axis):
    mean = jnp.mean(values, axis=axis, keepdims=True)
    centered = values - mean
    variance = jnp.mean(centered * centered, axis=axis, keepdims=True)
    return centered * lax.rsqrt(variance + 1e-05) * gain + offset


def triangle(
    pair_now,
    pair_mask,
    layer_index,
    gain_in,
    shift_in,
    proj_weight,
    gate_weight,
    gain_out,
    shift_out,
    out_weight,
):
    normed = layer_norm(
        pair_now.astype(jnp.float32), gain_in[layer_index], shift_in[layer_index], -1
    ).astype(jnp.bfloat16)
    packed = jnp.einsum(
        "rnc,ch->hrn", normed, proj_weight[layer_index], preferred_element_type=jnp.float32
    )
    masked = pair_mask.astype(jnp.float32)[None, :, :]
    left = (masked * jax.nn.sigmoid(packed[0:H]) * packed[H : 2 * H]).astype(jnp.bfloat16)
    right = (masked * jax.nn.sigmoid(packed[2 * H : 3 * H]) * packed[3 * H :]).astype(jnp.bfloat16)
    gating = jax.nn.sigmoid(
        jnp.einsum(
            "rnc,cd->rnd", normed, gate_weight[layer_index], preferred_element_type=jnp.float32
        )
    )
    lifted_left, lifted_right = (
        lax.all_to_all(left, "row", split_axis=0, concat_axis=1, tiled=True),
        lax.all_to_all(right, "row", split_axis=0, concat_axis=1, tiled=True),
    )
    if layer_index == 0:
        product = jnp.einsum(
            "hik,hjk->hij", lifted_left, lifted_right, preferred_element_type=jnp.float32
        )
    else:
        product = jnp.einsum(
            "hki,hkj->hij", lifted_left, lifted_right, preferred_element_type=jnp.float32
        )
    product = product.astype(jnp.bfloat16)
    out_gain = gain_out[layer_index][:, None, None]
    out_shift = shift_out[layer_index][:, None, None]
    out_proj = out_weight[layer_index]
    returned = lax.all_to_all(product, "row", split_axis=1, concat_axis=0, tiled=True)
    scaled = layer_norm(returned.astype(jnp.float32), out_gain, out_shift, 0).astype(jnp.bfloat16)
    update = jnp.einsum("hrn,hc->rnc", scaled, out_proj, preferred_element_type=jnp.float32)
    return (pair_now.astype(jnp.float32) + gating * update).astype(jnp.bfloat16)


def exchanged(
    pair_rep,
    pair_mask,
    gain_in,
    shift_in,
    proj_weight,
    gate_weight,
    gain_out,
    shift_out,
    out_weight,
):
    current = pair_rep
    for layer_index in range(2):
        current = triangle(
            current,
            pair_mask,
            layer_index,
            gain_in,
            shift_in,
            proj_weight,
            gate_weight,
            gain_out,
            shift_out,
            out_weight,
        )
    return current


def solution(mesh):
    n_group, n_row = mesh.shape["groups"], mesh.shape["row"]

    def shards(pair_rep, *rest):
        per, tokens, _ = pair_rep.shape
        small = pair_rep.size * n_row * 2 <= GATHER_LIMIT
        fits = n_row & (n_row - 1) == 0 and n_row > 3 and tokens % 32 == 0 and tokens <= pair_rep.shape[2]
        if small and fits:
            return gathered(n_group, n_row, pair_rep, *rest)
        return exchanged(pair_rep, *rest)

    in_specs = (
        P(("groups", "row"), None, None),
        P(("groups", "row"), None),
        P(),
        P(),
        P(),
        P(),
        P(),
        P(),
        P(),
    )
    out_specs = P(("groups", "row"), None, None)
    return jax.shard_map(shards, mesh=mesh, in_specs=in_specs, out_specs=out_specs, check_vma=False)
```

```python
import functools

import jax
import jax.numpy as jnp
from jax import lax
from jax.experimental import pallas as pl
from jax.experimental.pallas import tpu as pltpu
from jax.sharding import PartitionSpec as P

EPS = 1e-05
MARK_ROWS = 16
GATHER_LIMIT = 4 << 20


def matmul(left, right):
    return jnp.dot(left, right, preferred_element_type=jnp.float32)


def normed_matmul(values, gain, weights, biases):
    centered = values - jnp.mean(values, axis=-1, keepdims=True)
    scale = lax.rsqrt(jnp.mean(centered * centered, axis=-1, keepdims=True) + EPS)
    factor = (centered * gain).astype(jnp.bfloat16)
    return [matmul(factor, weight) * scale + bias for weight, bias in zip(weights, biases, strict=True)]


def gated(packed, width):
    return (jnp.tanh(packed[:, :width]) + 1.0) * packed[:, width:]


def seat(device, n_row):
    place = device % 2
    step, weight = n_row // 2, 2
    while step > 4:
        place = place + weight * (device // step % 2)
        step, weight = step // 2, 2 * weight
    return place


def seats(n_row):
    return max(2, n_row // 4)


def hold(values):
    return pltpu.with_memory_space_constraint(values, pltpu.HBM)


def mark_rows(n_row, per):
    return -(-(seats(n_row) * per + 1) // MARK_ROWS) * MARK_ROWS


def join_kernel(n_row, own, mask, other, other_mask, out_ref, marks):
    rows = own.shape[0]
    per, tokens = mask.shape
    width = out_ref.shape[1]
    me = lax.axis_index("row")
    out_ref[0:rows, :] = own[...]
    out_ref[rows : 2 * rows, :] = other[...]
    marks[...] = jnp.zeros_like(marks)
    last = seats(n_row) * per
    seen = []
    for device, ref in ((me, mask), (me ^ 1, other_mask)):
        mine = ref[...].astype(jnp.float32)
        first = seat(device, n_row) * per
        marks[pl.ds(first, per), :] = jnp.broadcast_to(jnp.max(mine, axis=1, keepdims=True), (per, width))
        seen.append(jnp.max(mine, axis=0, keepdims=True))
    marks[last : last + 1, 0:tokens] = jnp.maximum(*seen)
    out_ref[2 * rows :, :] = marks[...].astype(jnp.bfloat16)


def join(n_row, own, mask, other, other_mask):
    rows, width = own.shape
    extra = mark_rows(n_row, mask.shape[0])
    vmem = pl.BlockSpec(memory_space=pltpu.VMEM)
    return pl.pallas_call(
        functools.partial(join_kernel, n_row),
        out_shape=jax.ShapeDtypeStruct((2 * rows + extra, width), jnp.bfloat16),
        in_specs=[vmem] * 4,
        out_specs=vmem,
        scratch_shapes=[pltpu.VMEM((extra, width), jnp.float32)],
        compiler_params=pltpu.CompilerParams(vmem_limit_bytes=1 << 20),
    )(own, mask, other, other_mask)


def fetch_kernel(count, *refs):
    sources, targets, sems = refs[:count], refs[count : 2 * count], refs[2 * count]
    copies = [pltpu.make_async_copy(s, t, sems.at[n]) for n, (s, t) in enumerate(zip(sources, targets, strict=True))]
    for copy in copies:
        copy.start()
    for copy in copies:
        copy.wait()


def fetch(*arrays):
    count = len(arrays)
    return pl.pallas_call(
        functools.partial(fetch_kernel, count),
        out_shape=[jax.ShapeDtypeStruct(a.shape, a.dtype) for a in arrays],
        in_specs=[pl.BlockSpec(memory_space=pltpu.HBM)] * count,
        out_specs=[pl.BlockSpec(memory_space=pltpu.VMEM)] * count,
        scratch_shapes=[pltpu.SemaphoreType.DMA((count,))],
        compiler_params=pltpu.CompilerParams(vmem_limit_bytes=1 << 20),
    )(*[hold(a) for a in arrays])


def load_kernel(sources, targets):
    (gain_in, shift_in, proj, gate, gain_out, shift_out, out), sems = sources[:7], sources[-1]
    held = sources[7:-1]
    copies = [
        pltpu.make_async_copy(source, target, sems.at[n])
        for n, (source, target) in enumerate(
            zip((proj, gate, out, shift_in, shift_out, gain_in, gain_out), (*held, targets[0], targets[1]), strict=True)
        )
    ]
    for copy in copies:
        copy.start()
    for copy in copies:
        copy.wait()
    proj, gate, out, shift_in, shift_out = held
    _, _, proj_half, gate_half, out_half, proj_bias, gate_bias, out_bias = targets
    half = jnp.array(0.5, jnp.bfloat16)
    for weight, halved, bias, shift in (
        (proj, proj_half, proj_bias, shift_in),
        (gate, gate_half, gate_bias, shift_in),
        (out, out_half, out_bias, shift_out),
    ):
        halved[...] = weight[...] * half
        exact = shift[...]
        high = exact.astype(jnp.bfloat16)
        low = (exact - high.astype(jnp.float32)).astype(jnp.bfloat16)
        rows = jnp.concatenate([high, low] + [jnp.zeros_like(high)] * 6, axis=0)
        for u in range(2):
            both = matmul(rows, weight[u])
            bias[u : u + 1, :] = 0.5 * (both[u : u + 1, :] + both[u + 2 : u + 3, :])


def load(gain_in, shift_in, proj, gate, gain_out, shift_out, out):
    arrays = (gain_in, shift_in, proj, gate, gain_out, shift_out, out)
    weights = (proj, gate, out)
    shapes = [(a.shape, a.dtype) for a in (gain_in, gain_out, *weights)]
    shapes += [((a.shape[0], a.shape[2]), jnp.float32) for a in weights]
    vmem = pl.BlockSpec(memory_space=pltpu.VMEM)

    def kernel(*refs):
        load_kernel((*refs[:7], *refs[7 + len(shapes) :]), refs[7 : 7 + len(shapes)])

    return pl.pallas_call(
        kernel,
        out_shape=[jax.ShapeDtypeStruct(*shape) for shape in shapes],
        in_specs=[pl.BlockSpec(memory_space=pltpu.HBM)] * len(arrays),
        out_specs=[vmem] * len(shapes),
        scratch_shapes=[pltpu.VMEM(a.shape, a.dtype) for a in (*weights, shift_in, shift_out)]
        + [pltpu.SemaphoreType.DMA((len(arrays),))],
        compiler_params=pltpu.CompilerParams(vmem_limit_bytes=4 << 20),
    )(*[hold(a) for a in arrays])


class Layout:
    def __init__(self, n_row, order, steps, tokens):
        self.n_row, self.order, self.steps, self.tokens = n_row, order, steps, tokens
        self.per = tokens // n_row
        self.group = len(order) * self.per
        self.chunk = self.group * tokens
        self.pitch = tokens + 8
        self.marks = mark_rows(n_row, self.per)
        self.column_marks = seats(n_row) * self.per

    def places(self):
        me = lax.axis_index("row")
        for n, step in enumerate(self.steps):
            for slot, place in enumerate(self.order):
                yield n * self.group + slot * self.per, me ^ (step ^ place)

    def pairs(self, n):
        return [(n, q) for q in range(n + 1)] + [(p, n) for p in range(n)]


def prepare(lay, n, block, gain, proj, gate_weight, proj_bias, gate_bias, outs, scratch):
    z, left, right_t, gate, near = outs
    marks, rough, right, columns, seen = scratch
    tokens, group, per, chunk, pitch = lay.tokens, lay.group, lay.per, lay.chunk, lay.pitch
    width = z.shape[-1]
    places = list(lay.places())
    marks[...] = block[chunk:, :].astype(jnp.float32)
    diagonal = lax.broadcasted_iota(jnp.int32, (tokens, tokens), 0)
    diagonal = diagonal == lax.broadcasted_iota(jnp.int32, (tokens, tokens), 1)
    row = jnp.minimum(marks[lay.column_marks : lay.column_marks + 1, 0:tokens], 1.0)
    column = jnp.sum(jnp.where(diagonal, row, 0.0), axis=1, keepdims=True)
    columns[...] = jnp.broadcast_to(column, (tokens, width))
    for first, at in places:
        seen[first : first + per, :] = columns[pl.ds(at * per, per), :]
    for first, at in places[n * len(lay.order) : (n + 1) * len(lay.order)]:
        near[first - n * group : first - n * group + per, :] = marks[pl.ds(seat(at, lay.n_row) * per, per), :]
    for t in range(group):
        rough[t * pitch : t * pitch + tokens, :] = block[t * tokens : (t + 1) * tokens, :].astype(jnp.float32)
    for first, at in places:
        for t in range(per):
            z[pl.ds(first + t, group, stride=pitch), :] = rough[pl.ds(at * per + t, group, stride=pitch), :]
    values = jnp.concatenate([z[t * pitch : t * pitch + tokens, :] for t in range(group)], axis=0)
    packed, gates = normed_matmul(
        values, gain[0:1, :], (proj[0], gate_weight[0]), (proj_bias[0:1, :], gate_bias[0:1, :])
    )
    left[...] = gated(packed[:, 0 : 2 * width], width)
    value = gated(packed[:, 2 * width :], width)
    for t in range(group):
        right[t * pitch : t * pitch + tokens, :] = value[t * tokens : (t + 1) * tokens, :]
    for k in range(tokens):
        right_t[k * group : (k + 1) * group, :] = right[pl.ds(k, group, stride=pitch), :] * seen[k : k + 1, :]
    gate[...] = jnp.tanh(gates) + 1.0


def block_sums(lay, left, rights):
    tokens, group = lay.tokens, lay.group
    width = left.shape[-1]
    totals = [[jnp.zeros((group, width), jnp.float32)] * group for _ in rights]
    for k in range(tokens):
        rows = [right[k * group : (k + 1) * group, :] for right in rights]
        for i in range(group):
            value = left[i * tokens + k : i * tokens + k + 1, :]
            for q, row in enumerate(rows):
                totals[q][i] = totals[q][i] + value * row
    return totals


def complete(lay, n, lefts, rights, sums):
    size = lay.group * lay.group
    totals = block_sums(lay, lefts[n], rights)
    for p in range(n):
        totals += block_sums(lay, lefts[p], rights[n : n + 1])
    for place, total in enumerate(totals):
        sums[place * size : (place + 1) * size, :] = jnp.concatenate(total, axis=0)


def group_kernel(lay, n, block, *refs):
    lefts, rights, refs = refs[:n], refs[n : 2 * n], refs[2 * n :]
    params, outs, sums, scratch = refs[:5], refs[5:10], refs[10], refs[11:]
    prepare(lay, n, block, *params, outs, scratch)
    complete(lay, n, [*lefts, outs[1]], [*rights, outs[2]], sums)


def group_shapes(lay, n, width):
    count = len(lay.pairs(n)) * lay.group * lay.group
    rows = [lay.group * lay.pitch, lay.chunk, lay.chunk, lay.chunk, lay.group, count]
    return [(r, width) for r in rows]


def scratch_shapes(lay, width):
    rows = [lay.marks] + [lay.group * lay.pitch] * 2 + [lay.tokens] * 2
    return [pltpu.VMEM((r, width), jnp.float32) for r in rows]


def complete_group(lay, n, block, lefts, rights, params):
    width = block.shape[-1]
    vmem = pl.BlockSpec(memory_space=pltpu.VMEM)
    shapes = group_shapes(lay, n, width)
    sums = shapes[-1][0] * lay.tokens * width
    return pl.pallas_call(
        functools.partial(group_kernel, lay, n),
        out_shape=[jax.ShapeDtypeStruct(shape, jnp.float32) for shape in shapes],
        in_specs=[vmem] * (1 + 2 * n + len(params)),
        out_specs=[vmem] * len(shapes),
        scratch_shapes=scratch_shapes(lay, width),
        cost_estimate=pl.CostEstimate(
            flops=10 * lay.chunk * width * width + 2 * sums,
            bytes_accessed=20 * lay.chunk * width,
            transcendentals=3 * lay.chunk * width,
        ),
        compiler_params=pltpu.CompilerParams(vmem_limit_bytes=4 << 20),
    )(block, *lefts, *rights, *params)


def updates_kernel(lay, block, *refs):
    last = len(lay.steps) - 1
    done = [refs[6 * n : 6 * n + 6] for n in range(last)]
    refs = refs[6 * last :]
    gain_in, gain_out, proj, gate_weight, out_weight, proj_bias, gate_bias, out_bias = refs[:8]
    out_even, out_odd = refs[8:10]
    own, scratch = refs[10:16], refs[16:21]
    right1, middle, left1, result1 = refs[21:]
    tokens, per, group, chunk, pitch = lay.tokens, lay.per, lay.group, lay.chunk, lay.pitch
    width = out_even.shape[-1]
    rows = per * tokens
    done = done + [own]

    def run():
        prepare(lay, last, block, gain_in, proj, gate_weight, proj_bias, gate_bias, own[:5], scratch)
        complete(lay, last, [arrays[1] for arrays in done], [arrays[2] for arrays in done], own[5])

        real = jnp.concatenate([arrays[4][...] for arrays in done], axis=0)
        for p in range(last + 1):
            z, _, _, gate, near, _ = done[p]
            products = []
            for i in range(group):
                parts = []
                for q in range(last + 1):
                    n = max(p, q)
                    start = (lay.pairs(n).index((p, q)) * group + i) * group
                    parts.append(done[n][5][start : start + group, :])
                products.append(jnp.concatenate(parts, axis=0) * (real * near[i : i + 1, :]))
            products = jnp.concatenate(products, axis=0)
            (change,) = normed_matmul(products, gain_out[0:1, :], (out_weight[0],), (out_bias[0:1, :],))
            held = jnp.concatenate([z[t * pitch : t * pitch + tokens, :] for t in range(group)], axis=0)
            middle[p * chunk : (p + 1) * chunk, :] = held + gate[...] * change

        for p in range(last + 1):
            at = slice(p * chunk, (p + 1) * chunk)
            (packed,) = normed_matmul(
                middle[at, :], gain_in[1:2, :], (proj[1, :, 2 * width :],), (proj_bias[1:2, 2 * width :],)
            )
            right1[at, :] = gated(packed, width)

        ours = [*range(per, 2 * per), *range(per)]
        columns = jnp.concatenate([middle[pl.ds(r, tokens, stride=tokens), :] for r in ours], axis=0)
        (packed,) = normed_matmul(
            columns, gain_in[1:2, :], (proj[1, :, 0 : 2 * width],), (proj_bias[1:2, 0 : 2 * width],)
        )
        left1[...] = gated(packed, width) * jnp.concatenate([real] * len(ours), axis=0)
        totals = [jnp.zeros((tokens, width), jnp.float32)] * len(ours)
        for k in range(tokens):
            row = right1[k * tokens : (k + 1) * tokens, :]
            for r in range(len(ours)):
                totals[r] = totals[r] + left1[r * tokens + k : r * tokens + k + 1, :] * row
        near = done[0][4]
        product = jnp.concatenate([t * (real * near[r : r + 1, :]) for r, t in zip(ours, totals, strict=True)], axis=0)
        (change,) = normed_matmul(product, gain_out[1:2, :], (out_weight[1],), (out_bias[1:2, :],))
        held = jnp.concatenate([middle[rows : 2 * rows, :], middle[0:rows, :]], axis=0)
        (gates,) = normed_matmul(held, gain_in[1:2, :], (gate_weight[1],), (gate_bias[1:2, :],))
        result = held + (jnp.tanh(gates) + 1.0) * change
        rough = scratch[1]
        for r in range(len(ours)):
            rough[r * pitch : r * pitch + tokens, :] = result[r * tokens : (r + 1) * tokens, :]
        for first, at in lay.places():
            for t in range(per):
                row = rough[pl.ds(first + t, len(ours), stride=pitch), :]
                result1[pl.ds(at * per + t, len(ours), stride=pitch), :] = row
        halves = [result1[r * pitch : r * pitch + tokens, :] for r in range(len(ours))]
        out_even[...] = jnp.concatenate(halves[:per], axis=0).astype(jnp.bfloat16)
        out_odd[...] = jnp.concatenate(halves[per:], axis=0).astype(jnp.bfloat16)

    pl.when(lax.axis_index("row") % 2 == 1)(run)


def updates(lay, blocks, params):
    width = blocks[0].shape[-1]
    rows = lay.per * lay.tokens
    pairs = lay.tokens * lay.tokens
    gain_in, _, proj, gate_weight, _, proj_bias, gate_bias, _ = params
    group_params = (gain_in, proj, gate_weight, proj_bias, gate_bias)
    done = []
    for n, block in enumerate(blocks[:-1]):
        lefts, rights = [arrays[1] for arrays in done], [arrays[2] for arrays in done]
        done.append(complete_group(lay, n, block, lefts, rights, group_params))
    arrays = [array for arrays in done for array in arrays]
    vmem = pl.BlockSpec(memory_space=pltpu.VMEM)
    shapes = group_shapes(lay, len(blocks) - 1, width)
    tail = [(pairs, width), (pairs, width), (2 * rows, width), (2 * lay.per * lay.pitch, width)]
    return pl.pallas_call(
        functools.partial(updates_kernel, lay),
        out_shape=[jax.ShapeDtypeStruct((rows, width), jnp.bfloat16)] * 2,
        in_specs=[vmem] * (1 + len(arrays) + len(params)),
        out_specs=[vmem] * 2,
        scratch_shapes=[pltpu.VMEM(shape, jnp.float32) for shape in shapes]
        + scratch_shapes(lay, width)
        + [pltpu.VMEM(shape, jnp.float32) for shape in tail],
        compiler_params=pltpu.CompilerParams(vmem_limit_bytes=8 << 20),
    )(blocks[-1], *arrays, *params)


def swap(values, step, n_row):
    return lax.ppermute(values, "row", [(i, i ^ step) for i in range(n_row)])


def odd_swap(values, step, n_group, n_row):
    if n_group % 2:
        return swap(values, step, n_row)
    target = [(g, i ^ step) if i % 2 else (g ^ 1, i) for g in range(n_group) for i in range(n_row)]
    pairs = [(source, g * n_row + i) for source, (g, i) in enumerate(target)]
    return lax.ppermute(values, ("groups", "row"), pairs)


def merge(first, second, rows):
    return jnp.concatenate([first[:rows], second[:rows], first[rows:] + second[rows:]], axis=0)


def gathered(n_group, n_row, pair_rep, pair_mask, *params):
    per, tokens, width = pair_rep.shape
    rows = per * tokens
    me = lax.axis_index("row")
    own = pair_rep.reshape(rows, width)
    other = swap(own, 1, n_row)
    other_mask = swap(pair_mask, 1, n_row)
    own, mask = fetch(own, pair_mask)
    other, other_mask, own, mask = lax.optimization_barrier((other, other_mask, own, mask))
    held = join(n_row, own, mask, other, other_mask)
    order = [0, 1]
    step = n_row // 2
    while step > 4:
        count = len(order)
        held = merge(held, odd_swap(held, step, n_group, n_row), count * rows)
        order = order + [place ^ step for place in order]
        step //= 2
    held, *params = lax.optimization_barrier((held, *load(*params)))
    steps = [0] + list(range(2, 2 * step, 2))
    steps[2:] = reversed(steps[2:])
    blocks = [held] + [odd_swap(held, place, n_group, n_row) for place in steps[1:]]
    even, odd = updates(Layout(n_row, order, steps, tokens), blocks, params)
    out = jnp.where(me % 2 == 1, odd, swap(even, 1, n_row))
    return out.reshape(per, tokens, width)


H = 128


def layer_norm(values, gain, offset, axis):
    mean = jnp.mean(values, axis=axis, keepdims=True)
    centered = values - mean
    variance = jnp.mean(centered * centered, axis=axis, keepdims=True)
    return centered * lax.rsqrt(variance + 1e-05) * gain + offset


def triangle(
    pair_now,
    pair_mask,
    layer_index,
    gain_in,
    shift_in,
    proj_weight,
    gate_weight,
    gain_out,
    shift_out,
    out_weight,
):
    normed = layer_norm(
        pair_now.astype(jnp.float32), gain_in[layer_index], shift_in[layer_index], -1
    ).astype(jnp.bfloat16)
    packed = jnp.einsum(
        "rnc,ch->hrn", normed, proj_weight[layer_index], preferred_element_type=jnp.float32
    )
    masked = pair_mask.astype(jnp.float32)[None, :, :]
    left = (masked * jax.nn.sigmoid(packed[0:H]) * packed[H : 2 * H]).astype(jnp.bfloat16)
    right = (masked * jax.nn.sigmoid(packed[2 * H : 3 * H]) * packed[3 * H :]).astype(jnp.bfloat16)
    gating = jax.nn.sigmoid(
        jnp.einsum(
            "rnc,cd->rnd", normed, gate_weight[layer_index], preferred_element_type=jnp.float32
        )
    )
    lifted_left, lifted_right = (
        lax.all_to_all(left, "row", split_axis=0, concat_axis=1, tiled=True),
        lax.all_to_all(right, "row", split_axis=0, concat_axis=1, tiled=True),
    )
    if layer_index == 0:
        product = jnp.einsum(
            "hik,hjk->hij", lifted_left, lifted_right, preferred_element_type=jnp.float32
        )
    else:
        product = jnp.einsum(
            "hki,hkj->hij", lifted_left, lifted_right, preferred_element_type=jnp.float32
        )
    product = product.astype(jnp.bfloat16)
    out_gain = gain_out[layer_index][:, None, None]
    out_shift = shift_out[layer_index][:, None, None]
    out_proj = out_weight[layer_index]
    returned = lax.all_to_all(product, "row", split_axis=1, concat_axis=0, tiled=True)
    scaled = layer_norm(returned.astype(jnp.float32), out_gain, out_shift, 0).astype(jnp.bfloat16)
    update = jnp.einsum("hrn,hc->rnc", scaled, out_proj, preferred_element_type=jnp.float32)
    return (pair_now.astype(jnp.float32) + gating * update).astype(jnp.bfloat16)


def exchanged(
    pair_rep,
    pair_mask,
    gain_in,
    shift_in,
    proj_weight,
    gate_weight,
    gain_out,
    shift_out,
    out_weight,
):
    current = pair_rep
    for layer_index in range(2):
        current = triangle(
            current,
            pair_mask,
            layer_index,
            gain_in,
            shift_in,
            proj_weight,
            gate_weight,
            gain_out,
            shift_out,
            out_weight,
        )
    return current


def solution(mesh):
    n_group, n_row = mesh.shape["groups"], mesh.shape["row"]

    def shards(pair_rep, *rest):
        per, tokens, _ = pair_rep.shape
        small = pair_rep.size * n_row * 2 <= GATHER_LIMIT
        fits = n_row & (n_row - 1) == 0 and n_row > 3 and tokens % 32 == 0 and tokens <= pair_rep.shape[2]
        if small and fits:
            return gathered(n_group, n_row, pair_rep, *rest)
        return exchanged(pair_rep, *rest)

    in_specs = (
        P(("groups", "row"), None, None),
        P(("groups", "row"), None),
        P(),
        P(),
        P(),
        P(),
        P(),
        P(),
        P(),
    )
    out_specs = P(("groups", "row"), None, None)
    return jax.shard_map(shards, mesh=mesh, in_specs=in_specs, out_specs=out_specs, check_vma=False)
```

```python
import functools

import jax
import jax.numpy as jnp
from jax import lax
from jax.experimental import pallas as pl
from jax.experimental.pallas import tpu as pltpu
from jax.sharding import PartitionSpec as P

EPS = 1e-05
MARK_ROWS = 16
GATHER_LIMIT = 4 << 20


def matmul(left, right):
    return jnp.dot(left, right, preferred_element_type=jnp.float32)


def normed_matmul(values, gain, weights, biases):
    centered = values - jnp.mean(values, axis=-1, keepdims=True)
    scale = lax.rsqrt(jnp.mean(centered * centered, axis=-1, keepdims=True) + EPS)
    factor = (centered * gain).astype(jnp.bfloat16)
    return [matmul(factor, weight) * scale + bias for weight, bias in zip(weights, biases, strict=True)]


def gated(packed, width):
    return (jnp.tanh(packed[:, :width]) + 1.0) * packed[:, width:]


def seat(device, n_row):
    place = device % 2
    step, weight = n_row // 2, 2
    while step > 4:
        place = place + weight * (device // step % 2)
        step, weight = step // 2, 2 * weight
    return place


def seats(n_row):
    return max(2, n_row // 4)


def hold(values):
    return pltpu.with_memory_space_constraint(values, pltpu.HBM)


def mark_rows(n_row, per):
    return -(-(seats(n_row) * per + 1) // MARK_ROWS) * MARK_ROWS


def join_kernel(n_row, own, mask, other, other_mask, out_ref, marks):
    rows = own.shape[0]
    per, tokens = mask.shape
    width = out_ref.shape[1]
    me = lax.axis_index("row")
    out_ref[0:rows, :] = own[...]
    out_ref[rows : 2 * rows, :] = other[...]
    marks[...] = jnp.zeros_like(marks)
    last = seats(n_row) * per
    seen = []
    for device, ref in ((me, mask), (me ^ 1, other_mask)):
        mine = ref[...].astype(jnp.float32)
        first = seat(device, n_row) * per
        marks[pl.ds(first, per), :] = jnp.broadcast_to(jnp.max(mine, axis=1, keepdims=True), (per, width))
        seen.append(jnp.max(mine, axis=0, keepdims=True))
    marks[last : last + 1, 0:tokens] = jnp.maximum(*seen)
    out_ref[2 * rows :, :] = marks[...].astype(jnp.bfloat16)


def join(n_row, own, mask, other, other_mask):
    rows, width = own.shape
    extra = mark_rows(n_row, mask.shape[0])
    vmem = pl.BlockSpec(memory_space=pltpu.VMEM)
    return pl.pallas_call(
        functools.partial(join_kernel, n_row),
        out_shape=jax.ShapeDtypeStruct((2 * rows + extra, width), jnp.bfloat16),
        in_specs=[vmem] * 4,
        out_specs=vmem,
        scratch_shapes=[pltpu.VMEM((extra, width), jnp.float32)],
        compiler_params=pltpu.CompilerParams(vmem_limit_bytes=1 << 20),
    )(own, mask, other, other_mask)


def fetch_kernel(count, *refs):
    sources, targets, sems = refs[:count], refs[count : 2 * count], refs[2 * count]
    copies = [pltpu.make_async_copy(s, t, sems.at[n]) for n, (s, t) in enumerate(zip(sources, targets, strict=True))]
    for copy in copies:
        copy.start()
    for copy in copies:
        copy.wait()


def fetch(*arrays):
    count = len(arrays)
    return pl.pallas_call(
        functools.partial(fetch_kernel, count),
        out_shape=[jax.ShapeDtypeStruct(a.shape, a.dtype) for a in arrays],
        in_specs=[pl.BlockSpec(memory_space=pltpu.HBM)] * count,
        out_specs=[pl.BlockSpec(memory_space=pltpu.VMEM)] * count,
        scratch_shapes=[pltpu.SemaphoreType.DMA((count,))],
        compiler_params=pltpu.CompilerParams(vmem_limit_bytes=1 << 20),
    )(*[hold(a) for a in arrays])


def load_kernel(sources, targets):
    (gain_in, shift_in, proj, gate, gain_out, shift_out, out), sems = sources[:7], sources[-1]
    held = sources[7:-1]
    copies = [
        pltpu.make_async_copy(source, target, sems.at[n])
        for n, (source, target) in enumerate(
            zip((proj, gate, out, shift_in, shift_out, gain_in, gain_out), (*held, targets[0], targets[1]), strict=True)
        )
    ]
    for copy in copies:
        copy.start()
    for copy in copies:
        copy.wait()
    proj, gate, out, shift_in, shift_out = held
    _, _, proj_half, gate_half, out_half, proj_bias, gate_bias, out_bias = targets
    half = jnp.array(0.5, jnp.bfloat16)
    for weight, halved, bias, shift in (
        (proj, proj_half, proj_bias, shift_in),
        (gate, gate_half, gate_bias, shift_in),
        (out, out_half, out_bias, shift_out),
    ):
        halved[...] = weight[...] * half
        exact = shift[...]
        high = exact.astype(jnp.bfloat16)
        low = (exact - high.astype(jnp.float32)).astype(jnp.bfloat16)
        rows = jnp.concatenate([high, low] + [jnp.zeros_like(high)] * 6, axis=0)
        for u in range(2):
            both = matmul(rows, weight[u])
            bias[u : u + 1, :] = 0.5 * (both[u : u + 1, :] + both[u + 2 : u + 3, :])


def load(gain_in, shift_in, proj, gate, gain_out, shift_out, out):
    arrays = (gain_in, shift_in, proj, gate, gain_out, shift_out, out)
    weights = (proj, gate, out)
    shapes = [(a.shape, a.dtype) for a in (gain_in, gain_out, *weights)]
    shapes += [((a.shape[0], a.shape[2]), jnp.float32) for a in weights]
    vmem = pl.BlockSpec(memory_space=pltpu.VMEM)

    def kernel(*refs):
        load_kernel((*refs[:7], *refs[7 + len(shapes) :]), refs[7 : 7 + len(shapes)])

    return pl.pallas_call(
        kernel,
        out_shape=[jax.ShapeDtypeStruct(*shape) for shape in shapes],
        in_specs=[pl.BlockSpec(memory_space=pltpu.HBM)] * len(arrays),
        out_specs=[vmem] * len(shapes),
        scratch_shapes=[pltpu.VMEM(a.shape, a.dtype) for a in (*weights, shift_in, shift_out)]
        + [pltpu.SemaphoreType.DMA((len(arrays),))],
        compiler_params=pltpu.CompilerParams(vmem_limit_bytes=4 << 20),
    )(*[hold(a) for a in arrays])


class Layout:
    def __init__(self, n_row, order, steps, tokens):
        self.n_row, self.order, self.steps, self.tokens = n_row, order, steps, tokens
        self.per = tokens // n_row
        self.group = len(order) * self.per
        self.chunk = self.group * tokens
        self.pitch = tokens + 8
        self.marks = mark_rows(n_row, self.per)
        self.column_marks = seats(n_row) * self.per

    def places(self):
        me = lax.axis_index("row")
        for n, step in enumerate(self.steps):
            for slot, place in enumerate(self.order):
                yield n * self.group + slot * self.per, me ^ (step ^ place)

    def pairs(self, n):
        return [(n, q) for q in range(n + 1)] + [(p, n) for p in range(n)]


def prepare(lay, n, block, gain, proj, gate_weight, proj_bias, gate_bias, outs, scratch):
    z, left, right_t, gate, near = outs
    marks, rough, right, columns, seen = scratch
    tokens, group, per, chunk, pitch = lay.tokens, lay.group, lay.per, lay.chunk, lay.pitch
    width = z.shape[-1]
    places = list(lay.places())
    marks[...] = block[chunk:, :].astype(jnp.float32)
    diagonal = lax.broadcasted_iota(jnp.int32, (tokens, tokens), 0)
    diagonal = diagonal == lax.broadcasted_iota(jnp.int32, (tokens, tokens), 1)
    row = jnp.minimum(marks[lay.column_marks : lay.column_marks + 1, 0:tokens], 1.0)
    column = jnp.sum(jnp.where(diagonal, row, 0.0), axis=1, keepdims=True)
    columns[...] = jnp.broadcast_to(column, (tokens, width))
    for first, at in places:
        seen[first : first + per, :] = columns[pl.ds(at * per, per), :]
    for first, at in places[n * len(lay.order) : (n + 1) * len(lay.order)]:
        near[first - n * group : first - n * group + per, :] = marks[pl.ds(seat(at, lay.n_row) * per, per), :]
    for t in range(group):
        rough[t * pitch : t * pitch + tokens, :] = block[t * tokens : (t + 1) * tokens, :].astype(jnp.float32)
    for first, at in places:
        for t in range(per):
            z[pl.ds(first + t, group, stride=pitch), :] = rough[pl.ds(at * per + t, group, stride=pitch), :]
    values = jnp.concatenate([z[t * pitch : t * pitch + tokens, :] for t in range(group)], axis=0)
    packed, gates = normed_matmul(
        values, gain[0:1, :], (proj[0], gate_weight[0]), (proj_bias[0:1, :], gate_bias[0:1, :])
    )
    left[...] = gated(packed[:, 0 : 2 * width], width)
    value = gated(packed[:, 2 * width :], width)
    for t in range(group):
        right[t * pitch : t * pitch + tokens, :] = value[t * tokens : (t + 1) * tokens, :]
    for k in range(tokens):
        right_t[k * group : (k + 1) * group, :] = right[pl.ds(k, group, stride=pitch), :] * seen[k : k + 1, :]
    gate[...] = jnp.tanh(gates) + 1.0


def block_sums(lay, left, rights):
    tokens, group = lay.tokens, lay.group
    width = left.shape[-1]
    totals = [[jnp.zeros((group, width), jnp.float32)] * group for _ in rights]
    for k in range(tokens):
        rows = [right[k * group : (k + 1) * group, :] for right in rights]
        for i in range(group):
            value = left[i * tokens + k : i * tokens + k + 1, :]
            for q, row in enumerate(rows):
                totals[q][i] = totals[q][i] + value * row
    return totals


def complete(lay, n, lefts, rights, sums):
    size = lay.group * lay.group
    totals = block_sums(lay, lefts[n], rights)
    for p in range(n):
        totals += block_sums(lay, lefts[p], rights[n : n + 1])
    for place, total in enumerate(totals):
        sums[place * size : (place + 1) * size, :] = jnp.concatenate(total, axis=0)


def group_kernel(lay, n, block, *refs):
    lefts, rights, refs = refs[:n], refs[n : 2 * n], refs[2 * n :]
    params, outs, sums, scratch = refs[:5], refs[5:10], refs[10], refs[11:]
    prepare(lay, n, block, *params, outs, scratch)
    complete(lay, n, [*lefts, outs[1]], [*rights, outs[2]], sums)


def group_shapes(lay, n, width):
    count = len(lay.pairs(n)) * lay.group * lay.group
    rows = [(lay.group + 1) * lay.pitch, lay.chunk, lay.chunk, lay.chunk, lay.group, count]
    return [(r, width) for r in rows]


def scratch_shapes(lay, width):
    rows = [lay.marks] + [(lay.group + 1) * lay.pitch] * 2 + [lay.tokens] * 2
    return [pltpu.VMEM((r, width), jnp.float32) for r in rows]


def complete_group(lay, n, block, lefts, rights, params):
    width = block.shape[-1]
    vmem = pl.BlockSpec(memory_space=pltpu.VMEM)
    shapes = group_shapes(lay, n, width)
    sums = shapes[-1][0] * lay.tokens * width
    return pl.pallas_call(
        functools.partial(group_kernel, lay, n),
        out_shape=[jax.ShapeDtypeStruct(shape, jnp.float32) for shape in shapes],
        in_specs=[vmem] * (1 + 2 * n + len(params)),
        out_specs=[vmem] * len(shapes),
        scratch_shapes=scratch_shapes(lay, width),
        cost_estimate=pl.CostEstimate(
            flops=10 * lay.chunk * width * width + 2 * sums,
            bytes_accessed=20 * lay.chunk * width,
            transcendentals=3 * lay.chunk * width,
        ),
        compiler_params=pltpu.CompilerParams(vmem_limit_bytes=4 << 20),
    )(block, *lefts, *rights, *params)


def finish(lay, ours, middle, right, real, params, scratch, out):
    gain_in, gain_out, proj, gate_weight, out_weight, proj_bias, gate_bias, out_bias = params
    left, rough, result = scratch
    tokens, per, pitch = lay.tokens, lay.per, lay.pitch
    width = out.shape[-1]
    marks = real[...]
    columns = jnp.concatenate([middle[pl.ds(r, tokens, stride=pitch), :] for r in ours], axis=0)
    (packed,) = normed_matmul(columns, gain_in[1:2, :], (proj[1, :, 0 : 2 * width],), (proj_bias[1:2, 0 : 2 * width],))
    left[...] = gated(packed, width) * jnp.concatenate([marks] * len(ours), axis=0)
    held = jnp.concatenate([middle[r * pitch : r * pitch + tokens, :] for r in ours], axis=0)
    (gates,) = normed_matmul(held, gain_in[1:2, :], (gate_weight[1],), (gate_bias[1:2, :],))
    gates = jnp.tanh(gates) + 1.0
    totals = [jnp.zeros((tokens, width), jnp.float32)] * len(ours)
    for k in range(tokens):
        row = right[k * tokens : (k + 1) * tokens, :]
        for r in range(len(ours)):
            totals[r] = totals[r] + left[r * tokens + k : r * tokens + k + 1, :] * row
    product = jnp.concatenate([t * (marks * real[r : r + 1, :]) for r, t in zip(ours, totals, strict=True)], axis=0)
    (change,) = normed_matmul(product, gain_out[1:2, :], (out_weight[1],), (out_bias[1:2, :],))
    value = held + gates * change
    for r in range(len(ours)):
        rough[r * pitch : r * pitch + tokens, :] = value[r * tokens : (r + 1) * tokens, :]
    for first, at in lay.places():
        for t in range(per):
            row = rough[pl.ds(first + t, len(ours), stride=pitch), :]
            result[pl.ds(at * per + t, len(ours), stride=pitch), :] = row
    halves = [result[r * pitch : r * pitch + tokens, :] for r in range(len(ours))]
    out[...] = jnp.concatenate(halves, axis=0).astype(jnp.bfloat16)


def finish_scratch(lay, width):
    rows = [lay.per * lay.tokens, (lay.per + 1) * lay.pitch, (lay.per + 1) * lay.pitch]
    return [pltpu.VMEM((r, width), jnp.float32) for r in rows]


def odd_kernel(lay, middle, right, real, *refs):
    params, out, scratch = refs[:8], refs[8], refs[9:]
    odd = lax.axis_index("row") % 2 == 1
    pl.when(odd)(lambda: finish(lay, range(lay.per), middle, right, real, params, scratch, out))


def updates_kernel(lay, block, *refs):
    last = len(lay.steps) - 1
    done = [refs[6 * n : 6 * n + 6] for n in range(last)]
    params, refs = refs[6 * last : 6 * last + 8], refs[6 * last + 8 :]
    gain_in, gain_out, proj, gate_weight, out_weight, proj_bias, gate_bias, out_bias = params
    out, middle, right1, real = refs[:4]
    own, scratch, last_scratch = refs[4:10], refs[10:15], refs[15:]
    tokens, per, group, chunk, pitch = lay.tokens, lay.per, lay.group, lay.chunk, lay.pitch
    width = out.shape[-1]
    done = done + [own]

    def run():
        prepare(lay, last, block, gain_in, proj, gate_weight, proj_bias, gate_bias, own[:5], scratch)
        complete(lay, last, [arrays[1] for arrays in done], [arrays[2] for arrays in done], own[5])

        marks = jnp.concatenate([arrays[4][...] for arrays in done], axis=0)
        real[...] = marks
        for p in range(last + 1):
            z, _, _, gate, near, _ = done[p]
            products = []
            for i in range(group):
                parts = []
                for q in range(last + 1):
                    n = max(p, q)
                    start = (lay.pairs(n).index((p, q)) * group + i) * group
                    parts.append(done[n][5][start : start + group, :])
                products.append(jnp.concatenate(parts, axis=0) * (marks * near[i : i + 1, :]))
            products = jnp.concatenate(products, axis=0)
            (change,) = normed_matmul(products, gain_out[0:1, :], (out_weight[0],), (out_bias[0:1, :],))
            held = jnp.concatenate([z[t * pitch : t * pitch + tokens, :] for t in range(group)], axis=0)
            moved = held + gate[...] * change
            for t in range(group):
                at = (p * group + t) * pitch
                middle[at : at + tokens, :] = moved[t * tokens : (t + 1) * tokens, :]

        for p in range(last + 1):
            starts = [(p * group + t) * pitch for t in range(group)]
            values = jnp.concatenate([middle[at : at + tokens, :] for at in starts], axis=0)
            (packed,) = normed_matmul(
                values, gain_in[1:2, :], (proj[1, :, 2 * width :],), (proj_bias[1:2, 2 * width :],)
            )
            right1[p * chunk : (p + 1) * chunk, :] = gated(packed, width)

        finish(lay, range(per, 2 * per), middle, right1, real, params, last_scratch, out)

    pl.when(lax.axis_index("row") % 2 == 1)(run)


def updates(lay, blocks, params):
    width = blocks[0].shape[-1]
    rows = lay.per * lay.tokens
    pairs = lay.tokens * lay.tokens
    gain_in, _, proj, gate_weight, _, proj_bias, gate_bias, _ = params
    group_params = (gain_in, proj, gate_weight, proj_bias, gate_bias)
    done = []
    for n, block in enumerate(blocks[:-1]):
        lefts, rights = [arrays[1] for arrays in done], [arrays[2] for arrays in done]
        done.append(complete_group(lay, n, block, lefts, rights, group_params))
    arrays = [array for arrays in done for array in arrays]
    vmem = pl.BlockSpec(memory_space=pltpu.VMEM)
    out = jax.ShapeDtypeStruct((rows, width), jnp.bfloat16)
    shared = [((lay.tokens + 1) * lay.pitch, width), (pairs, width), (lay.tokens, width)]
    even, *shared = pl.pallas_call(
        functools.partial(updates_kernel, lay),
        out_shape=[out] + [jax.ShapeDtypeStruct(shape, jnp.float32) for shape in shared],
        in_specs=[vmem] * (1 + len(arrays) + len(params)),
        out_specs=[vmem] * 4,
        scratch_shapes=[pltpu.VMEM(shape, jnp.float32) for shape in group_shapes(lay, len(blocks) - 1, width)]
        + scratch_shapes(lay, width)
        + finish_scratch(lay, width),
        compiler_params=pltpu.CompilerParams(vmem_limit_bytes=8 << 20),
    )(blocks[-1], *arrays, *params)
    odd = pl.pallas_call(
        functools.partial(odd_kernel, lay),
        out_shape=out,
        in_specs=[vmem] * (3 + len(params)),
        out_specs=vmem,
        scratch_shapes=finish_scratch(lay, width),
        cost_estimate=pl.CostEstimate(
            flops=8 * rows * width * width, bytes_accessed=8 * pairs * width, transcendentals=2 * rows * width
        ),
        compiler_params=pltpu.CompilerParams(vmem_limit_bytes=4 << 20),
    )(*shared, *params)
    return even, odd


def swap(values, step, n_row):
    return lax.ppermute(values, "row", [(i, i ^ step) for i in range(n_row)])


def odd_swap(values, step, n_group, n_row):
    if n_group % 2:
        return swap(values, step, n_row)
    target = [(g, i ^ step) if i % 2 else (g ^ 1, i) for g in range(n_group) for i in range(n_row)]
    pairs = [(source, g * n_row + i) for source, (g, i) in enumerate(target)]
    return lax.ppermute(values, ("groups", "row"), pairs)


def merge(first, second, rows):
    return jnp.concatenate([first[:rows], second[:rows], first[rows:] + second[rows:]], axis=0)


def gathered(n_group, n_row, pair_rep, pair_mask, *params):
    per, tokens, width = pair_rep.shape
    rows = per * tokens
    me = lax.axis_index("row")
    own = pair_rep.reshape(rows, width)
    other = swap(own, 1, n_row)
    other_mask = swap(pair_mask, 1, n_row)
    own, mask = fetch(own, pair_mask)
    other, other_mask, own, mask = lax.optimization_barrier((other, other_mask, own, mask))
    held = join(n_row, own, mask, other, other_mask)
    order = [0, 1]
    step = n_row // 2
    while step > 4:
        count = len(order)
        held = merge(held, odd_swap(held, step, n_group, n_row), count * rows)
        order = order + [place ^ step for place in order]
        step //= 2
    held, *params = lax.optimization_barrier((held, *load(*params)))
    steps = [0] + list(range(2, 2 * step, 2))
    steps[2:] = reversed(steps[2:])
    blocks = [held] + [odd_swap(held, place, n_group, n_row) for place in steps[1:]]
    even, odd = updates(Layout(n_row, order, steps, tokens), blocks, params)
    out = jnp.where(me % 2 == 1, odd, swap(even, 1, n_row))
    return out.reshape(per, tokens, width)


H = 128


def layer_norm(values, gain, offset, axis):
    mean = jnp.mean(values, axis=axis, keepdims=True)
    centered = values - mean
    variance = jnp.mean(centered * centered, axis=axis, keepdims=True)
    return centered * lax.rsqrt(variance + 1e-05) * gain + offset


def triangle(
    pair_now,
    pair_mask,
    layer_index,
    gain_in,
    shift_in,
    proj_weight,
    gate_weight,
    gain_out,
    shift_out,
    out_weight,
):
    normed = layer_norm(
        pair_now.astype(jnp.float32), gain_in[layer_index], shift_in[layer_index], -1
    ).astype(jnp.bfloat16)
    packed = jnp.einsum(
        "rnc,ch->hrn", normed, proj_weight[layer_index], preferred_element_type=jnp.float32
    )
    masked = pair_mask.astype(jnp.float32)[None, :, :]
    left = (masked * jax.nn.sigmoid(packed[0:H]) * packed[H : 2 * H]).astype(jnp.bfloat16)
    right = (masked * jax.nn.sigmoid(packed[2 * H : 3 * H]) * packed[3 * H :]).astype(jnp.bfloat16)
    gating = jax.nn.sigmoid(
        jnp.einsum(
            "rnc,cd->rnd", normed, gate_weight[layer_index], preferred_element_type=jnp.float32
        )
    )
    lifted_left, lifted_right = (
        lax.all_to_all(left, "row", split_axis=0, concat_axis=1, tiled=True),
        lax.all_to_all(right, "row", split_axis=0, concat_axis=1, tiled=True),
    )
    if layer_index == 0:
        product = jnp.einsum(
            "hik,hjk->hij", lifted_left, lifted_right, preferred_element_type=jnp.float32
        )
    else:
        product = jnp.einsum(
            "hki,hkj->hij", lifted_left, lifted_right, preferred_element_type=jnp.float32
        )
    product = product.astype(jnp.bfloat16)
    out_gain = gain_out[layer_index][:, None, None]
    out_shift = shift_out[layer_index][:, None, None]
    out_proj = out_weight[layer_index]
    returned = lax.all_to_all(product, "row", split_axis=1, concat_axis=0, tiled=True)
    scaled = layer_norm(returned.astype(jnp.float32), out_gain, out_shift, 0).astype(jnp.bfloat16)
    update = jnp.einsum("hrn,hc->rnc", scaled, out_proj, preferred_element_type=jnp.float32)
    return (pair_now.astype(jnp.float32) + gating * update).astype(jnp.bfloat16)


def exchanged(
    pair_rep,
    pair_mask,
    gain_in,
    shift_in,
    proj_weight,
    gate_weight,
    gain_out,
    shift_out,
    out_weight,
):
    current = pair_rep
    for layer_index in range(2):
        current = triangle(
            current,
            pair_mask,
            layer_index,
            gain_in,
            shift_in,
            proj_weight,
            gate_weight,
            gain_out,
            shift_out,
            out_weight,
        )
    return current


def solution(mesh):
    n_group, n_row = mesh.shape["groups"], mesh.shape["row"]

    def shards(pair_rep, *rest):
        per, tokens, _ = pair_rep.shape
        small = pair_rep.size * n_row * 2 <= GATHER_LIMIT
        fits = n_row & (n_row - 1) == 0 and n_row > 7 and tokens % 32 == 0 and tokens <= pair_rep.shape[2]
        if small and fits:
            return gathered(n_group, n_row, pair_rep, *rest)
        return exchanged(pair_rep, *rest)

    in_specs = (
        P(("groups", "row"), None, None),
        P(("groups", "row"), None),
        P(),
        P(),
        P(),
        P(),
        P(),
        P(),
        P(),
    )
    out_specs = P(("groups", "row"), None, None)
    return jax.shard_map(shards, mesh=mesh, in_specs=in_specs, out_specs=out_specs, check_vma=False)
```

```python
import functools

import jax
import jax.numpy as jnp
from jax import lax
from jax.experimental import pallas as pl
from jax.experimental.pallas import tpu as pltpu
from jax.sharding import PartitionSpec as P

EPS = 1e-05
MARK_ROWS = 16
GATHER_LIMIT = 4 << 20


def matmul(left, right):
    return jnp.dot(left, right, preferred_element_type=jnp.float32)


def normed_piece(values, gain, weights, biases):
    width = values.shape[-1]
    centered = values - jnp.mean(values, axis=-1, keepdims=True)
    scale = lax.rsqrt(jnp.sum(centered * centered, axis=-1, keepdims=True) + width * EPS)
    factor = (centered * (gain * width**0.5)).astype(jnp.bfloat16)
    return [matmul(factor, weight) * scale + bias for weight, bias in zip(weights, biases, strict=True)]


def normed_matmul(values, gain, weights, biases):
    pieces = [normed_piece(values[at : at + 128], gain, weights, biases) for at in range(0, values.shape[0], 128)]
    return [jnp.concatenate(parts, axis=0) for parts in zip(*pieces, strict=True)]


def gated(packed, width):
    return (jnp.tanh(packed[:, :width]) + 1.0) * packed[:, width:]


def seat(device, n_row):
    place = device % 2
    step, weight = n_row // 2, 2
    while step > 4:
        place = place + weight * (device // step % 2)
        step, weight = step // 2, 2 * weight
    return place


def seats(n_row):
    return max(2, n_row // 4)


def hold(values):
    return pltpu.with_memory_space_constraint(values, pltpu.HBM)


def mark_rows(n_row, per):
    return -(-(seats(n_row) * per + 1) // MARK_ROWS) * MARK_ROWS


def join_kernel(n_row, own, mask, other, other_mask, out_ref, marks):
    rows = own.shape[0]
    per, tokens = mask.shape
    width = out_ref.shape[1]
    me = lax.axis_index("row")
    out_ref[0:rows, :] = own[...]
    out_ref[rows : 2 * rows, :] = other[...]
    marks[...] = jnp.zeros_like(marks)
    last = seats(n_row) * per
    seen = []
    for device, ref in ((me, mask), (me ^ 1, other_mask)):
        mine = ref[...].astype(jnp.float32)
        first = seat(device, n_row) * per
        marks[pl.ds(first, per), :] = jnp.broadcast_to(jnp.max(mine, axis=1, keepdims=True), (per, width))
        seen.append(jnp.max(mine, axis=0, keepdims=True))
    marks[last : last + 1, 0:tokens] = jnp.maximum(*seen)
    out_ref[2 * rows :, :] = marks[...].astype(jnp.bfloat16)


def join(n_row, own, mask, other, other_mask):
    rows, width = own.shape
    extra = mark_rows(n_row, mask.shape[0])
    vmem = pl.BlockSpec(memory_space=pltpu.VMEM)
    return pl.pallas_call(
        functools.partial(join_kernel, n_row),
        out_shape=jax.ShapeDtypeStruct((2 * rows + extra, width), jnp.bfloat16),
        in_specs=[vmem] * 4,
        out_specs=vmem,
        scratch_shapes=[pltpu.VMEM((extra, width), jnp.float32)],
        compiler_params=pltpu.CompilerParams(vmem_limit_bytes=1 << 20),
    )(own, mask, other, other_mask)


def fetch_kernel(count, *refs):
    sources, targets, sems = refs[:count], refs[count : 2 * count], refs[2 * count]
    copies = [pltpu.make_async_copy(s, t, sems.at[n]) for n, (s, t) in enumerate(zip(sources, targets, strict=True))]
    for copy in copies:
        copy.start()
    for copy in copies:
        copy.wait()


def fetch(*arrays):
    count = len(arrays)
    return pl.pallas_call(
        functools.partial(fetch_kernel, count),
        out_shape=[jax.ShapeDtypeStruct(a.shape, a.dtype) for a in arrays],
        in_specs=[pl.BlockSpec(memory_space=pltpu.HBM)] * count,
        out_specs=[pl.BlockSpec(memory_space=pltpu.VMEM)] * count,
        scratch_shapes=[pltpu.SemaphoreType.DMA((count,))],
        compiler_params=pltpu.CompilerParams(vmem_limit_bytes=1 << 20),
    )(*[hold(a) for a in arrays])


def load_kernel(sources, targets):
    (gain_in, shift_in, proj, gate, gain_out, shift_out, out), sems = sources[:7], sources[-1]
    held = sources[7:-1]
    copies = [
        pltpu.make_async_copy(source, target, sems.at[n])
        for n, (source, target) in enumerate(
            zip((proj, gate, out, shift_in, shift_out, gain_in, gain_out), (*held, targets[0], targets[1]), strict=True)
        )
    ]
    for copy in copies:
        copy.start()
    for copy in copies:
        copy.wait()
    proj, gate, out, shift_in, shift_out = held
    _, _, proj_half, gate_half, out_half, proj_bias, gate_bias, out_bias = targets
    half = jnp.array(0.5, jnp.bfloat16)
    for weight, halved, bias, shift in (
        (proj, proj_half, proj_bias, shift_in),
        (gate, gate_half, gate_bias, shift_in),
        (out, out_half, out_bias, shift_out),
    ):
        halved[...] = weight[...] * half
        exact = shift[...]
        high = exact.astype(jnp.bfloat16)
        low = (exact - high.astype(jnp.float32)).astype(jnp.bfloat16)
        rows = jnp.concatenate([high, low] + [jnp.zeros_like(high)] * 6, axis=0)
        for u in range(2):
            both = matmul(rows, weight[u])
            bias[u : u + 1, :] = 0.5 * (both[u : u + 1, :] + both[u + 2 : u + 3, :])


def load(gain_in, shift_in, proj, gate, gain_out, shift_out, out):
    arrays = (gain_in, shift_in, proj, gate, gain_out, shift_out, out)
    weights = (proj, gate, out)
    shapes = [(a.shape, a.dtype) for a in (gain_in, gain_out, *weights)]
    shapes += [((a.shape[0], a.shape[2]), jnp.float32) for a in weights]
    vmem = pl.BlockSpec(memory_space=pltpu.VMEM)

    def kernel(*refs):
        load_kernel((*refs[:7], *refs[7 + len(shapes) :]), refs[7 : 7 + len(shapes)])

    return pl.pallas_call(
        kernel,
        out_shape=[jax.ShapeDtypeStruct(*shape) for shape in shapes],
        in_specs=[pl.BlockSpec(memory_space=pltpu.HBM)] * len(arrays),
        out_specs=[vmem] * len(shapes),
        scratch_shapes=[pltpu.VMEM(a.shape, a.dtype) for a in (*weights, shift_in, shift_out)]
        + [pltpu.SemaphoreType.DMA((len(arrays),))],
        compiler_params=pltpu.CompilerParams(vmem_limit_bytes=4 << 20),
    )(*[hold(a) for a in arrays])


class Layout:
    def __init__(self, n_row, order, steps, tokens):
        self.n_row, self.order, self.steps, self.tokens = n_row, order, steps, tokens
        self.per = tokens // n_row
        self.group = len(order) * self.per
        self.chunk = self.group * tokens
        self.pitch = tokens + 8
        self.marks = mark_rows(n_row, self.per)
        self.column_marks = seats(n_row) * self.per

    def places(self):
        me = lax.axis_index("row")
        for n, step in enumerate(self.steps):
            for slot, place in enumerate(self.order):
                yield n * self.group + slot * self.per, me ^ (step ^ place)

    def pairs(self, n):
        return [(n, q) for q in range(n + 1)] + [(p, n) for p in range(n)]


def prepare(lay, n, block, gain, proj, gate_weight, proj_bias, gate_bias, outs, scratch):
    z, left, right_t, gate, near = outs
    marks, rough, right, columns, seen = scratch
    tokens, group, per, chunk, pitch = lay.tokens, lay.group, lay.per, lay.chunk, lay.pitch
    width = z.shape[-1]
    places = list(lay.places())
    marks[...] = block[chunk:, :].astype(jnp.float32)
    diagonal = lax.broadcasted_iota(jnp.int32, (tokens, tokens), 0)
    diagonal = diagonal == lax.broadcasted_iota(jnp.int32, (tokens, tokens), 1)
    row = jnp.minimum(marks[lay.column_marks : lay.column_marks + 1, 0:tokens], 1.0)
    column = jnp.sum(jnp.where(diagonal, row, 0.0), axis=1, keepdims=True)
    columns[...] = jnp.broadcast_to(column, (tokens, width))
    for first, at in places:
        seen[first : first + per, :] = columns[pl.ds(at * per, per), :]
    for first, at in places[n * len(lay.order) : (n + 1) * len(lay.order)]:
        near[first - n * group : first - n * group + per, :] = marks[pl.ds(seat(at, lay.n_row) * per, per), :]
    for t in range(group):
        rough[t * pitch : t * pitch + tokens, :] = block[t * tokens : (t + 1) * tokens, :].astype(jnp.float32)
    for first, at in places:
        for t in range(per):
            z[pl.ds(first + t, group, stride=pitch), :] = rough[pl.ds(at * per + t, group, stride=pitch), :]
    values = jnp.concatenate([z[t * pitch : t * pitch + tokens, :] for t in range(group)], axis=0)
    packed, gates = normed_matmul(
        values, gain[0:1, :], (proj[0], gate_weight[0]), (proj_bias[0:1, :], gate_bias[0:1, :])
    )
    value = gated(packed[:, 0 : 2 * width], width)
    for t in range(group):
        left[t * tokens : (t + 1) * tokens, :] = value[t * tokens : (t + 1) * tokens, :] * near[t : t + 1, :]
    value = gated(packed[:, 2 * width :], width)
    for t in range(group):
        right[t * pitch : t * pitch + tokens, :] = value[t * tokens : (t + 1) * tokens, :]
    for k in range(tokens):
        real = near[...] * seen[k : k + 1, :]
        right_t[k * group : (k + 1) * group, :] = right[pl.ds(k, group, stride=pitch), :] * real
    gate[...] = jnp.tanh(gates) + 1.0


def block_sums(lay, blocks, size):
    tokens, group = lay.tokens, lay.group
    width = blocks[0][0].shape[-1]
    results = []
    for start in range(0, len(blocks), size):
        some = blocks[start : start + size]
        totals = [[jnp.zeros((group, width), jnp.float32)] * group for _ in some]
        for k in range(tokens):
            rows = {id(right): right[k * group : (k + 1) * group, :] for _, right in some}
            for i in range(group):
                values = {id(left): left[i * tokens + k : i * tokens + k + 1, :] for left, _ in some}
                for total, (left, right) in zip(totals, some, strict=True):
                    total[i] = total[i] + values[id(left)] * rows[id(right)]
        results += totals
    return results


def complete(lay, n, lefts, rights, sums):
    size = lay.group * lay.group
    totals = block_sums(lay, [(lefts[p], rights[q]) for p, q in lay.pairs(n)], 5)
    for place, total in enumerate(totals):
        sums[place * size : (place + 1) * size, :] = jnp.concatenate(total, axis=0)


def group_kernel(lay, n, block, *refs):
    lefts, rights, refs = refs[:n], refs[n : 2 * n], refs[2 * n :]
    params, outs, sums, scratch = refs[:5], refs[5:10], refs[10], refs[11:]

    def run():
        prepare(lay, n, block, *params, outs, scratch)
        complete(lay, n, [*lefts, outs[1]], [*rights, outs[2]], sums)

    pl.when(lax.axis_index("row") % 2 == 1)(run)


def group_shapes(lay, n, width):
    count = len(lay.pairs(n)) * lay.group * lay.group
    rows = [(lay.group + 1) * lay.pitch, lay.chunk, lay.chunk, lay.chunk, lay.group, count]
    return [(r, width) for r in rows]


def scratch_shapes(lay, width):
    rows = [lay.marks] + [(lay.group + 1) * lay.pitch] * 2 + [lay.tokens] * 2
    return [pltpu.VMEM((r, width), jnp.float32) for r in rows]


def complete_group(lay, n, block, lefts, rights, params):
    width = block.shape[-1]
    vmem = pl.BlockSpec(memory_space=pltpu.VMEM)
    shapes = group_shapes(lay, n, width)
    sums = shapes[-1][0] * lay.tokens * width
    return pl.pallas_call(
        functools.partial(group_kernel, lay, n),
        out_shape=[jax.ShapeDtypeStruct(shape, jnp.float32) for shape in shapes],
        in_specs=[vmem] * (1 + 2 * n + len(params)),
        out_specs=[vmem] * len(shapes),
        scratch_shapes=scratch_shapes(lay, width),
        cost_estimate=pl.CostEstimate(
            flops=10 * lay.chunk * width * width + 2 * sums,
            bytes_accessed=20 * lay.chunk * width,
            transcendentals=3 * lay.chunk * width,
        ),
        compiler_params=pltpu.CompilerParams(vmem_limit_bytes=4 << 20),
    )(block, *lefts, *rights, *params)


def finish(lay, ours, middle, right, real, params, scratch, out):
    gain_in, gain_out, proj, gate_weight, out_weight, proj_bias, gate_bias, out_bias = params
    left, rough, result = scratch
    tokens, per, pitch = lay.tokens, lay.per, lay.pitch
    width = out.shape[-1]
    marks = real[...]
    columns = jnp.concatenate([middle[pl.ds(r, tokens, stride=pitch), :] for r in ours], axis=0)
    (packed,) = normed_matmul(columns, gain_in[1:2, :], (proj[1, :, 0 : 2 * width],), (proj_bias[1:2, 0 : 2 * width],))
    left[...] = gated(packed, width) * jnp.concatenate([marks] * len(ours), axis=0)
    held = jnp.concatenate([middle[r * pitch : r * pitch + tokens, :] for r in ours], axis=0)
    (gates,) = normed_matmul(held, gain_in[1:2, :], (gate_weight[1],), (gate_bias[1:2, :],))
    gates = jnp.tanh(gates) + 1.0
    totals = [jnp.zeros((tokens, width), jnp.float32)] * len(ours)
    for k in range(tokens):
        row = right[k * tokens : (k + 1) * tokens, :]
        for r in range(len(ours)):
            totals[r] = totals[r] + left[r * tokens + k : r * tokens + k + 1, :] * row
    product = jnp.concatenate([t * (marks * real[r : r + 1, :]) for r, t in zip(ours, totals, strict=True)], axis=0)
    (change,) = normed_matmul(product, gain_out[1:2, :], (out_weight[1],), (out_bias[1:2, :],))
    value = held + gates * change
    for r in range(len(ours)):
        rough[r * pitch : r * pitch + tokens, :] = value[r * tokens : (r + 1) * tokens, :]
    for first, at in lay.places():
        for t in range(per):
            row = rough[pl.ds(first + t, len(ours), stride=pitch), :]
            result[pl.ds(at * per + t, len(ours), stride=pitch), :] = row
    halves = [result[r * pitch : r * pitch + tokens, :] for r in range(len(ours))]
    out[...] = jnp.concatenate(halves, axis=0).astype(jnp.bfloat16)


def finish_scratch(lay, width):
    rows = [lay.per * lay.tokens, (lay.per + 1) * lay.pitch, (lay.per + 1) * lay.pitch]
    return [pltpu.VMEM((r, width), jnp.float32) for r in rows]


def odd_kernel(lay, middle, right, real, *refs):
    params, out, scratch = refs[:8], refs[8], refs[9:]
    odd = lax.axis_index("row") % 2 == 1
    pl.when(odd)(lambda: finish(lay, range(lay.per), middle, right, real, params, scratch, out))


def updates_kernel(lay, block, *refs):
    last = len(lay.steps) - 1
    done = [refs[6 * n : 6 * n + 6] for n in range(last)]
    params, refs = refs[6 * last : 6 * last + 8], refs[6 * last + 8 :]
    gain_in, gain_out, proj, gate_weight, out_weight, proj_bias, gate_bias, out_bias = params
    out, middle, right1, real = refs[:4]
    own, scratch, last_scratch = refs[4:10], refs[10:15], refs[15:]
    tokens, per, group, chunk, pitch = lay.tokens, lay.per, lay.group, lay.chunk, lay.pitch
    width = out.shape[-1]
    done = done + [own]

    def run():
        prepare(lay, last, block, gain_in, proj, gate_weight, proj_bias, gate_bias, own[:5], scratch)
        complete(lay, last, [arrays[1] for arrays in done], [arrays[2] for arrays in done], own[5])

        marks = jnp.concatenate([arrays[4][...] for arrays in done], axis=0)
        real[...] = marks
        for p in range(last + 1):
            z, _, _, gate, _, _ = done[p]
            products = []
            for i in range(group):
                parts = []
                for q in range(last + 1):
                    n = max(p, q)
                    start = (lay.pairs(n).index((p, q)) * group + i) * group
                    parts.append(done[n][5][start : start + group, :])
                products += parts
            products = jnp.concatenate(products, axis=0)
            (change,) = normed_matmul(products, gain_out[0:1, :], (out_weight[0],), (out_bias[0:1, :],))
            held = jnp.concatenate([z[t * pitch : t * pitch + tokens, :] for t in range(group)], axis=0)
            moved = held + gate[...] * change
            for t in range(group):
                at = (p * group + t) * pitch
                middle[at : at + tokens, :] = moved[t * tokens : (t + 1) * tokens, :]

        for p in range(last + 1):
            starts = [(p * group + t) * pitch for t in range(group)]
            values = jnp.concatenate([middle[at : at + tokens, :] for at in starts], axis=0)
            (packed,) = normed_matmul(
                values, gain_in[1:2, :], (proj[1, :, 2 * width :],), (proj_bias[1:2, 2 * width :],)
            )
            right1[p * chunk : (p + 1) * chunk, :] = gated(packed, width)

        finish(lay, range(per, 2 * per), middle, right1, real, params, last_scratch, out)

    pl.when(lax.axis_index("row") % 2 == 1)(run)


def updates(lay, blocks, params):
    width = blocks[0].shape[-1]
    rows = lay.per * lay.tokens
    pairs = lay.tokens * lay.tokens
    gain_in, _, proj, gate_weight, _, proj_bias, gate_bias, _ = params
    group_params = (gain_in, proj, gate_weight, proj_bias, gate_bias)
    done = []
    for n, block in enumerate(blocks[:-1]):
        lefts, rights = [arrays[1] for arrays in done], [arrays[2] for arrays in done]
        done.append(complete_group(lay, n, block, lefts, rights, group_params))
    arrays = [array for arrays in done for array in arrays]
    vmem = pl.BlockSpec(memory_space=pltpu.VMEM)
    out = jax.ShapeDtypeStruct((rows, width), jnp.bfloat16)
    shared = [((lay.tokens + 1) * lay.pitch, width), (pairs, width), (lay.tokens, width)]
    even, *shared = pl.pallas_call(
        functools.partial(updates_kernel, lay),
        out_shape=[out] + [jax.ShapeDtypeStruct(shape, jnp.float32) for shape in shared],
        in_specs=[vmem] * (1 + len(arrays) + len(params)),
        out_specs=[vmem] * 4,
        scratch_shapes=[pltpu.VMEM(shape, jnp.float32) for shape in group_shapes(lay, len(blocks) - 1, width)]
        + scratch_shapes(lay, width)
        + finish_scratch(lay, width),
        compiler_params=pltpu.CompilerParams(vmem_limit_bytes=8 << 20),
    )(blocks[-1], *arrays, *params)
    odd = pl.pallas_call(
        functools.partial(odd_kernel, lay),
        out_shape=out,
        in_specs=[vmem] * (3 + len(params)),
        out_specs=vmem,
        scratch_shapes=finish_scratch(lay, width),
        cost_estimate=pl.CostEstimate(
            flops=8 * rows * width * width, bytes_accessed=8 * pairs * width, transcendentals=2 * rows * width
        ),
        compiler_params=pltpu.CompilerParams(vmem_limit_bytes=4 << 20),
    )(*shared, *params)
    return even, odd


def swap(values, step, n_row):
    return lax.ppermute(values, "row", [(i, i ^ step) for i in range(n_row)])


def odd_swap(values, step, n_group, n_row, even_step=0):
    if n_group % 2:
        return swap(values, step, n_row)
    idle = [(g, i ^ even_step) if even_step else (g ^ 1, i) for g in range(n_group) for i in range(n_row)]
    target = [(n // n_row, n % n_row ^ step) if n % 2 else place for n, place in enumerate(idle)]
    pairs = [(source, g * n_row + i) for source, (g, i) in enumerate(target)]
    return lax.ppermute(values, ("groups", "row"), pairs)


def merge(first, second, rows):
    return jnp.concatenate([first[:rows], second[:rows], first[rows:] + second[rows:]], axis=0)


def gathered(n_group, n_row, pair_rep, pair_mask, *params):
    per, tokens, width = pair_rep.shape
    rows = per * tokens
    me = lax.axis_index("row")
    own = pair_rep.reshape(rows, width)
    other = swap(own, 1, n_row)
    other_mask = swap(pair_mask, 1, n_row)
    own, mask = fetch(own, pair_mask)
    other, other_mask, own, mask = lax.optimization_barrier((other, other_mask, own, mask))
    held = join(n_row, own, mask, other, other_mask)
    order = [0, 1]
    step = n_row // 2
    while step > 4:
        count = len(order)
        held = merge(held, odd_swap(held, step, n_group, n_row, 2), count * rows)
        order = order + [place ^ step for place in order]
        step //= 2
    held, *params = lax.optimization_barrier((held, *load(*params)))
    steps = [0] + list(range(2, 2 * step, 2))
    steps[2:] = reversed(steps[2:])
    blocks = [held] + [odd_swap(held, place, n_group, n_row) for place in steps[1:]]
    even, odd = updates(Layout(n_row, order, steps, tokens), blocks, params)
    out = jnp.where(me % 2 == 1, odd, swap(even, 1, n_row))
    return out.reshape(per, tokens, width)


H = 128


def layer_norm(values, gain, offset, axis):
    mean = jnp.mean(values, axis=axis, keepdims=True)
    centered = values - mean
    variance = jnp.mean(centered * centered, axis=axis, keepdims=True)
    return centered * lax.rsqrt(variance + 1e-05) * gain + offset


def triangle(
    pair_now,
    pair_mask,
    layer_index,
    gain_in,
    shift_in,
    proj_weight,
    gate_weight,
    gain_out,
    shift_out,
    out_weight,
):
    normed = layer_norm(
        pair_now.astype(jnp.float32), gain_in[layer_index], shift_in[layer_index], -1
    ).astype(jnp.bfloat16)
    packed = jnp.einsum(
        "rnc,ch->hrn", normed, proj_weight[layer_index], preferred_element_type=jnp.float32
    )
    masked = pair_mask.astype(jnp.float32)[None, :, :]
    left = (masked * jax.nn.sigmoid(packed[0:H]) * packed[H : 2 * H]).astype(jnp.bfloat16)
    right = (masked * jax.nn.sigmoid(packed[2 * H : 3 * H]) * packed[3 * H :]).astype(jnp.bfloat16)
    gating = jax.nn.sigmoid(
        jnp.einsum(
            "rnc,cd->rnd", normed, gate_weight[layer_index], preferred_element_type=jnp.float32
        )
    )
    lifted_left, lifted_right = (
        lax.all_to_all(left, "row", split_axis=0, concat_axis=1, tiled=True),
        lax.all_to_all(right, "row", split_axis=0, concat_axis=1, tiled=True),
    )
    if layer_index == 0:
        product = jnp.einsum(
            "hik,hjk->hij", lifted_left, lifted_right, preferred_element_type=jnp.float32
        )
    else:
        product = jnp.einsum(
            "hki,hkj->hij", lifted_left, lifted_right, preferred_element_type=jnp.float32
        )
    product = product.astype(jnp.bfloat16)
    out_gain = gain_out[layer_index][:, None, None]
    out_shift = shift_out[layer_index][:, None, None]
    out_proj = out_weight[layer_index]
    returned = lax.all_to_all(product, "row", split_axis=1, concat_axis=0, tiled=True)
    scaled = layer_norm(returned.astype(jnp.float32), out_gain, out_shift, 0).astype(jnp.bfloat16)
    update = jnp.einsum("hrn,hc->rnc", scaled, out_proj, preferred_element_type=jnp.float32)
    return (pair_now.astype(jnp.float32) + gating * update).astype(jnp.bfloat16)


def exchanged(
    pair_rep,
    pair_mask,
    gain_in,
    shift_in,
    proj_weight,
    gate_weight,
    gain_out,
    shift_out,
    out_weight,
):
    current = pair_rep
    for layer_index in range(2):
        current = triangle(
            current,
            pair_mask,
            layer_index,
            gain_in,
            shift_in,
            proj_weight,
            gate_weight,
            gain_out,
            shift_out,
            out_weight,
        )
    return current


def solution(mesh):
    n_group, n_row = mesh.shape["groups"], mesh.shape["row"]

    def shards(pair_rep, *rest):
        per, tokens, _ = pair_rep.shape
        small = pair_rep.size * n_row * 2 <= GATHER_LIMIT
        fits = n_row & (n_row - 1) == 0 and n_row > 7 and tokens % 32 == 0 and tokens <= pair_rep.shape[2]
        if small and fits:
            return gathered(n_group, n_row, pair_rep, *rest)
        return exchanged(pair_rep, *rest)

    in_specs = (
        P(("groups", "row"), None, None),
        P(("groups", "row"), None),
        P(),
        P(),
        P(),
        P(),
        P(),
        P(),
        P(),
    )
    out_specs = P(("groups", "row"), None, None)
    return jax.shard_map(shards, mesh=mesh, in_specs=in_specs, out_specs=out_specs, check_vma=False)
```

```python
import functools

import jax
import jax.numpy as jnp
from jax import lax
from jax.experimental import pallas as pl
from jax.experimental.pallas import tpu as pltpu
from jax.sharding import PartitionSpec as P

EPS = 1e-05
MARK_ROWS = 16
GATHER_LIMIT = 4 << 20


def matmul(left, right):
    return jnp.dot(left, right, preferred_element_type=jnp.float32)


def normed_piece(values, gain, weights, biases):
    width = values.shape[-1]
    centered = values - jnp.mean(values, axis=-1, keepdims=True)
    scale = lax.rsqrt(jnp.sum(centered * centered, axis=-1, keepdims=True) + width * EPS)
    factor = (centered * (gain * width**0.5)).astype(jnp.bfloat16)
    return [matmul(factor, weight) * scale + bias for weight, bias in zip(weights, biases, strict=True)]


def normed_matmul(values, gain, weights, biases):
    pieces = [normed_piece(values[at : at + 128], gain, weights, biases) for at in range(0, values.shape[0], 128)]
    return [jnp.concatenate(parts, axis=0) for parts in zip(*pieces, strict=True)]


def gated(packed, width):
    return (jnp.tanh(packed[:, :width]) + 1.0) * packed[:, width:]


def seat(device, n_row):
    place = device % 2
    step, weight = n_row // 2, 2
    while step > 4:
        place = place + weight * (device // step % 2)
        step, weight = step // 2, 2 * weight
    return place


def seats(n_row):
    return max(2, n_row // 4)


def hold(values):
    return pltpu.with_memory_space_constraint(values, pltpu.HBM)


def mark_rows(n_row, per):
    return -(-(seats(n_row) * per + 1) // MARK_ROWS) * MARK_ROWS


def join_kernel(n_row, own, mask, other, other_mask, out_ref, marks):
    rows = own.shape[0]
    per, tokens = mask.shape
    width = out_ref.shape[1]
    me = lax.axis_index("row")
    out_ref[0:rows, :] = own[...]
    out_ref[rows : 2 * rows, :] = other[...]
    marks[...] = jnp.zeros_like(marks)
    last = seats(n_row) * per
    seen = []
    for device, ref in ((me, mask), (me ^ 1, other_mask)):
        mine = ref[...].astype(jnp.float32)
        first = seat(device, n_row) * per
        marks[pl.ds(first, per), :] = jnp.broadcast_to(jnp.max(mine, axis=1, keepdims=True), (per, width))
        seen.append(jnp.max(mine, axis=0, keepdims=True))
    marks[last : last + 1, 0:tokens] = jnp.maximum(*seen)
    out_ref[2 * rows :, :] = marks[...].astype(jnp.bfloat16)


def join(n_row, own, mask, other, other_mask):
    rows, width = own.shape
    extra = mark_rows(n_row, mask.shape[0])
    vmem = pl.BlockSpec(memory_space=pltpu.VMEM)
    return pl.pallas_call(
        functools.partial(join_kernel, n_row),
        out_shape=jax.ShapeDtypeStruct((2 * rows + extra, width), jnp.bfloat16),
        in_specs=[vmem] * 4,
        out_specs=vmem,
        scratch_shapes=[pltpu.VMEM((extra, width), jnp.float32)],
        compiler_params=pltpu.CompilerParams(vmem_limit_bytes=1 << 20),
    )(own, mask, other, other_mask)


def fetch_kernel(count, *refs):
    sources, targets, sems = refs[:count], refs[count : 2 * count], refs[2 * count]
    copies = [pltpu.make_async_copy(s, t, sems.at[n]) for n, (s, t) in enumerate(zip(sources, targets, strict=True))]
    for copy in copies:
        copy.start()
    for copy in copies:
        copy.wait()


def fetch(*arrays):
    count = len(arrays)
    return pl.pallas_call(
        functools.partial(fetch_kernel, count),
        out_shape=[jax.ShapeDtypeStruct(a.shape, a.dtype) for a in arrays],
        in_specs=[pl.BlockSpec(memory_space=pltpu.HBM)] * count,
        out_specs=[pl.BlockSpec(memory_space=pltpu.VMEM)] * count,
        scratch_shapes=[pltpu.SemaphoreType.DMA((count,))],
        compiler_params=pltpu.CompilerParams(vmem_limit_bytes=1 << 20),
    )(*[hold(a) for a in arrays])


def load_kernel(sources, targets):
    (gain_in, shift_in, proj, gate, gain_out, shift_out, out), sems = sources[:7], sources[-1]
    held = sources[7:-1]
    copies = [
        pltpu.make_async_copy(source, target, sems.at[n])
        for n, (source, target) in enumerate(
            zip((proj, gate, out, shift_in, shift_out, gain_in, gain_out), (*held, targets[0], targets[1]), strict=True)
        )
    ]
    for copy in copies:
        copy.start()
    for copy in copies:
        copy.wait()
    proj, gate, out, shift_in, shift_out = held
    _, _, proj_half, gate_half, out_half, proj_bias, gate_bias, out_bias = targets
    half = jnp.array(0.5, jnp.bfloat16)
    for weight, halved, bias, shift in (
        (proj, proj_half, proj_bias, shift_in),
        (gate, gate_half, gate_bias, shift_in),
        (out, out_half, out_bias, shift_out),
    ):
        halved[...] = weight[...] * half
        exact = shift[...]
        high = exact.astype(jnp.bfloat16)
        low = (exact - high.astype(jnp.float32)).astype(jnp.bfloat16)
        rows = jnp.concatenate([high, low] + [jnp.zeros_like(high)] * 6, axis=0)
        for u in range(2):
            both = matmul(rows, weight[u])
            bias[u : u + 1, :] = 0.5 * (both[u : u + 1, :] + both[u + 2 : u + 3, :])


def load(gain_in, shift_in, proj, gate, gain_out, shift_out, out):
    arrays = (gain_in, shift_in, proj, gate, gain_out, shift_out, out)
    weights = (proj, gate, out)
    shapes = [(a.shape, a.dtype) for a in (gain_in, gain_out, *weights)]
    shapes += [((a.shape[0], a.shape[2]), jnp.float32) for a in weights]
    vmem = pl.BlockSpec(memory_space=pltpu.VMEM)

    def kernel(*refs):
        load_kernel((*refs[:7], *refs[7 + len(shapes) :]), refs[7 : 7 + len(shapes)])

    return pl.pallas_call(
        kernel,
        out_shape=[jax.ShapeDtypeStruct(*shape) for shape in shapes],
        in_specs=[pl.BlockSpec(memory_space=pltpu.HBM)] * len(arrays),
        out_specs=[vmem] * len(shapes),
        scratch_shapes=[pltpu.VMEM(a.shape, a.dtype) for a in (*weights, shift_in, shift_out)]
        + [pltpu.SemaphoreType.DMA((len(arrays),))],
        compiler_params=pltpu.CompilerParams(vmem_limit_bytes=4 << 20),
    )(*[hold(a) for a in arrays])


class Layout:
    def __init__(self, n_row, order, steps, tokens):
        self.n_row, self.order, self.steps, self.tokens = n_row, order, steps, tokens
        self.per = tokens // n_row
        self.group = len(order) * self.per
        self.chunk = self.group * tokens
        self.pitch = tokens + 8
        self.marks = mark_rows(n_row, self.per)
        self.column_marks = seats(n_row) * self.per

    def places(self):
        me = lax.axis_index("row")
        for n, step in enumerate(self.steps):
            for slot, place in enumerate(self.order):
                yield n * self.group + slot * self.per, me ^ (step ^ place)

    def pairs(self, n):
        return [(n, q) for q in range(n + 1)] + [(p, n) for p in range(n)]


def prepare(lay, n, block, gain, proj, gate_weight, proj_bias, gate_bias, outs, scratch):
    z, left, right_t, gate, near = outs
    marks, rough, right, columns, seen = scratch
    tokens, group, per, chunk, pitch = lay.tokens, lay.group, lay.per, lay.chunk, lay.pitch
    width = z.shape[-1]
    places = list(lay.places())
    marks[...] = block[chunk:, :].astype(jnp.float32)
    diagonal = lax.broadcasted_iota(jnp.int32, (tokens, tokens), 0)
    diagonal = diagonal == lax.broadcasted_iota(jnp.int32, (tokens, tokens), 1)
    row = jnp.minimum(marks[lay.column_marks : lay.column_marks + 1, 0:tokens], 1.0)
    column = jnp.sum(jnp.where(diagonal, row, 0.0), axis=1, keepdims=True)
    columns[...] = jnp.broadcast_to(column, (tokens, width))
    for first, at in places:
        seen[first : first + per, :] = columns[pl.ds(at * per, per), :]
    for first, at in places[n * len(lay.order) : (n + 1) * len(lay.order)]:
        near[first - n * group : first - n * group + per, :] = marks[pl.ds(seat(at, lay.n_row) * per, per), :]
    for t in range(group):
        rough[t * pitch : t * pitch + tokens, :] = block[t * tokens : (t + 1) * tokens, :].astype(jnp.float32)
    for first, at in places:
        for t in range(per):
            z[pl.ds(first + t, group, stride=pitch), :] = rough[pl.ds(at * per + t, group, stride=pitch), :]
    values = jnp.concatenate([z[t * pitch : t * pitch + tokens, :] for t in range(group)], axis=0)
    packed, gates = normed_matmul(
        values, gain[0:1, :], (proj[0], gate_weight[0]), (proj_bias[0:1, :], gate_bias[0:1, :])
    )
    value = gated(packed[:, 0 : 2 * width], width)
    for t in range(group):
        left[t * tokens : (t + 1) * tokens, :] = value[t * tokens : (t + 1) * tokens, :] * near[t : t + 1, :]
    value = gated(packed[:, 2 * width :], width)
    for t in range(group):
        right[t * pitch : t * pitch + tokens, :] = value[t * tokens : (t + 1) * tokens, :]
    for k in range(tokens):
        real = near[...] * seen[k : k + 1, :]
        right_t[k * group : (k + 1) * group, :] = right[pl.ds(k, group, stride=pitch), :] * real
    gate[...] = jnp.tanh(gates) + 1.0


def block_sums(lay, blocks, size):
    tokens, group = lay.tokens, lay.group
    width = blocks[0][0].shape[-1]
    results = []
    for start in range(0, len(blocks), size):
        some = blocks[start : start + size]
        totals = [[jnp.zeros((group, width), jnp.float32)] * group for _ in some]
        for k in range(tokens):
            rows = {id(right): right[k * group : (k + 1) * group, :] for _, right in some}
            for i in range(group):
                values = {id(left): left[i * tokens + k : i * tokens + k + 1, :] for left, _ in some}
                for total, (left, right) in zip(totals, some, strict=True):
                    total[i] = total[i] + values[id(left)] * rows[id(right)]
        results += totals
    return results


def complete(lay, n, lefts, rights, sums):
    size = lay.group * lay.group
    totals = block_sums(lay, [(lefts[p], rights[q]) for p, q in lay.pairs(n)], 4)
    for place, total in enumerate(totals):
        sums[place * size : (place + 1) * size, :] = jnp.concatenate(total, axis=0)


def group_kernel(lay, n, block, *refs):
    lefts, rights, refs = refs[:n], refs[n : 2 * n], refs[2 * n :]
    params, outs, sums, scratch = refs[:5], refs[5:10], refs[10], refs[11:]

    def run():
        prepare(lay, n, block, *params, outs, scratch)
        complete(lay, n, [*lefts, outs[1]], [*rights, outs[2]], sums)

    pl.when(lax.axis_index("row") % 2 == 1)(run)


def group_shapes(lay, n, width):
    count = len(lay.pairs(n)) * lay.group * lay.group
    rows = [(lay.group + 1) * lay.pitch, lay.chunk, lay.chunk, lay.chunk, lay.group, count]
    return [(r, width) for r in rows]


def scratch_shapes(lay, width):
    rows = [lay.marks] + [(lay.group + 1) * lay.pitch] * 2 + [lay.tokens] * 2
    return [pltpu.VMEM((r, width), jnp.float32) for r in rows]


def complete_group(lay, n, block, lefts, rights, params):
    width = block.shape[-1]
    vmem = pl.BlockSpec(memory_space=pltpu.VMEM)
    shapes = group_shapes(lay, n, width)
    sums = shapes[-1][0] * lay.tokens * width
    return pl.pallas_call(
        functools.partial(group_kernel, lay, n),
        out_shape=[jax.ShapeDtypeStruct(shape, jnp.float32) for shape in shapes],
        in_specs=[vmem] * (1 + 2 * n + len(params)),
        out_specs=[vmem] * len(shapes),
        scratch_shapes=scratch_shapes(lay, width),
        cost_estimate=pl.CostEstimate(
            flops=10 * lay.chunk * width * width + 2 * sums,
            bytes_accessed=20 * lay.chunk * width,
            transcendentals=3 * lay.chunk * width,
        ),
        compiler_params=pltpu.CompilerParams(vmem_limit_bytes=4 << 20),
    )(block, *lefts, *rights, *params)


def finish(lay, ours, middle, right, real, params, scratch, out):
    gain_in, gain_out, proj, gate_weight, out_weight, proj_bias, gate_bias, out_bias = params
    left, rough, result = scratch
    tokens, per, pitch = lay.tokens, lay.per, lay.pitch
    width = out.shape[-1]
    marks = real[...]
    columns = jnp.concatenate([middle[pl.ds(r, tokens, stride=pitch), :] for r in ours], axis=0)
    (packed,) = normed_matmul(columns, gain_in[1:2, :], (proj[1, :, 0 : 2 * width],), (proj_bias[1:2, 0 : 2 * width],))
    left[...] = gated(packed, width) * jnp.concatenate([marks] * len(ours), axis=0)
    held = jnp.concatenate([middle[r * pitch : r * pitch + tokens, :] for r in ours], axis=0)
    (gates,) = normed_matmul(held, gain_in[1:2, :], (gate_weight[1],), (gate_bias[1:2, :],))
    gates = jnp.tanh(gates) + 1.0
    totals = [jnp.zeros((tokens, width), jnp.float32)] * len(ours)
    for k in range(tokens):
        row = right[k * tokens : (k + 1) * tokens, :]
        for r in range(len(ours)):
            totals[r] = totals[r] + left[r * tokens + k : r * tokens + k + 1, :] * row
    product = jnp.concatenate([t * (marks * real[r : r + 1, :]) for r, t in zip(ours, totals, strict=True)], axis=0)
    (change,) = normed_matmul(product, gain_out[1:2, :], (out_weight[1],), (out_bias[1:2, :],))
    value = held + gates * change
    for r in range(len(ours)):
        rough[r * pitch : r * pitch + tokens, :] = value[r * tokens : (r + 1) * tokens, :]
    for first, at in lay.places():
        for t in range(per):
            row = rough[pl.ds(first + t, len(ours), stride=pitch), :]
            result[pl.ds(at * per + t, len(ours), stride=pitch), :] = row
    halves = [result[r * pitch : r * pitch + tokens, :] for r in range(len(ours))]
    out[...] = jnp.concatenate(halves, axis=0).astype(jnp.bfloat16)


def finish_scratch(lay, width):
    rows = [lay.per * lay.tokens, (lay.per + 1) * lay.pitch, (lay.per + 1) * lay.pitch]
    return [pltpu.VMEM((r, width), jnp.float32) for r in rows]


def odd_kernel(lay, middle, right, real, *refs):
    params, out, scratch = refs[:8], refs[8], refs[9:]
    odd = lax.axis_index("row") % 2 == 1
    pl.when(odd)(lambda: finish(lay, range(lay.per), middle, right, real, params, scratch, out))


def updates_kernel(lay, block, *refs):
    last = len(lay.steps) - 1
    done = [refs[6 * n : 6 * n + 6] for n in range(last)]
    params, refs = refs[6 * last : 6 * last + 8], refs[6 * last + 8 :]
    gain_in, gain_out, proj, gate_weight, out_weight, proj_bias, gate_bias, out_bias = params
    out, middle, right1, real = refs[:4]
    own, scratch, last_scratch = refs[4:10], refs[10:15], refs[15:]
    tokens, per, group, chunk, pitch = lay.tokens, lay.per, lay.group, lay.chunk, lay.pitch
    width = out.shape[-1]
    done = done + [own]

    def run():
        prepare(lay, last, block, gain_in, proj, gate_weight, proj_bias, gate_bias, own[:5], scratch)
        complete(lay, last, [arrays[1] for arrays in done], [arrays[2] for arrays in done], own[5])

        marks = jnp.concatenate([arrays[4][...] for arrays in done], axis=0)
        real[...] = marks
        for p in range(last + 1):
            z, _, _, gate, _, _ = done[p]
            products = []
            for i in range(group):
                parts = []
                for q in range(last + 1):
                    n = max(p, q)
                    start = (lay.pairs(n).index((p, q)) * group + i) * group
                    parts.append(done[n][5][start : start + group, :])
                products += parts
            products = jnp.concatenate(products, axis=0)
            (change,) = normed_matmul(products, gain_out[0:1, :], (out_weight[0],), (out_bias[0:1, :],))
            held = jnp.concatenate([z[t * pitch : t * pitch + tokens, :] for t in range(group)], axis=0)
            moved = held + gate[...] * change
            for t in range(group):
                at = (p * group + t) * pitch
                middle[at : at + tokens, :] = moved[t * tokens : (t + 1) * tokens, :]

        for p in range(last + 1):
            starts = [(p * group + t) * pitch for t in range(group)]
            values = jnp.concatenate([middle[at : at + tokens, :] for at in starts], axis=0)
            (packed,) = normed_matmul(
                values, gain_in[1:2, :], (proj[1, :, 2 * width :],), (proj_bias[1:2, 2 * width :],)
            )
            right1[p * chunk : (p + 1) * chunk, :] = gated(packed, width)

        finish(lay, range(per, 2 * per), middle, right1, real, params, last_scratch, out)

    pl.when(lax.axis_index("row") % 2 == 1)(run)


def updates(lay, blocks, params):
    width = blocks[0].shape[-1]
    rows = lay.per * lay.tokens
    pairs = lay.tokens * lay.tokens
    gain_in, _, proj, gate_weight, _, proj_bias, gate_bias, _ = params
    group_params = (gain_in, proj, gate_weight, proj_bias, gate_bias)
    done = []
    for n, block in enumerate(blocks[:-1]):
        lefts, rights = [arrays[1] for arrays in done], [arrays[2] for arrays in done]
        done.append(complete_group(lay, n, block, lefts, rights, group_params))
    arrays = [array for arrays in done for array in arrays]
    vmem = pl.BlockSpec(memory_space=pltpu.VMEM)
    out = jax.ShapeDtypeStruct((rows, width), jnp.bfloat16)
    shared = [((lay.tokens + 1) * lay.pitch, width), (pairs, width), (lay.tokens, width)]
    even, *shared = pl.pallas_call(
        functools.partial(updates_kernel, lay),
        out_shape=[out] + [jax.ShapeDtypeStruct(shape, jnp.float32) for shape in shared],
        in_specs=[vmem] * (1 + len(arrays) + len(params)),
        out_specs=[vmem] * 4,
        scratch_shapes=[pltpu.VMEM(shape, jnp.float32) for shape in group_shapes(lay, len(blocks) - 1, width)]
        + scratch_shapes(lay, width)
        + finish_scratch(lay, width),
        compiler_params=pltpu.CompilerParams(vmem_limit_bytes=8 << 20),
    )(blocks[-1], *arrays, *params)
    odd = pl.pallas_call(
        functools.partial(odd_kernel, lay),
        out_shape=out,
        in_specs=[vmem] * (3 + len(params)),
        out_specs=vmem,
        scratch_shapes=finish_scratch(lay, width),
        cost_estimate=pl.CostEstimate(
            flops=8 * rows * width * width, bytes_accessed=8 * pairs * width, transcendentals=2 * rows * width
        ),
        compiler_params=pltpu.CompilerParams(vmem_limit_bytes=4 << 20),
    )(*shared, *params)
    return even, odd


def swap(values, step, n_row):
    return lax.ppermute(values, "row", [(i, i ^ step) for i in range(n_row)])


def odd_swap(values, step, n_group, n_row, even_step=0):
    if n_group % 2:
        return swap(values, step, n_row)
    idle = [(g, i ^ even_step) if even_step else (g ^ 1, i) for g in range(n_group) for i in range(n_row)]
    target = [(n // n_row, n % n_row ^ step) if n % 2 else place for n, place in enumerate(idle)]
    pairs = [(source, g * n_row + i) for source, (g, i) in enumerate(target)]
    return lax.ppermute(values, ("groups", "row"), pairs)


def merge(first, second, rows):
    return jnp.concatenate([first[:rows], second[:rows], first[rows:] + second[rows:]], axis=0)


def gathered(n_group, n_row, pair_rep, pair_mask, *params):
    per, tokens, width = pair_rep.shape
    rows = per * tokens
    me = lax.axis_index("row")
    own = pair_rep.reshape(rows, width)
    other = swap(own, 1, n_row)
    other_mask = swap(pair_mask, 1, n_row)
    own, mask = fetch(own, pair_mask)
    other, other_mask, own, mask = lax.optimization_barrier((other, other_mask, own, mask))
    held = join(n_row, own, mask, other, other_mask)
    order = [0, 1]
    step = n_row // 2
    while step > 4:
        count = len(order)
        held = merge(held, odd_swap(held, step, n_group, n_row, 2), count * rows)
        order = order + [place ^ step for place in order]
        step //= 2
    held, *params = lax.optimization_barrier((held, *load(*params)))
    steps = [0] + list(range(2, 2 * step, 2))
    steps[2:] = reversed(steps[2:])
    blocks = [held] + [odd_swap(held, place, n_group, n_row) for place in steps[1:]]
    even, odd = updates(Layout(n_row, order, steps, tokens), blocks, params)
    out = jnp.where(me % 2 == 1, odd, swap(even, 1, n_row))
    return out.reshape(per, tokens, width)


H = 128


def layer_norm(values, gain, offset, axis):
    mean = jnp.mean(values, axis=axis, keepdims=True)
    centered = values - mean
    variance = jnp.mean(centered * centered, axis=axis, keepdims=True)
    return centered * lax.rsqrt(variance + 1e-05) * gain + offset


def triangle(
    pair_now,
    pair_mask,
    layer_index,
    gain_in,
    shift_in,
    proj_weight,
    gate_weight,
    gain_out,
    shift_out,
    out_weight,
):
    normed = layer_norm(
        pair_now.astype(jnp.float32), gain_in[layer_index], shift_in[layer_index], -1
    ).astype(jnp.bfloat16)
    packed = jnp.einsum(
        "rnc,ch->hrn", normed, proj_weight[layer_index], preferred_element_type=jnp.float32
    )
    masked = pair_mask.astype(jnp.float32)[None, :, :]
    left = (masked * jax.nn.sigmoid(packed[0:H]) * packed[H : 2 * H]).astype(jnp.bfloat16)
    right = (masked * jax.nn.sigmoid(packed[2 * H : 3 * H]) * packed[3 * H :]).astype(jnp.bfloat16)
    gating = jax.nn.sigmoid(
        jnp.einsum(
            "rnc,cd->rnd", normed, gate_weight[layer_index], preferred_element_type=jnp.float32
        )
    )
    lifted_left, lifted_right = (
        lax.all_to_all(left, "row", split_axis=0, concat_axis=1, tiled=True),
        lax.all_to_all(right, "row", split_axis=0, concat_axis=1, tiled=True),
    )
    if layer_index == 0:
        product = jnp.einsum(
            "hik,hjk->hij", lifted_left, lifted_right, preferred_element_type=jnp.float32
        )
    else:
        product = jnp.einsum(
            "hki,hkj->hij", lifted_left, lifted_right, preferred_element_type=jnp.float32
        )
    product = product.astype(jnp.bfloat16)
    out_gain = gain_out[layer_index][:, None, None]
    out_shift = shift_out[layer_index][:, None, None]
    out_proj = out_weight[layer_index]
    returned = lax.all_to_all(product, "row", split_axis=1, concat_axis=0, tiled=True)
    scaled = layer_norm(returned.astype(jnp.float32), out_gain, out_shift, 0).astype(jnp.bfloat16)
    update = jnp.einsum("hrn,hc->rnc", scaled, out_proj, preferred_element_type=jnp.float32)
    return (pair_now.astype(jnp.float32) + gating * update).astype(jnp.bfloat16)


def exchanged(
    pair_rep,
    pair_mask,
    gain_in,
    shift_in,
    proj_weight,
    gate_weight,
    gain_out,
    shift_out,
    out_weight,
):
    current = pair_rep
    for layer_index in range(2):
        current = triangle(
            current,
            pair_mask,
            layer_index,
            gain_in,
            shift_in,
            proj_weight,
            gate_weight,
            gain_out,
            shift_out,
            out_weight,
        )
    return current


def solution(mesh):
    n_group, n_row = mesh.shape["groups"], mesh.shape["row"]

    def shards(pair_rep, *rest):
        per, tokens, _ = pair_rep.shape
        small = pair_rep.size * n_row * 2 <= GATHER_LIMIT
        fits = n_row & (n_row - 1) == 0 and n_row > 7 and tokens % 32 == 0 and tokens <= pair_rep.shape[2]
        if small and fits:
            return gathered(n_group, n_row, pair_rep, *rest)
        return exchanged(pair_rep, *rest)

    in_specs = (
        P(("groups", "row"), None, None),
        P(("groups", "row"), None),
        P(),
        P(),
        P(),
        P(),
        P(),
        P(),
        P(),
    )
    out_specs = P(("groups", "row"), None, None)
    return jax.shard_map(shards, mesh=mesh, in_specs=in_specs, out_specs=out_specs, check_vma=False)
```

```python
import functools

import jax
import jax.numpy as jnp
from jax import lax
from jax.experimental import pallas as pl
from jax.experimental.pallas import tpu as pltpu
from jax.sharding import PartitionSpec as P

EPS = 1e-05
MARK_ROWS = 16
GATHER_LIMIT = 4 << 20


def matmul(left, right):
    return jnp.dot(left, right, preferred_element_type=jnp.float32)


def normed_piece(values, gain, weights, biases):
    width = values.shape[-1]
    centered = values - jnp.mean(values, axis=-1, keepdims=True)
    scale = lax.rsqrt(jnp.sum(centered * centered, axis=-1, keepdims=True) + width * EPS)
    factor = (centered * (gain * width**0.5)).astype(jnp.bfloat16)
    return [matmul(factor, weight) * scale + bias for weight, bias in zip(weights, biases, strict=True)]


def normed_matmul(values, gain, weights, biases):
    pieces = [normed_piece(values[at : at + 128], gain, weights, biases) for at in range(0, values.shape[0], 128)]
    return [jnp.concatenate(parts, axis=0) for parts in zip(*pieces, strict=True)]


def gated(packed, width):
    return (jnp.tanh(packed[:, :width]) + 1.0) * packed[:, width:]


def seat(device, n_row):
    place = device % 2
    step, weight = n_row // 2, 2
    while step > 4:
        place = place + weight * (device // step % 2)
        step, weight = step // 2, 2 * weight
    return place


def seats(n_row):
    return max(2, n_row // 4)


def hold(values):
    return pltpu.with_memory_space_constraint(values, pltpu.HBM)


def mark_rows(n_row, per):
    return -(-(seats(n_row) * per + 1) // MARK_ROWS) * MARK_ROWS


def join_kernel(n_row, own, mask, other, other_mask, out_ref, marks):
    rows = own.shape[0]
    per, tokens = mask.shape
    width = out_ref.shape[1]
    me = lax.axis_index("row")
    out_ref[0:rows, :] = own[...]
    out_ref[rows : 2 * rows, :] = other[...]
    marks[...] = jnp.zeros_like(marks)
    last = seats(n_row) * per
    seen = []
    for device, ref in ((me, mask), (me ^ 1, other_mask)):
        mine = ref[...].astype(jnp.float32)
        first = seat(device, n_row) * per
        marks[pl.ds(first, per), :] = jnp.broadcast_to(jnp.max(mine, axis=1, keepdims=True), (per, width))
        seen.append(jnp.max(mine, axis=0, keepdims=True))
    marks[last : last + 1, 0:tokens] = jnp.maximum(*seen)
    out_ref[2 * rows :, :] = marks[...].astype(jnp.bfloat16)


def join(n_row, own, mask, other, other_mask):
    rows, width = own.shape
    extra = mark_rows(n_row, mask.shape[0])
    vmem = pl.BlockSpec(memory_space=pltpu.VMEM)
    return pl.pallas_call(
        functools.partial(join_kernel, n_row),
        out_shape=jax.ShapeDtypeStruct((2 * rows + extra, width), jnp.bfloat16),
        in_specs=[vmem] * 4,
        out_specs=vmem,
        scratch_shapes=[pltpu.VMEM((extra, width), jnp.float32)],
        compiler_params=pltpu.CompilerParams(vmem_limit_bytes=1 << 20),
    )(own, mask, other, other_mask)


def fetch_kernel(count, *refs):
    sources, targets, sems = refs[:count], refs[count : 2 * count], refs[2 * count]
    copies = [pltpu.make_async_copy(s, t, sems.at[n]) for n, (s, t) in enumerate(zip(sources, targets, strict=True))]
    for copy in copies:
        copy.start()
    for copy in copies:
        copy.wait()


def fetch(*arrays):
    count = len(arrays)
    return pl.pallas_call(
        functools.partial(fetch_kernel, count),
        out_shape=[jax.ShapeDtypeStruct(a.shape, a.dtype) for a in arrays],
        in_specs=[pl.BlockSpec(memory_space=pltpu.HBM)] * count,
        out_specs=[pl.BlockSpec(memory_space=pltpu.VMEM)] * count,
        scratch_shapes=[pltpu.SemaphoreType.DMA((count,))],
        compiler_params=pltpu.CompilerParams(vmem_limit_bytes=1 << 20),
    )(*[hold(a) for a in arrays])


def load_kernel(sources, targets):
    (gain_in, shift_in, proj, gate, gain_out, shift_out, out), sems = sources[:7], sources[-1]
    held = sources[7:-1]
    copies = [
        pltpu.make_async_copy(source, target, sems.at[n])
        for n, (source, target) in enumerate(
            zip((proj, gate, out, shift_in, shift_out, gain_in, gain_out), (*held, targets[0], targets[1]), strict=True)
        )
    ]
    for copy in copies:
        copy.start()
    for copy in copies:
        copy.wait()
    proj, gate, out, shift_in, shift_out = held
    _, _, proj_half, gate_half, out_half, proj_bias, gate_bias, out_bias = targets
    half = jnp.array(0.5, jnp.bfloat16)
    for weight, halved, bias, shift in (
        (proj, proj_half, proj_bias, shift_in),
        (gate, gate_half, gate_bias, shift_in),
        (out, out_half, out_bias, shift_out),
    ):
        halved[...] = weight[...] * half
        exact = shift[...]
        high = exact.astype(jnp.bfloat16)
        low = (exact - high.astype(jnp.float32)).astype(jnp.bfloat16)
        rows = jnp.concatenate([high, low] + [jnp.zeros_like(high)] * 6, axis=0)
        for u in range(2):
            both = matmul(rows, weight[u])
            bias[u : u + 1, :] = 0.5 * (both[u : u + 1, :] + both[u + 2 : u + 3, :])


def load(gain_in, shift_in, proj, gate, gain_out, shift_out, out):
    arrays = (gain_in, shift_in, proj, gate, gain_out, shift_out, out)
    weights = (proj, gate, out)
    shapes = [(a.shape, a.dtype) for a in (gain_in, gain_out, *weights)]
    shapes += [((a.shape[0], a.shape[2]), jnp.float32) for a in weights]
    vmem = pl.BlockSpec(memory_space=pltpu.VMEM)

    def kernel(*refs):
        load_kernel((*refs[:7], *refs[7 + len(shapes) :]), refs[7 : 7 + len(shapes)])

    return pl.pallas_call(
        kernel,
        out_shape=[jax.ShapeDtypeStruct(*shape) for shape in shapes],
        in_specs=[pl.BlockSpec(memory_space=pltpu.HBM)] * len(arrays),
        out_specs=[vmem] * len(shapes),
        scratch_shapes=[pltpu.VMEM(a.shape, a.dtype) for a in (*weights, shift_in, shift_out)]
        + [pltpu.SemaphoreType.DMA((len(arrays),))],
        compiler_params=pltpu.CompilerParams(vmem_limit_bytes=4 << 20),
    )(*[hold(a) for a in arrays])


class Layout:
    def __init__(self, n_row, order, steps, tokens):
        self.n_row, self.order, self.steps, self.tokens = n_row, order, steps, tokens
        self.per = tokens // n_row
        self.group = len(order) * self.per
        self.chunk = self.group * tokens
        self.pitch = tokens + 8
        self.marks = mark_rows(n_row, self.per)
        self.column_marks = seats(n_row) * self.per

    def places(self):
        me = lax.axis_index("row")
        for n, step in enumerate(self.steps):
            for slot, place in enumerate(self.order):
                yield n * self.group + slot * self.per, me ^ (step ^ place)

    def pairs(self, n):
        return [(p, n) for p in range(n)] + [(n, q) for q in range(n + 1)]


def prepare(lay, n, block, gain, proj, gate_weight, proj_bias, gate_bias, outs, scratch):
    z, left, right_t, gate, near = outs
    marks, rough, right, columns, seen = scratch
    tokens, group, per, chunk, pitch = lay.tokens, lay.group, lay.per, lay.chunk, lay.pitch
    width = z.shape[-1]
    places = list(lay.places())
    marks[...] = block[chunk:, :].astype(jnp.float32)
    diagonal = lax.broadcasted_iota(jnp.int32, (tokens, tokens), 0)
    diagonal = diagonal == lax.broadcasted_iota(jnp.int32, (tokens, tokens), 1)
    row = jnp.minimum(marks[lay.column_marks : lay.column_marks + 1, 0:tokens], 1.0)
    column = jnp.sum(jnp.where(diagonal, row, 0.0), axis=1, keepdims=True)
    columns[...] = jnp.broadcast_to(column, (tokens, width))
    for first, at in places:
        seen[first : first + per, :] = columns[pl.ds(at * per, per), :]
    for first, at in places[n * len(lay.order) : (n + 1) * len(lay.order)]:
        near[first - n * group : first - n * group + per, :] = marks[pl.ds(seat(at, lay.n_row) * per, per), :]
    for t in range(group):
        rough[t * pitch : t * pitch + tokens, :] = block[t * tokens : (t + 1) * tokens, :].astype(jnp.float32)
    for first, at in places:
        for t in range(per):
            z[pl.ds(first + t, group, stride=pitch), :] = rough[pl.ds(at * per + t, group, stride=pitch), :]
    values = jnp.concatenate([z[t * pitch : t * pitch + tokens, :] for t in range(group)], axis=0)
    packed, gates = normed_matmul(
        values, gain[0:1, :], (proj[0], gate_weight[0]), (proj_bias[0:1, :], gate_bias[0:1, :])
    )
    value = gated(packed[:, 0 : 2 * width], width)
    for t in range(group):
        left[t * tokens : (t + 1) * tokens, :] = value[t * tokens : (t + 1) * tokens, :] * near[t : t + 1, :]
    value = gated(packed[:, 2 * width :], width)
    for t in range(group):
        right[t * pitch : t * pitch + tokens, :] = value[t * tokens : (t + 1) * tokens, :]
    for k in range(tokens):
        real = near[...] * seen[k : k + 1, :]
        right_t[k * group : (k + 1) * group, :] = right[pl.ds(k, group, stride=pitch), :] * real
    gate[...] = jnp.tanh(gates) + 1.0


def block_sums(lay, blocks, size):
    tokens, group = lay.tokens, lay.group
    width = blocks[0][0].shape[-1]
    results = []
    for start in range(0, len(blocks), size):
        some = blocks[start : start + size]
        totals = [[jnp.zeros((group, width), jnp.float32)] * group for _ in some]
        for k in range(tokens):
            rows = {id(right): right[k * group : (k + 1) * group, :] for _, right in some}
            for i in range(group):
                values = {id(left): left[i * tokens + k : i * tokens + k + 1, :] for left, _ in some}
                for total, (left, right) in zip(totals, some, strict=True):
                    total[i] = total[i] + values[id(left)] * rows[id(right)]
        results += totals
    return results


def complete(lay, n, lefts, rights, sums):
    size = lay.group * lay.group
    totals = block_sums(lay, [(lefts[p], rights[q]) for p, q in lay.pairs(n)], 4)
    for place, total in enumerate(totals):
        sums[place * size : (place + 1) * size, :] = jnp.concatenate(total, axis=0)


def group_kernel(lay, n, block, *refs):
    lefts, rights, refs = refs[:n], refs[n : 2 * n], refs[2 * n :]
    params, outs, sums, scratch = refs[:5], refs[5:10], refs[10], refs[11:]

    def run():
        prepare(lay, n, block, *params, outs, scratch)
        complete(lay, n, [*lefts, outs[1]], [*rights, outs[2]], sums)

    pl.when(lax.axis_index("row") % 2 == 1)(run)


def group_shapes(lay, n, width):
    count = len(lay.pairs(n)) * lay.group * lay.group
    rows = [(lay.group + 1) * lay.pitch, lay.chunk, lay.chunk, lay.chunk, lay.group, count]
    return [(r, width) for r in rows]


def scratch_shapes(lay, width):
    rows = [lay.marks] + [(lay.group + 1) * lay.pitch] * 2 + [lay.tokens] * 2
    return [pltpu.VMEM((r, width), jnp.float32) for r in rows]


def complete_group(lay, n, block, lefts, rights, params):
    width = block.shape[-1]
    vmem = pl.BlockSpec(memory_space=pltpu.VMEM)
    shapes = group_shapes(lay, n, width)
    sums = shapes[-1][0] * lay.tokens * width
    return pl.pallas_call(
        functools.partial(group_kernel, lay, n),
        out_shape=[jax.ShapeDtypeStruct(shape, jnp.float32) for shape in shapes],
        in_specs=[vmem] * (1 + 2 * n + len(params)),
        out_specs=[vmem] * len(shapes),
        scratch_shapes=scratch_shapes(lay, width),
        cost_estimate=pl.CostEstimate(
            flops=10 * lay.chunk * width * width + 2 * sums,
            bytes_accessed=20 * lay.chunk * width,
            transcendentals=3 * lay.chunk * width,
        ),
        compiler_params=pltpu.CompilerParams(vmem_limit_bytes=4 << 20),
    )(block, *lefts, *rights, *params)


def finish(lay, ours, middle, right, real, params, scratch, out):
    gain_in, gain_out, proj, gate_weight, out_weight, proj_bias, gate_bias, out_bias = params
    left, rough, result = scratch
    tokens, per, pitch = lay.tokens, lay.per, lay.pitch
    width = out.shape[-1]
    marks = real[...]
    columns = jnp.concatenate([middle[pl.ds(r, tokens, stride=pitch), :] for r in ours], axis=0)
    (packed,) = normed_matmul(columns, gain_in[1:2, :], (proj[1, :, 0 : 2 * width],), (proj_bias[1:2, 0 : 2 * width],))
    left[...] = gated(packed, width) * jnp.concatenate([marks] * len(ours), axis=0)
    held = jnp.concatenate([middle[r * pitch : r * pitch + tokens, :] for r in ours], axis=0)
    (gates,) = normed_matmul(held, gain_in[1:2, :], (gate_weight[1],), (gate_bias[1:2, :],))
    gates = jnp.tanh(gates) + 1.0
    totals = [jnp.zeros((tokens, width), jnp.float32)] * len(ours)
    for k in range(tokens):
        row = right[k * tokens : (k + 1) * tokens, :]
        for r in range(len(ours)):
            totals[r] = totals[r] + left[r * tokens + k : r * tokens + k + 1, :] * row
    product = jnp.concatenate([t * (marks * real[r : r + 1, :]) for r, t in zip(ours, totals, strict=True)], axis=0)
    (change,) = normed_matmul(product, gain_out[1:2, :], (out_weight[1],), (out_bias[1:2, :],))
    value = held + gates * change
    for r in range(len(ours)):
        rough[r * pitch : r * pitch + tokens, :] = value[r * tokens : (r + 1) * tokens, :]
    for first, at in lay.places():
        for t in range(per):
            row = rough[pl.ds(first + t, len(ours), stride=pitch), :]
            result[pl.ds(at * per + t, len(ours), stride=pitch), :] = row
    halves = [result[r * pitch : r * pitch + tokens, :] for r in range(len(ours))]
    out[...] = jnp.concatenate(halves, axis=0).astype(jnp.bfloat16)


def finish_scratch(lay, width):
    rows = [lay.per * lay.tokens, (lay.per + 1) * lay.pitch, (lay.per + 1) * lay.pitch]
    return [pltpu.VMEM((r, width), jnp.float32) for r in rows]


def odd_kernel(lay, middle, right, real, *refs):
    params, out, scratch = refs[:8], refs[8], refs[9:]
    odd = lax.axis_index("row") % 2 == 1
    pl.when(odd)(lambda: finish(lay, range(lay.per), middle, right, real, params, scratch, out))


def updates_kernel(lay, block, *refs):
    last = len(lay.steps) - 1
    done = [refs[6 * n : 6 * n + 6] for n in range(last)]
    params, refs = refs[6 * last : 6 * last + 8], refs[6 * last + 8 :]
    gain_in, gain_out, proj, gate_weight, out_weight, proj_bias, gate_bias, out_bias = params
    out, middle, right1, real = refs[:4]
    own, scratch, last_scratch = refs[4:10], refs[10:15], refs[15:]
    tokens, per, group, chunk, pitch = lay.tokens, lay.per, lay.group, lay.chunk, lay.pitch
    width = out.shape[-1]
    done = done + [own]

    def run():
        prepare(lay, last, block, gain_in, proj, gate_weight, proj_bias, gate_bias, own[:5], scratch)
        complete(lay, last, [arrays[1] for arrays in done], [arrays[2] for arrays in done], own[5])

        marks = jnp.concatenate([arrays[4][...] for arrays in done], axis=0)
        real[...] = marks
        for p in range(last + 1):
            z, _, _, gate, _, _ = done[p]
            products = []
            for i in range(group):
                parts = []
                for q in range(last + 1):
                    n = max(p, q)
                    start = (lay.pairs(n).index((p, q)) * group + i) * group
                    parts.append(done[n][5][start : start + group, :])
                products += parts
            products = jnp.concatenate(products, axis=0)
            (change,) = normed_matmul(products, gain_out[0:1, :], (out_weight[0],), (out_bias[0:1, :],))
            held = jnp.concatenate([z[t * pitch : t * pitch + tokens, :] for t in range(group)], axis=0)
            moved = held + gate[...] * change
            for t in range(group):
                at = (p * group + t) * pitch
                middle[at : at + tokens, :] = moved[t * tokens : (t + 1) * tokens, :]

        for p in range(last + 1):
            starts = [(p * group + t) * pitch for t in range(group)]
            values = jnp.concatenate([middle[at : at + tokens, :] for at in starts], axis=0)
            (packed,) = normed_matmul(
                values, gain_in[1:2, :], (proj[1, :, 2 * width :],), (proj_bias[1:2, 2 * width :],)
            )
            right1[p * chunk : (p + 1) * chunk, :] = gated(packed, width)

        finish(lay, range(per, 2 * per), middle, right1, real, params, last_scratch, out)

    pl.when(lax.axis_index("row") % 2 == 1)(run)


def updates(lay, blocks, params):
    width = blocks[0].shape[-1]
    rows = lay.per * lay.tokens
    pairs = lay.tokens * lay.tokens
    gain_in, _, proj, gate_weight, _, proj_bias, gate_bias, _ = params
    group_params = (gain_in, proj, gate_weight, proj_bias, gate_bias)
    done = []
    for n, block in enumerate(blocks[:-1]):
        lefts, rights = [arrays[1] for arrays in done], [arrays[2] for arrays in done]
        done.append(complete_group(lay, n, block, lefts, rights, group_params))
    arrays = [array for arrays in done for array in arrays]
    vmem = pl.BlockSpec(memory_space=pltpu.VMEM)
    out = jax.ShapeDtypeStruct((rows, width), jnp.bfloat16)
    shared = [((lay.tokens + 1) * lay.pitch, width), (pairs, width), (lay.tokens, width)]
    even, *shared = pl.pallas_call(
        functools.partial(updates_kernel, lay),
        out_shape=[out] + [jax.ShapeDtypeStruct(shape, jnp.float32) for shape in shared],
        in_specs=[vmem] * (1 + len(arrays) + len(params)),
        out_specs=[vmem] * 4,
        scratch_shapes=[pltpu.VMEM(shape, jnp.float32) for shape in group_shapes(lay, len(blocks) - 1, width)]
        + scratch_shapes(lay, width)
        + finish_scratch(lay, width),
        compiler_params=pltpu.CompilerParams(vmem_limit_bytes=8 << 20),
    )(blocks[-1], *arrays, *params)
    odd = pl.pallas_call(
        functools.partial(odd_kernel, lay),
        out_shape=out,
        in_specs=[vmem] * (3 + len(params)),
        out_specs=vmem,
        scratch_shapes=finish_scratch(lay, width),
        cost_estimate=pl.CostEstimate(
            flops=8 * rows * width * width, bytes_accessed=8 * pairs * width, transcendentals=2 * rows * width
        ),
        compiler_params=pltpu.CompilerParams(vmem_limit_bytes=4 << 20),
    )(*shared, *params)
    return even, odd


def swap(values, step, n_row):
    return lax.ppermute(values, "row", [(i, i ^ step) for i in range(n_row)])


def odd_swap(values, step, n_group, n_row, even_step=0):
    if n_group % 2:
        return swap(values, step, n_row)
    idle = [(g, i ^ even_step) if even_step else (g ^ 1, i) for g in range(n_group) for i in range(n_row)]
    target = [(n // n_row, n % n_row ^ step) if n % 2 else place for n, place in enumerate(idle)]
    pairs = [(source, g * n_row + i) for source, (g, i) in enumerate(target)]
    return lax.ppermute(values, ("groups", "row"), pairs)


def merge(first, second, rows):
    return jnp.concatenate([first[:rows], second[:rows], first[rows:] + second[rows:]], axis=0)


def gathered(n_group, n_row, pair_rep, pair_mask, *params):
    per, tokens, width = pair_rep.shape
    rows = per * tokens
    me = lax.axis_index("row")
    own = pair_rep.reshape(rows, width)
    other = swap(own, 1, n_row)
    other_mask = swap(pair_mask, 1, n_row)
    own, mask = fetch(own, pair_mask)
    other, other_mask, own, mask = lax.optimization_barrier((other, other_mask, own, mask))
    held = join(n_row, own, mask, other, other_mask)
    order = [0, 1]
    step = n_row // 2
    while step > 4:
        count = len(order)
        held = merge(held, odd_swap(held, step, n_group, n_row, 2), count * rows)
        order = order + [place ^ step for place in order]
        step //= 2
    held, *params = lax.optimization_barrier((held, *load(*params)))
    steps = [0] + list(range(2, 2 * step, 2))
    steps[2:] = reversed(steps[2:])
    blocks = [held] + [odd_swap(held, place, n_group, n_row) for place in steps[1:]]
    even, odd = updates(Layout(n_row, order, steps, tokens), blocks, params)
    out = jnp.where(me % 2 == 1, odd, swap(even, 1, n_row))
    return out.reshape(per, tokens, width)


H = 128


def layer_norm(values, gain, offset, axis):
    mean = jnp.mean(values, axis=axis, keepdims=True)
    centered = values - mean
    variance = jnp.mean(centered * centered, axis=axis, keepdims=True)
    return centered * lax.rsqrt(variance + 1e-05) * gain + offset


def triangle(
    pair_now,
    pair_mask,
    layer_index,
    gain_in,
    shift_in,
    proj_weight,
    gate_weight,
    gain_out,
    shift_out,
    out_weight,
):
    normed = layer_norm(
        pair_now.astype(jnp.float32), gain_in[layer_index], shift_in[layer_index], -1
    ).astype(jnp.bfloat16)
    packed = jnp.einsum(
        "rnc,ch->hrn", normed, proj_weight[layer_index], preferred_element_type=jnp.float32
    )
    masked = pair_mask.astype(jnp.float32)[None, :, :]
    left = (masked * jax.nn.sigmoid(packed[0:H]) * packed[H : 2 * H]).astype(jnp.bfloat16)
    right = (masked * jax.nn.sigmoid(packed[2 * H : 3 * H]) * packed[3 * H :]).astype(jnp.bfloat16)
    gating = jax.nn.sigmoid(
        jnp.einsum(
            "rnc,cd->rnd", normed, gate_weight[layer_index], preferred_element_type=jnp.float32
        )
    )
    lifted_left, lifted_right = (
        lax.all_to_all(left, "row", split_axis=0, concat_axis=1, tiled=True),
        lax.all_to_all(right, "row", split_axis=0, concat_axis=1, tiled=True),
    )
    if layer_index == 0:
        product = jnp.einsum(
            "hik,hjk->hij", lifted_left, lifted_right, preferred_element_type=jnp.float32
        )
    else:
        product = jnp.einsum(
            "hki,hkj->hij", lifted_left, lifted_right, preferred_element_type=jnp.float32
        )
    product = product.astype(jnp.bfloat16)
    out_gain = gain_out[layer_index][:, None, None]
    out_shift = shift_out[layer_index][:, None, None]
    out_proj = out_weight[layer_index]
    returned = lax.all_to_all(product, "row", split_axis=1, concat_axis=0, tiled=True)
    scaled = layer_norm(returned.astype(jnp.float32), out_gain, out_shift, 0).astype(jnp.bfloat16)
    update = jnp.einsum("hrn,hc->rnc", scaled, out_proj, preferred_element_type=jnp.float32)
    return (pair_now.astype(jnp.float32) + gating * update).astype(jnp.bfloat16)


def exchanged(
    pair_rep,
    pair_mask,
    gain_in,
    shift_in,
    proj_weight,
    gate_weight,
    gain_out,
    shift_out,
    out_weight,
):
    current = pair_rep
    for layer_index in range(2):
        current = triangle(
            current,
            pair_mask,
            layer_index,
            gain_in,
            shift_in,
            proj_weight,
            gate_weight,
            gain_out,
            shift_out,
            out_weight,
        )
    return current


def solution(mesh):
    n_group, n_row = mesh.shape["groups"], mesh.shape["row"]

    def shards(pair_rep, *rest):
        per, tokens, _ = pair_rep.shape
        small = pair_rep.size * n_row * 2 <= GATHER_LIMIT
        fits = n_row & (n_row - 1) == 0 and n_row > 7 and tokens % 32 == 0 and tokens <= pair_rep.shape[2]
        if small and fits:
            return gathered(n_group, n_row, pair_rep, *rest)
        return exchanged(pair_rep, *rest)

    in_specs = (
        P(("groups", "row"), None, None),
        P(("groups", "row"), None),
        P(),
        P(),
        P(),
        P(),
        P(),
        P(),
        P(),
    )
    out_specs = P(("groups", "row"), None, None)
    return jax.shard_map(shards, mesh=mesh, in_specs=in_specs, out_specs=out_specs, check_vma=False)
```
